512 devices in a mesh: store: 32 (over z, core), feat: 16 (over y, x).
Axes of the slice: x: 4, y: 4, z: 16, core: 2. Of those that a mesh axis runs over, the one named last changes fastest.
Arguments:
- features: float32 [768, 131072], P('feat', 'store'), may hold values from -6 to 6
- serve_rows: int32 [32, 32, 256], P('store'), may hold values from 0 to 4095
- row_counts: int32 [32, 32], P('store'), may hold values from 1 to 256, as said below
- layer1_index: int32 [32, 11, 512], P('store'), may hold values from 0 to 8191
- layer2_index: int32 [32, 16, 512], P('store'), may hold values from 0 to 511
- w1_self: bfloat16 [768, 1024], P('feat'), may hold values from -0.21875 to 0.21875
- w1_neigh: bfloat16 [768, 1024], P('feat'), may hold values from -0.21875 to 0.21875
- w2_self_t: bfloat16 [1024, 1024], P('feat'), may hold values from -0.1875 to 0.1875
- w2_neigh_t: bfloat16 [1024, 1024], P('feat'), may hold values from -0.1875 to 0.1875
- out_grad: bfloat16 [1024, 16384], P('feat', 'store'), may hold values from -0.1875 to 0.1875
Outputs:
- h2: bfloat16 [1024, 16384], P('feat', 'store')
- grad_w1_self: float32 [768, 1024], P('feat')
- grad_w1_neigh: float32 [768, 1024], P('feat')
- grad_w2_self_t: float32 [1024, 1024], P('feat')
- grad_w2_neigh_t: float32 [1024, 1024], P('feat')
The draws below stay inside these ranges and needn't reach their ends.
Inputs may be any that keep to these rules, and one draw needn't show every extreme that they name: Of the 256 slots that owner o fills for trainer t, the first row_counts[t, o] are used; in every draw some trainer uses all 256 slots of every owner.
All inputs are finite; a program needn't handle non-finite values.
Results may differ from the reference program's by a relative error of at most 0.009.
Values may be sent and summed in bfloat16 or wider, within the bound.
A program may use at most 64 MiB of HBM per device.

```python
import jax
import jax.numpy as jnp
from jax import lax

F = 768
H = 1024
FAN1 = 10
FAN2 = 15
ROWS_DEV = 4096
IN_ROWS = 8192
N1 = 512
B = 512
CAP = 256
NODES = 131072
N_STORE = 32
N_FEAT = 16


def draw_row_counts(key, part):
    key = jax.random.fold_in(key, 7)
    keys = jax.random.split(key, 3)
    heat = jnp.left_shift(jnp.int32(1), jax.random.randint(keys[0], (N_STORE,), 0, 5))
    base = jax.random.randint(keys[1], (N_STORE, N_STORE), 1, CAP + 1)
    counts = jnp.minimum(CAP, (base * heat[None, :] + 7) // 8)
    full_trainer = jax.random.randint(keys[2], (), 0, N_STORE)
    trainer_ids = jnp.arange(N_STORE, dtype=jnp.int32)[:, None]
    return jnp.where(trainer_ids == full_trainer, CAP, counts).astype(jnp.int32)


def plant(drawn, own_key, low, high):
    longest = drawn.shape.index(max(drawn.shape))
    spots = []
    for shift in (0, 1):
        where = [jax.random.randint(jax.random.fold_in(own_key, axis), (), 0, length) for axis, length in enumerate(drawn.shape)]
        where[longest] = (where[longest] + shift) % drawn.shape[longest]
        spots.append(tuple(where))
    return drawn.at[spots[0]].set(low).at[spots[1]].set(high)


def steps_of(own_key, shape, cuts, low, top_value):
    factor_of = 1.0
    for position, blocks in cuts:
        heights = jax.random.uniform(jax.random.fold_in(jax.random.fold_in(own_key, 6), position), (blocks,), jnp.float32, low / len(cuts), top_value / len(cuts))
        factor_of = factor_of * jnp.repeat(jnp.exp(heights), shape[position] // blocks).reshape((-1,) + (1,) * (len(shape) - 1 - position))
    return factor_of


def normal_values(own_key, extent, spread, most, shards=(), kind=jnp.bfloat16):
    loudness = steps_of(own_key, extent, shards, -0.22, 0.18) if shards else 1.0
    values = jax.random.normal(own_key, extent, jnp.float32) * spread * loudness
    return jnp.minimum(jnp.maximum(values, -most), most).astype(kind)


def setup_inputs(seed: int = 0) -> dict:
    streams_of = jax.random.split(jax.random.key(seed), 11)
    return {
        "features": normal_values(streams_of[0], (F, NODES), 1.0, 6.0, ((0, 16), (1, 32)), jnp.float32),
        "serve_rows": plant(jax.random.randint(streams_of[1], (N_STORE, N_STORE, CAP), 0, ROWS_DEV), jax.random.fold_in(streams_of[1], 1), 0, ROWS_DEV - 1).astype(jnp.int32),
        "row_counts": draw_row_counts(jax.random.fold_in(streams_of[10], 71), 0),
        "layer1_index": plant(jax.random.randint(streams_of[3], (N_STORE, FAN1 + 1, N1), 0, IN_ROWS), jax.random.fold_in(streams_of[3], 1), 0, IN_ROWS - 1).astype(jnp.int32),
        "layer2_index": plant(jax.random.randint(streams_of[4], (N_STORE, FAN2 + 1, B), 0, N1), jax.random.fold_in(streams_of[4], 1), 0, N1 - 1).astype(jnp.int32),
        "w1_self": normal_values(streams_of[5], (F, H), F ** -0.5, 0.21875, ((0, 16),)),
        "w1_neigh": normal_values(streams_of[6], (F, H), F ** -0.5, 0.21875, ((0, 16),)),
        "w2_self_t": normal_values(streams_of[7], (H, H), H ** -0.5, 0.1875, ((0, 16),)),
        "w2_neigh_t": normal_values(streams_of[8], (H, H), H ** -0.5, 0.1875, ((0, 16),)),
        "out_grad": normal_values(streams_of[9], (H, B * N_STORE), (4.0 / (N_STORE * B) ** 0.5), 0.1875, ((0, 16), (1, 32))),
    }


def silu_slope(values):
    sigma_val = jax.nn.sigmoid(values)
    return sigma_val * (1.0 + values * (1.0 - sigma_val))


def reference(features, serve_rows, row_counts, layer1_index, layer2_index, w1_self, w1_neigh, w2_self_t, w2_neigh_t, out_grad):
    hid_width = H // N_FEAT
    owner_base = jnp.arange(N_STORE, dtype=jnp.int32) * ROWS_DEV
    w1_self_wide = w1_self.astype(jnp.float32)
    w1_neigh_wide = w1_neigh.astype(jnp.float32)
    w2_self_groups = w2_self_t.astype(jnp.float32).reshape(N_FEAT, hid_width, H)
    w2_neigh_groups = w2_neigh_t.astype(jnp.float32).reshape(N_FEAT, hid_width, H)

    def one_trainer(totals, trainer):
        picked = lax.dynamic_index_in_dim(serve_rows, trainer, 1, keepdims=False)
        table_rows = (picked + owner_base[:, None]).reshape(-1).astype(jnp.int32)
        inputs = jnp.take(features, table_rows, axis=1)
        counts = lax.dynamic_index_in_dim(row_counts, trainer, 0, keepdims=False)
        raw_index = lax.dynamic_index_in_dim(layer1_index, trainer, 0, keepdims=False)
        owner_ids = raw_index // CAP
        slot_ids = (owner_ids * CAP + (raw_index % CAP) % jnp.take(counts, owner_ids)).astype(jnp.int32)
        fetched = jnp.take(inputs, slot_ids, axis=1)
        self_one = fetched[:, 0].astype(jnp.bfloat16)
        neigh_one = (jnp.sum(fetched[:, 1:], axis=1) / FAN1).astype(jnp.bfloat16)
        pre_one = jnp.dot(self_one.astype(jnp.float32).T, w1_self_wide, precision=lax.Precision.HIGHEST)
        pre_one = pre_one + jnp.dot(neigh_one.astype(jnp.float32).T, w1_neigh_wide, precision=lax.Precision.HIGHEST)
        hid_one = jax.nn.silu(pre_one).astype(jnp.bfloat16)
        index_two = lax.dynamic_index_in_dim(layer2_index, trainer, 0, keepdims=False)
        self_two = jnp.take(hid_one, index_two[0], axis=0)
        neigh_two = (jnp.sum(jnp.take(hid_one, index_two[1:], axis=0).astype(jnp.float32), axis=0) / FAN2).astype(jnp.bfloat16)
        pre_two = jnp.dot(w2_self_t, self_two.T, preferred_element_type=jnp.float32)
        pre_two = pre_two + jnp.dot(w2_neigh_t, neigh_two.T, preferred_element_type=jnp.float32)
        out_block = jax.nn.silu(pre_two).astype(jnp.bfloat16)
        grad_out = lax.dynamic_slice_in_dim(out_grad, trainer * B, B, 1).astype(jnp.float32)
        grad_pre_two = (grad_out * silu_slope(pre_two)).astype(jnp.bfloat16)
        grad_w2s = jnp.dot(grad_pre_two, self_two, preferred_element_type=jnp.float32)
        grad_w2n = jnp.dot(grad_pre_two, neigh_two, preferred_element_type=jnp.float32)
        grad_groups = grad_pre_two.astype(jnp.float32).reshape(N_FEAT, hid_width, B)
        self_terms = jnp.einsum("gkb,gkh->bgh", grad_groups, w2_self_groups, precision=lax.Precision.HIGHEST)
        neigh_terms = jnp.einsum("gkb,gkh->bgh", grad_groups, w2_neigh_groups, precision=lax.Precision.HIGHEST)
        back_self = jax.ops.segment_sum(self_terms, index_two[0], num_segments=N1)
        back_neigh = jnp.zeros((N1, N_FEAT, H), jnp.float32)
        for neighbour in range(1, FAN2 + 1):
            back_neigh = back_neigh + jax.ops.segment_sum(neigh_terms, index_two[neighbour], num_segments=N1)
        grad_hid_one = jnp.sum(back_self + back_neigh / FAN2, axis=1)
        grad_pre_one = (grad_hid_one * silu_slope(pre_one)).astype(jnp.bfloat16)
        grad_w1s = jnp.dot(self_one, grad_pre_one, preferred_element_type=jnp.float32)
        grad_w1n = jnp.dot(neigh_one, grad_pre_one, preferred_element_type=jnp.float32)
        updated = (totals[0] + grad_w1s, totals[1] + grad_w1n, totals[2] + grad_w2s, totals[3] + grad_w2n)
        return updated, out_block

    start_totals = (jnp.zeros((F, H), jnp.float32), jnp.zeros((F, H), jnp.float32), jnp.zeros((H, H), jnp.float32), jnp.zeros((H, H), jnp.float32))
    totals, blocks = lax.scan(one_trainer, start_totals, jnp.arange(N_STORE, dtype=jnp.int32))
    h2 = jnp.transpose(blocks, (1, 0, 2)).reshape(H, N_STORE * B)
    return (h2, totals[0], totals[1], totals[2], totals[3])
```

```python
import functools

import jax
import jax.numpy as jnp
from jax import lax
from jax.experimental import pallas as pl
from jax.experimental.pallas import tpu as pltpu
from jax.sharding import PartitionSpec as P

MESH = pl.DeviceIdType.MESH
F32 = jnp.float32
BF16 = jnp.bfloat16
LOW = 256


def slope(values):
    sig = jax.nn.sigmoid(values)
    return sig * (1.0 + values * (1.0 - sig))


def nt_dot(left, right):
    return lax.dot_general(left, right, (((1,), (1,)), ((), ())), preferred_element_type=F32)


def dot(left, right):
    return jnp.dot(left, right, preferred_element_type=F32)


def halves(values):
    upper = values.astype(BF16)
    return upper, (values - upper.astype(F32)).astype(BF16)


def await_bytes(ref, sem):
    pltpu.make_async_copy(ref, ref, sem).wait()


def kernel(
    n_store,
    n_feat,
    features,
    serve_rows,
    row_counts,
    index_one,
    index_two,
    w1_self,
    w1_neigh,
    w2_self,
    w2_neigh,
    out_grad,
    h2,
    out_w1s,
    out_w1n,
    out_w2s,
    out_w2n,
    table,
    stage,
    rows_in,
    owner_of,
    pick,
    both,
    nodes_out,
    nodes_in,
    w1_own,
    w1_all,
    hid_own,
    hid_all,
    self_t,
    count_t,
    back_out,
    back_in,
    slope_own,
    slope_all,
    tiles2,
    tiles2_in,
    sum2,
    sum2_all,
    tiles1,
    tiles1_in,
    sum1,
    sum1_all,
    send_sems,
    recv_sems,
    group_sems,
):
    my_store, my_feat = lax.axis_index("store"), lax.axis_index("feat")
    width, papers = features.shape
    cap = serve_rows.shape[2]
    entries, nodes = index_one.shape[1:]
    fan_one = entries - 1
    fan_two = index_two.shape[1] - 1
    hidden = w2_self.shape[1]
    units = w2_self.shape[0]
    own_rows = nodes // n_feat

    def store_peer(step):
        return lax.rem(my_store + step + n_store, n_store)

    def feat_peer(step):
        return lax.rem(my_feat + step + n_feat, n_feat)

    def send(src, dst, which, recv_sem, axis, peer):
        pltpu.make_async_remote_copy(
            src_ref=src,
            dst_ref=dst,
            send_sem=send_sems.at[which],
            recv_sem=recv_sem,
            device_id={axis: peer},
            device_id_type=MESH,
        ).start()

    def keep(src, dst, sem):
        pltpu.make_async_copy(src, dst, sem).start()

    def each_feat(fn):
        def step(k, carry):
            fn(feat_peer(k))
            return carry

        lax.fori_loop(1, n_feat, step, 0)

    def each_store(fn):
        def step(k, carry):
            fn(store_peer(k))
            return carry

        lax.fori_loop(1, n_store, step, 0)

    barrier = pltpu.get_barrier_semaphore()
    each_store(
        lambda peer: pl.semaphore_signal(barrier, inc=1, device_id={"store": peer}, device_id_type=MESH)
    )
    each_feat(
        lambda peer: pl.semaphore_signal(barrier, inc=1, device_id={"feat": peer}, device_id_type=MESH)
    )

    highs = papers // LOW
    for high in range(highs):
        table[high * width : (high + 1) * width, :] = features[:, high * LOW : (high + 1) * LOW].astype(BF16)
    w1_own[0:width, :] = w1_self[...]
    w1_own[width : 2 * width, :] = w1_neigh[...]
    pad_rows = w1_all.shape[1] - 2 * width
    for group in range(n_feat):
        w1_all[group, 2 * width :, :] = jnp.zeros((pad_rows, hidden), BF16)

    pl.semaphore_wait(barrier, n_store + n_feat - 2)

    low_ids = lax.broadcasted_iota(jnp.int32, (LOW, cap), 0)
    group_size = n_store // group_sems.shape[0]

    def serve(trainer):
        wanted = serve_rows[0, pl.ds(trainer, 1), :]
        low, high_of = wanted & (LOW - 1), wanted // LOW
        one_hot = jnp.where(low_ids == low, 1.0, 0.0).astype(BF16)
        found = dot(table[...], one_hot)
        total = jnp.zeros((width, cap), F32)
        for high in range(highs):
            total += jnp.where(high_of == high, found[high * width : (high + 1) * width, :], 0.0)
        stage[trainer] = total.astype(BF16)

    def serve_and_send(trainer):
        serve(trainer)
        send(stage.at[trainer], rows_in.at[my_store], 0, group_sems.at[my_store // group_size], "store", trainer)

    def send_w1(peer):
        send(w1_own, w1_all.at[my_feat, pl.ds(0, 2 * width)], 1, recv_sems.at[1], "feat", peer)

    def outward(k, carry):
        serve_and_send(store_peer(k))
        serve_and_send(store_peer(-k))
        return carry

    half_store = n_store // 2
    shared = min(half_store, n_feat)

    def outward_both(k, carry):
        outward(k, carry)
        send_w1(feat_peer(k))
        return carry

    lax.fori_loop(1, shared, outward_both, 0)
    lax.fori_loop(shared, half_store, outward, 0)
    for k in range(shared, n_feat):
        send_w1(feat_peer(k))
    serve_and_send(store_peer(half_store))
    serve(my_store)
    keep(stage.at[my_store], rows_in.at[my_store], group_sems.at[my_store // group_size])
    keep(w1_own, w1_all.at[my_feat, pl.ds(0, 2 * width)], recv_sems.at[1])

    raw = index_one[0]
    owners = raw // cap
    place = (raw & (cap - 1)).astype(F32)
    counts = jnp.ones(raw.shape, F32)
    for owner in range(n_store):
        counts = jnp.where(owners == owner, row_counts[0:1, owner : owner + 1].astype(F32), counts)
    place = place - jnp.floor((place + 0.5) / counts) * counts
    owner_of[0:entries, :] = owners
    place = place.astype(jnp.int32)
    slot_ids = lax.broadcasted_iota(jnp.int32, (cap, nodes), 0)
    for entry in range(entries):
        pick[entry] = jnp.where(slot_ids == place[entry : entry + 1, :], 1.0, 0.0).astype(BF16)

    strip = 64
    targets = index_two.shape[2]

    def second_tables(part, carry):
        node_ids = lax.broadcasted_iota(jnp.int32, (strip, targets), 0) + part * strip
        at = pl.ds(pl.multiple_of(part * strip, strip), strip)
        self_t[at, :] = jnp.where(node_ids == index_two[0, 0:1, :], 1.0, 0.0).astype(BF16)
        total = jnp.zeros((strip, targets), F32)
        for entry in range(1, fan_two + 1):
            total += jnp.where(node_ids == index_two[0, entry : entry + 1, :], 1.0, 0.0)
        count_t[at, :] = total.astype(BF16)
        return carry

    lax.fori_loop(0, nodes // strip, second_tables, 0)

    both[...] = jnp.zeros_like(both)

    def gather(entry, group, at):
        found = dot(rows_in[pl.ds(group * group_size, group_size)].reshape(group_size * width, cap), pick[entry])
        of = owner_of[pl.ds(entry, 1), :]
        total = both[at : at + width, :]
        for member in range(group_size):
            total += jnp.where(
                of == group * group_size + member, found[member * width : (member + 1) * width, :], 0.0
            )
        both[at : at + width, :] = total

    for group in range(n_store // group_size):
        await_bytes(rows_in.at[pl.ds(group * group_size, group_size)], group_sems.at[group])
        gather(0, group, 0)

        def neighbours(entry, carry, group=group):
            gather(entry, group, width)
            return carry

        lax.fori_loop(1, entries, neighbours, 0)
    both[width : 2 * width, :] = both[width : 2 * width, :] / fan_one
    node_inputs = both[0 : 2 * width, :].astype(BF16)
    turned = both[...].T.astype(BF16)
    for group in range(n_feat):
        nodes_out[group] = turned[group * own_rows : (group + 1) * own_rows, :]

    each_feat(lambda peer: send(nodes_out.at[peer], nodes_in.at[my_feat], 2, recv_sems.at[2], "feat", peer))
    keep(nodes_out.at[my_feat], nodes_in.at[my_feat], recv_sems.at[2])

    await_bytes(w1_all.at[:, pl.ds(0, 2 * width)], recv_sems.at[1])
    await_bytes(nodes_in, recv_sems.at[2])
    own_nodes = jnp.concatenate([nodes_in[group] for group in range(n_feat)], axis=1)
    pre_one = dot(own_nodes, w1_all[...].reshape(n_feat * w1_all.shape[1], hidden))
    hid_own[...] = (pre_one * jax.nn.sigmoid(pre_one)).astype(BF16)
    each_feat(lambda peer: send(hid_own, hid_all.at[my_feat], 3, recv_sems.at[3], "feat", peer))
    keep(hid_own, hid_all.at[my_feat], recv_sems.at[3])
    slope_one = slope(pre_one)
    await_bytes(hid_all, recv_sems.at[3])

    hid = hid_all[...].reshape(nodes, hidden)
    w2 = jnp.concatenate([w2_self[...], w2_neigh[...]], axis=0)
    mixed = nt_dot(w2, hid)
    upper, lower = halves(mixed)
    self_term = dot(jnp.concatenate([upper[:units], lower[:units]], axis=0), self_t[...])
    neigh_term = dot(jnp.concatenate([upper[units:], lower[units:]], axis=0), count_t[...])
    pre_two = self_term[:units] + self_term[units:] + (neigh_term[:units] + neigh_term[units:]) / fan_two
    h2[...] = (pre_two * jax.nn.sigmoid(pre_two)).astype(BF16)
    grad_two = (out_grad[...].astype(F32) * slope(pre_two)).astype(BF16)
    node_grad = jnp.concatenate([nt_dot(grad_two, self_t[...]), nt_dot(grad_two, count_t[...]) / fan_two], axis=0)
    upper, lower = halves(node_grad.T)
    back = dot(jnp.concatenate([upper, lower], axis=1), jnp.concatenate([w2, w2], axis=0))
    back_out[...] = back.astype(BF16).reshape(n_feat, own_rows, hidden)
    each_feat(lambda peer: send(back_out.at[peer], back_in.at[my_feat], 4, recv_sems.at[4], "feat", peer))
    keep(back_out.at[my_feat], back_in.at[my_feat], recv_sems.at[4])

    upper, lower = halves(node_grad)
    grad_w2 = dot(jnp.concatenate([upper, lower], axis=0), hid)
    grad_w2 = (grad_w2[: 2 * units] + grad_w2[2 * units :]).astype(BF16)
    across = hidden // 128
    for row in range(2 * units // 16):
        for col in range(across):
            tiles2[row * across + col] = grad_w2[row * 16 : (row + 1) * 16, col * 128 : (col + 1) * 128]
    share2 = tiles2.shape[0] // n_store
    each_store(
        lambda peer: send(
            tiles2.at[pl.ds(peer * share2, share2)], tiles2_in.at[my_store], 5, recv_sems.at[5], "store", peer
        )
    )
    keep(tiles2.at[pl.ds(my_store * share2, share2)], tiles2_in.at[my_store], recv_sems.at[5])

    await_bytes(back_in, recv_sems.at[4])
    total = back_in[0].astype(F32)
    for group in range(1, n_feat):
        total += back_in[group].astype(F32)
    slope_own[...] = (total * slope_one).astype(BF16)
    each_feat(lambda peer: send(slope_own, slope_all.at[my_feat], 6, recv_sems.at[6], "feat", peer))
    keep(slope_own, slope_all.at[my_feat], recv_sems.at[6])

    await_bytes(tiles2_in, recv_sems.at[5])
    total = tiles2_in[0].astype(F32)
    for store in range(1, n_store):
        total += tiles2_in[store].astype(F32)
    sum2[...] = total.astype(BF16)
    each_store(
        lambda peer: send(sum2, sum2_all.at[pl.ds(my_store * share2, share2)], 7, recv_sems.at[7], "store", peer)
    )
    keep(sum2, sum2_all.at[pl.ds(my_store * share2, share2)], recv_sems.at[7])

    await_bytes(slope_all, recv_sems.at[6])
    grad_w1 = dot(node_inputs, slope_all[...].reshape(nodes, hidden)).astype(BF16)
    for row in range(2 * width // 16):
        for col in range(across):
            tiles1[row * across + col] = grad_w1[row * 16 : (row + 1) * 16, col * 128 : (col + 1) * 128]
    share1 = sum1.shape[0]
    summers = tiles1.shape[0] // share1

    def send_tiles1(peer):
        @pl.when(peer < summers)
        def _():
            send(tiles1.at[pl.ds(peer * share1, share1)], tiles1_in.at[my_store], 8, recv_sems.at[8], "store", peer)

    each_store(send_tiles1)

    await_bytes(sum2_all, recv_sems.at[7])
    for row in range(2 * units // 16):
        out, at = (out_w2s, row * 16) if row * 16 < units else (out_w2n, row * 16 - units)
        for col in range(across):
            out[at : at + 16, col * 128 : (col + 1) * 128] = sum2_all[row * across + col].astype(F32)

    @pl.when(my_store < summers)
    def _():
        keep(tiles1.at[pl.ds(my_store * share1, share1)], tiles1_in.at[my_store], recv_sems.at[8])
        await_bytes(tiles1_in, recv_sems.at[8])
        total = tiles1_in[0].astype(F32)
        for store in range(1, n_store):
            total += tiles1_in[store].astype(F32)
        sum1[...] = total.astype(BF16)
        each_store(
            lambda peer: send(sum1, sum1_all.at[pl.ds(my_store * share1, share1)], 9, recv_sems.at[9], "store", peer)
        )
        keep(sum1, sum1_all.at[pl.ds(my_store * share1, share1)], recv_sems.at[9])

    await_bytes(sum1_all, recv_sems.at[9])
    for row in range(2 * width // 16):
        out, at = (out_w1s, row * 16) if row * 16 < width else (out_w1n, row * 16 - width)
        for col in range(across):
            out[at : at + 16, col * 128 : (col + 1) * 128] = sum1_all[row * across + col].astype(F32)

    await_bytes(stage.at[pl.ds(0, n_store - 1)], send_sems.at[0])
    await_bytes(w1_all.at[pl.ds(0, n_feat - 1), pl.ds(0, 2 * width)], send_sems.at[1])
    await_bytes(nodes_out.at[pl.ds(0, n_feat - 1)], send_sems.at[2])
    await_bytes(hid_all.at[pl.ds(0, n_feat - 1)], send_sems.at[3])
    await_bytes(back_out.at[pl.ds(0, n_feat - 1)], send_sems.at[4])
    await_bytes(tiles2.at[pl.ds(0, (n_store - 1) * share2)], send_sems.at[5])
    await_bytes(slope_all.at[pl.ds(0, n_feat - 1)], send_sems.at[6])
    await_bytes(sum2_all.at[pl.ds(0, (n_store - 1) * share2)], send_sems.at[7])
    await_bytes(tiles1.at[pl.ds(0, (summers - 1) * share1)], send_sems.at[8])

    @pl.when(my_store >= summers)
    def _():
        await_bytes(tiles1.at[pl.ds(0, share1)], send_sems.at[8])

    @pl.when(my_store < summers)
    def _():
        await_bytes(tiles1_in.at[pl.ds(0, n_store - 1)], send_sems.at[9])


def body(n_store, n_feat, *args):
    features, serve_rows, _, index_one, index_two, w1_self, _, w2_self, _, out_grad = args
    width, papers = features.shape
    cap = serve_rows.shape[2]
    entries, nodes = index_one.shape[1:]
    targets = index_two.shape[2]
    hidden, units = w2_self.shape[1], w2_self.shape[0]
    own_rows = nodes // n_feat
    padded = -(-2 * width // 128) * 128
    tiles2 = 2 * units // 16 * (hidden // 128)
    tiles1 = 2 * width // 16 * (hidden // 128)
    share2 = tiles2 // n_store
    share1 = -(-tiles1 // n_store)
    groups = 4
    scratch = [
        pltpu.VMEM((papers // LOW * width, LOW), BF16),
        pltpu.VMEM((n_store, width, cap), BF16),
        pltpu.VMEM((n_store, width, cap), BF16),
        pltpu.VMEM((entries, nodes), jnp.int32),
        pltpu.VMEM((entries, cap, nodes), BF16),
        pltpu.VMEM((padded, nodes), F32),
        pltpu.VMEM((n_feat, own_rows, padded), BF16),
        pltpu.VMEM((n_feat, own_rows, padded), BF16),
        pltpu.VMEM((2 * width, hidden), BF16),
        pltpu.VMEM((n_feat, padded, hidden), BF16),
        pltpu.VMEM((own_rows, hidden), BF16),
        pltpu.VMEM((n_feat, own_rows, hidden), BF16),
        pltpu.VMEM((nodes, targets), BF16),
        pltpu.VMEM((nodes, targets), BF16),
        pltpu.VMEM((n_feat, own_rows, hidden), BF16),
        pltpu.VMEM((n_feat, own_rows, hidden), BF16),
        pltpu.VMEM((own_rows, hidden), BF16),
        pltpu.VMEM((n_feat, own_rows, hidden), BF16),
        pltpu.VMEM((tiles2, 16, 128), BF16),
        pltpu.VMEM((n_store, share2, 16, 128), BF16),
        pltpu.VMEM((share2, 16, 128), BF16),
        pltpu.VMEM((tiles2, 16, 128), BF16),
        pltpu.VMEM((tiles1, 16, 128), BF16),
        pltpu.VMEM((n_store, share1, 16, 128), BF16),
        pltpu.VMEM((share1, 16, 128), BF16),
        pltpu.VMEM((tiles1, 16, 128), BF16),
        pltpu.SemaphoreType.DMA((10,)),
        pltpu.SemaphoreType.DMA((10,)),
        pltpu.SemaphoreType.DMA((groups,)),
    ]
    return pl.pallas_call(
        functools.partial(kernel, n_store, n_feat),
        out_shape=[
            jax.ShapeDtypeStruct((units, targets), BF16),
            jax.ShapeDtypeStruct((width, hidden), F32),
            jax.ShapeDtypeStruct((width, hidden), F32),
            jax.ShapeDtypeStruct((units, hidden), F32),
            jax.ShapeDtypeStruct((units, hidden), F32),
        ],
        in_specs=[pl.BlockSpec(memory_space=pltpu.VMEM)] * len(args),
        out_specs=[pl.BlockSpec(memory_space=pltpu.VMEM)] * 5,
        scratch_shapes=scratch,
        compiler_params=pltpu.CompilerParams(
            collective_id=0, has_side_effects=True, vmem_limit_bytes=48 * 1024 * 1024
        ),
    )(*args)


def solution(mesh):
    return jax.shard_map(
        functools.partial(body, mesh.shape["store"], mesh.shape["feat"]),
        mesh=mesh,
        in_specs=(
            P("feat", "store"),
            P("store", None, None),
            P("store", None),
            P("store", None, None),
            P("store", None, None),
            P("feat", None),
            P("feat", None),
            P("feat", None),
            P("feat", None),
            P("feat", "store"),
        ),
        out_specs=(
            P("feat", "store"),
            P("feat", None),
            P("feat", None),
            P("feat", None),
            P("feat", None),
        ),
        check_vma=False,
    )
```

```python
import functools

import jax
import jax.numpy as jnp
from jax import lax
from jax.experimental import pallas as pl
from jax.experimental.pallas import tpu as pltpu
from jax.sharding import PartitionSpec as P

MESH = pl.DeviceIdType.MESH
F32 = jnp.float32
BF16 = jnp.bfloat16
LOW = 256


def slope(values):
    sig = jax.nn.sigmoid(values)
    return sig * (1.0 + values * (1.0 - sig))


def nt_dot(left, right):
    return lax.dot_general(left, right, (((1,), (1,)), ((), ())), preferred_element_type=F32)


def dot(left, right):
    return jnp.dot(left, right, preferred_element_type=F32)


def halves(values):
    upper = values.astype(BF16)
    return upper, (values - upper.astype(F32)).astype(BF16)


def await_bytes(ref, sem):
    pltpu.make_async_copy(ref, ref, sem).wait()


SENDS = ("rows", "w1", "w1_swap", "nodes", "hid0", "hid1", "back0", "back1", "slope0", "slope1") + tuple(
    total + stage for total in ("w2", "w1_0", "w1_1") for stage in ("_merge", "_reduce", "_spread", "_swap")
)
INPUTS = 10
GROUPS = 8
HALVES = 2


def kernel(
    n_store,
    n_feat,
    features_hbm,
    serve_rows_hbm,
    row_counts_hbm,
    index_one_hbm,
    index_two_hbm,
    w1_self_hbm,
    w1_neigh_hbm,
    w2_self_hbm,
    w2_neigh_hbm,
    out_grad_hbm,
    h2,
    out_w1s,
    out_w1n,
    out_w2s,
    out_w2n,
    features,
    serve_rows,
    row_counts,
    index_one,
    index_two,
    w2,
    out_grad,
    table,
    stage,
    rows_in,
    owner_of,
    pick,
    both,
    nodes_out,
    nodes_in,
    w1_own,
    w1_all,
    hid_own,
    hid_all,
    self_t,
    count_t,
    back_out,
    back_in,
    slope_own,
    slope_all,
    w2_total,
    w1_total_0,
    w1_total_1,
    input_sems,
    send_sems,
    recv_sems,
    group_sems,
):
    my_store, my_feat = lax.axis_index("store"), lax.axis_index("feat")
    my_chip, my_core = my_store // 2, lax.rem(my_store, 2)
    n_chip = n_store // 2
    width, papers = features.shape
    cap = serve_rows.shape[2]
    entries, nodes = index_one.shape[1:]
    fan_one = entries - 1
    fan_two = index_two.shape[1] - 1
    units, hidden = w2.shape[0] // 2, w2.shape[1]
    columns = hidden // HALVES
    own_rows = nodes // n_feat
    pad = both.shape[0] // 2
    pending = []

    def store_peer(step):
        return lax.rem(my_store + step + n_store, n_store)

    def feat_peer(step):
        return lax.rem(my_feat + step + n_feat, n_feat)

    def chip_peer(step):
        return lax.rem(my_chip + step + n_chip, n_chip)

    def send(src, dst, name, recv_sem, axis, peer):
        pltpu.make_async_remote_copy(
            src_ref=src,
            dst_ref=dst,
            send_sem=send_sems.at[SENDS.index(name)],
            recv_sem=recv_sem,
            device_id={axis: peer},
            device_id_type=MESH,
        ).start()

    def recv_of(name):
        return recv_sems.at[SENDS.index(name)]

    def later(ref, name):
        pending.append(lambda: await_bytes(ref, send_sems.at[SENDS.index(name)]))

    def keep(src, dst, sem):
        pltpu.make_async_copy(src, dst, sem).start()

    def loop(low, high, fn):
        def step(k, carry):
            fn(k)
            return carry

        lax.fori_loop(low, high, step, 0)

    def share(src_of, dst, name):
        loop(1, n_feat, lambda k: send(src_of(feat_peer(k)), dst, name, recv_of(name), "feat", feat_peer(k)))
        keep(src_of(my_feat), dst, recv_of(name))

    barrier = pltpu.get_barrier_semaphore()

    def greet(axis, peer):
        pl.semaphore_signal(barrier, inc=1, device_id={axis: peer}, device_id_type=MESH)

    reads = (
        (features_hbm, features),
        (serve_rows_hbm, serve_rows),
        (w1_self_hbm, w1_own.at[0]),
        (w1_neigh_hbm, w1_own.at[1]),
        (row_counts_hbm, row_counts),
        (index_one_hbm, index_one),
        (index_two_hbm, index_two),
        (w2_self_hbm, w2.at[pl.ds(0, units)]),
        (w2_neigh_hbm, w2.at[pl.ds(units, units)]),
        (out_grad_hbm, out_grad),
    )
    reads = [pltpu.make_async_copy(src, dst, input_sems.at[i]) for i, (src, dst) in enumerate(reads)]
    for read in reads:
        read.start()
    loop(1, n_store, lambda k: greet("store", store_peer(k)))
    loop(1, n_feat, lambda k: greet("feat", feat_peer(k)))
    for group in range(n_feat):
        for half in range(2):
            w1_all[group, half, width:, :] = jnp.zeros((pad - width, hidden), BF16)
    both[...] = jnp.zeros_like(both)

    reads[0].wait()
    reads[1].wait()
    highs = papers // LOW
    for high in range(highs):
        table[high * width : (high + 1) * width, :] = features[:, high * LOW : (high + 1) * LOW].astype(BF16)
    low_ids = lax.broadcasted_iota(jnp.int32, (LOW, cap), 0)

    def serve(trainer):
        wanted = serve_rows[0, pl.ds(trainer, 1), :]
        low, high_of = wanted & (LOW - 1), wanted // LOW
        one_hot = jnp.where(low_ids == low, 1.0, 0.0).astype(BF16)
        found = dot(table[...], one_hot)
        total = jnp.zeros((width, cap), F32)
        for high in range(highs):
            total += jnp.where(high_of == high, found[high * width : (high + 1) * width, :], 0.0)
        stage[trainer] = total.astype(BF16)

    loop(0, n_store, serve)
    for read in reads[2:]:
        read.wait()
    pl.semaphore_wait(barrier, n_store + n_feat - 2)

    half_store = n_store // 2
    group_size = n_store // GROUPS

    def send_rows(trainer, rank):
        send(stage.at[trainer], rows_in.at[rank], "rows", group_sems.at[rank // group_size], "store", trainer)

    def send_w1(peer):
        send(w1_own.at[my_core], w1_all.at[my_feat, my_core, pl.ds(0, width)], "w1", recv_of("w1"), "feat", peer)

    def send_pair(i):
        send_rows(store_peer(half_store - i), 2 * i - 1)
        send_rows(store_peer(i - half_store), 2 * i)

    def send_pair_and_w1(i):
        send_pair(i)
        send_w1(feat_peer(i))

    send_rows(store_peer(half_store), 0)
    shared = min(half_store, n_feat)
    loop(1, shared, send_pair_and_w1)
    loop(shared, half_store, send_pair)
    loop(shared, n_feat, lambda i: send_w1(feat_peer(i)))
    keep(stage.at[my_store], rows_in.at[n_store - 1], group_sems.at[GROUPS - 1])
    keep(w1_own.at[my_core], w1_all.at[my_feat, my_core, pl.ds(0, width)], recv_of("w1"))
    later(stage.at[pl.ds(0, n_store - 1)], "rows")
    later(w1_all.at[pl.ds(0, n_feat - 1), 0, pl.ds(0, width)], "w1")

    raw = index_one[0]
    owners = raw // cap
    place = (raw & (cap - 1)).astype(F32)
    counts = jnp.ones(raw.shape, F32)
    for owner in range(n_store):
        counts = jnp.where(owners == owner, row_counts[0:1, owner : owner + 1].astype(F32), counts)
    place = place - jnp.floor((place + 0.5) / counts) * counts
    owner_of[0:entries, :] = owners
    place = place.astype(jnp.int32)
    slot_ids = lax.broadcasted_iota(jnp.int32, (cap, nodes), 0)
    for entry in range(entries):
        pick[entry] = jnp.where(slot_ids == place[entry : entry + 1, :], 1.0, 0.0).astype(BF16)

    strip = 64
    targets = index_two.shape[2]

    def second_tables(part):
        node_ids = lax.broadcasted_iota(jnp.int32, (strip, targets), 0) + part * strip
        at = pl.ds(pl.multiple_of(part * strip, strip), strip)
        self_t[at, :] = jnp.where(node_ids == index_two[0, 0:1, :], 1.0, 0.0).astype(BF16)
        total = jnp.zeros((strip, targets), F32)
        for entry in range(1, fan_two + 1):
            total += jnp.where(node_ids == index_two[0, entry : entry + 1, :], 1.0, 0.0)
        count_t[at, :] = total.astype(BF16)

    loop(0, nodes // strip, second_tables)

    def gather(entry, group, at):
        found = dot(rows_in[pl.ds(group * group_size, group_size)].reshape(group_size * width, cap), pick[entry])
        of = owner_of[pl.ds(entry, 1), :]
        total = both[at : at + width, :]
        for member in range(group_size):
            rank = group * group_size + member
            offset = half_store - (rank + 1) // 2 if rank % 2 else rank // 2 - half_store
            total += jnp.where(of == store_peer(-offset), found[member * width : (member + 1) * width, :], 0.0)
        both[at : at + width, :] = total

    for group in range(GROUPS):
        await_bytes(rows_in.at[pl.ds(group * group_size, group_size)], group_sems.at[group])
        gather(0, group, 0)
        loop(1, entries, lambda entry, group=group: gather(entry, group, pad))
        if group == GROUPS - 3:
            await_bytes(w1_all.at[:, 0, pl.ds(0, width)], recv_of("w1"))
            mine = w1_all.at[:, my_core, pl.ds(0, width)]
            send(mine, mine, "w1_swap", recv_of("w1_swap"), "store", my_store + 1 - 2 * my_core)
            later(w1_all.at[:, 0, pl.ds(0, width)], "w1_swap")
    both[pad : pad + width, :] = both[pad : pad + width, :] / fan_one
    node_inputs = both[...].astype(BF16)
    turned = both[...].T.astype(BF16)
    for group in range(n_feat):
        nodes_out[group] = turned[group * own_rows : (group + 1) * own_rows, :]

    share(lambda peer: nodes_out.at[peer], nodes_in.at[my_feat], "nodes")
    later(nodes_out.at[pl.ds(0, n_feat - 1)], "nodes")

    await_bytes(w1_all.at[:, 0, pl.ds(0, width)], recv_of("w1_swap"))
    await_bytes(nodes_in, recv_of("nodes"))
    own_nodes = jnp.concatenate([nodes_in[group] for group in range(n_feat)], axis=1)
    slope_one = []
    for half in range(HALVES):
        cols = slice(half * columns, (half + 1) * columns)
        pre_one = dot(own_nodes, w1_all[:, :, :, cols].reshape(n_feat * 2 * pad, columns))
        hid_own[half] = (pre_one * jax.nn.sigmoid(pre_one)).astype(BF16)
        name = f"hid{half}"
        share(lambda peer, half=half: hid_own.at[half], hid_all.at[half, my_feat], name)
        later(hid_all.at[half, pl.ds(0, n_feat - 1)], name)
        slope_one.append(slope(pre_one))

    mixed = jnp.zeros((2 * units, nodes), F32)
    hid = []
    for half in range(HALVES):
        await_bytes(hid_all.at[half], recv_of(f"hid{half}"))
        hid.append(hid_all[half].reshape(nodes, columns))
        mixed += nt_dot(w2[:, half * columns : (half + 1) * columns], hid[half])
    upper, lower = halves(mixed)
    self_term = dot(jnp.concatenate([upper[:units], lower[:units]], axis=0), self_t[...])
    neigh_term = dot(jnp.concatenate([upper[units:], lower[units:]], axis=0), count_t[...])
    pre_two = self_term[:units] + self_term[units:] + (neigh_term[:units] + neigh_term[units:]) / fan_two
    grad_two = (out_grad[...].astype(F32) * slope(pre_two)).astype(BF16)
    node_grad = jnp.concatenate([nt_dot(grad_two, self_t[...]), nt_dot(grad_two, count_t[...]) / fan_two], axis=0)
    upper, lower = halves(node_grad.T)
    turned = jnp.concatenate([upper, lower], axis=1)
    for half in range(HALVES):
        weights = w2[:, half * columns : (half + 1) * columns]
        back = dot(turned, jnp.concatenate([weights, weights], axis=0))
        back_out[half] = back.astype(BF16).reshape(n_feat, own_rows, columns)
        name = f"back{half}"
        share(lambda peer, half=half: back_out.at[half, peer], back_in.at[half, my_feat], name)
        later(back_out.at[half, pl.ds(0, n_feat - 1)], name)
    h2[...] = (pre_two * jax.nn.sigmoid(pre_two)).astype(BF16)

    sibling = my_store + 1 - 2 * my_core

    def total_of(ref, name):
        tiles = ref.shape[1] // 2
        per = -(-tiles // n_chip)
        summers = tiles // per
        spread = summers * 4 == n_chip * 3

        def sums(chip):
            return lax.rem(chip, 4) != 3 if spread else chip < summers

        def first(chip):
            return (chip - chip // 4 if spread else chip) * per

        part, merged = ref.at[0], ref.at[1]
        arrived, total = ref.at[2], ref.at[3]

        def fill(half, grad, row0=0):
            across = grad.shape[1] // 128
            for row in range(grad.shape[0] // 16):
                for col in range(across):
                    part[half * tiles + row * across + col] = grad[
                        row * 16 : (row + 1) * 16, col * 128 : (col + 1) * 128
                    ]

        def merge():
            own = pl.ds((1 - my_core) * tiles, tiles)
            send(part.at[own], merged.at[pl.ds(0, tiles)], name + "_merge", recv_of(name + "_merge"), "store", sibling)
            later(part.at[pl.ds(0, tiles)], name + "_merge")

        def reduce():
            await_bytes(merged.at[pl.ds(0, tiles)], recv_of(name + "_merge"))
            both_cores = part[pl.ds(my_core * tiles, tiles)].astype(F32) + merged[0:tiles].astype(F32)
            merged[tiles : 2 * tiles] = both_cores.astype(BF16)

            def to(k):
                chip = chip_peer(k)

                @pl.when(sums(chip))
                def _():
                    send(
                        merged.at[pl.ds(tiles + first(chip), per)],
                        arrived.at[pl.ds(my_chip * per, per)],
                        name + "_reduce",
                        recv_of(name + "_reduce"),
                        "store",
                        chip * 2 + my_core,
                    )

            loop(1, n_chip, to)

            def sent():
                for count, wait_here in ((summers - 1, sums(my_chip)), (summers, jnp.logical_not(sums(my_chip)))):
                    if summers == n_chip and count == n_chip:
                        continue

                    @pl.when(wait_here)
                    def _(count=count):
                        await_bytes(merged.at[pl.ds(0, count * per)], send_sems.at[SENDS.index(name + "_reduce")])

            pending.append(sent)

        def spread_out():
            @pl.when(sums(my_chip))
            def _():
                mine = pl.ds(first(my_chip), per)
                keep(
                    merged.at[pl.ds(tiles + first(my_chip), per)],
                    arrived.at[pl.ds(my_chip * per, per)],
                    recv_of(name + "_reduce"),
                )
                await_bytes(arrived.at[pl.ds(0, n_chip * per)], recv_of(name + "_reduce"))
                summed = arrived[0:per].astype(F32)
                for chip in range(1, n_chip):
                    summed += arrived[chip * per : (chip + 1) * per].astype(F32)
                at = pl.ds(my_core * tiles + first(my_chip), per)
                total[at] = summed.astype(BF16)
                loop(
                    1,
                    n_chip,
                    lambda k: send(
                        total.at[at],
                        total.at[at],
                        name + "_spread",
                        recv_of(name + "_spread"),
                        "store",
                        chip_peer(k) * 2 + my_core,
                    ),
                )

            def sent():
                @pl.when(sums(my_chip))
                def _():
                    await_bytes(arrived.at[pl.ds(0, (n_chip - 1) * per)], send_sems.at[SENDS.index(name + "_spread")])

            pending.append(sent)

        def swap():
            for count, wait_here in ((summers - 1, sums(my_chip)), (summers, jnp.logical_not(sums(my_chip)))):
                if summers == n_chip and count == n_chip:
                    continue

                @pl.when(wait_here)
                def _(count=count):
                    await_bytes(total.at[pl.ds(0, count * per)], recv_of(name + "_spread"))

            mine = total.at[pl.ds(my_core * tiles, tiles)]
            send(mine, mine, name + "_swap", recv_of(name + "_swap"), "store", sibling)
            later(total.at[pl.ds(0, tiles)], name + "_swap")

        def write(outs, col0, cols, rows):
            await_bytes(total.at[pl.ds(0, tiles)], recv_of(name + "_swap"))
            across = cols // 128
            for half, out in enumerate(outs):
                for row in range(rows // 16):
                    for col in range(across):
                        out[row * 16 : (row + 1) * 16, col0 + col * 128 : col0 + (col + 1) * 128] = total[
                            half * tiles + row * across + col
                        ].astype(F32)

        return fill, merge, reduce, spread_out, swap, write

    fill, merge, reduce2, spread2, swap2, write2 = total_of(w2_total, "w2")
    upper, lower = halves(node_grad)
    stacked = jnp.concatenate([upper, lower], axis=0)
    grad_w2 = jnp.concatenate([dot(stacked, part) for part in hid], axis=1)
    grad_w2 = (grad_w2[: 2 * units] + grad_w2[2 * units :]).astype(BF16)
    fill(0, grad_w2[:units])
    fill(1, grad_w2[units:])
    merge()
    reduce2()

    for half in range(HALVES):
        name = f"back{half}"
        await_bytes(back_in.at[half], recv_of(name))
        total = back_in[half, 0].astype(F32)
        for group in range(1, n_feat):
            total += back_in[half, group].astype(F32)
        slope_own[half] = (total * slope_one[half]).astype(BF16)
        name = f"slope{half}"
        share(lambda peer, half=half: slope_own.at[half], slope_all.at[half, my_feat], name)
        later(slope_all.at[half, pl.ds(0, n_feat - 1)], name)
    spread2()

    steps = []
    for half, ref in enumerate((w1_total_0, w1_total_1)):
        await_bytes(slope_all.at[half], recv_of(f"slope{half}"))
        grad_w1 = dot(node_inputs, slope_all[half].reshape(nodes, columns)).astype(BF16)
        fill, merge, *rest = total_of(ref, f"w1_{half}")
        steps.append(rest)
        fill(0, grad_w1[0:width])
        fill(1, grad_w1[pad : pad + width])
        merge()
        rest[0]()
    swap2()
    steps[0][1]()
    steps[1][1]()
    write2((out_w2s, out_w2n), 0, hidden, units)
    steps[0][2]()
    steps[1][2]()
    steps[0][3]((out_w1s, out_w1n), 0, columns, width)
    steps[1][3]((out_w1s, out_w1n), columns, columns, width)

    for wait in pending:
        wait()


def body(n_store, n_feat, *args):
    features, serve_rows, _, index_one, index_two, w1_self, _, w2_self, _, out_grad = args
    width, papers = features.shape
    cap = serve_rows.shape[2]
    entries, nodes = index_one.shape[1:]
    targets = index_two.shape[2]
    hidden, units = w2_self.shape[1], w2_self.shape[0]
    own_rows = nodes // n_feat
    pad = -(-width // 64) * 64
    columns = hidden // HALVES
    blocks = (HALVES, n_feat, own_rows, columns)
    tiles2 = units // 16 * (hidden // 128)
    tiles1 = width // 16 * (columns // 128)

    def total_scratch(tiles):
        per = -(-tiles // (n_store // 2))
        return pltpu.VMEM((4, max(2 * tiles, n_store // 2 * per), 16, 128), BF16)

    scratch = [
        pltpu.VMEM(features.shape, F32),
        pltpu.VMEM(serve_rows.shape, jnp.int32),
        pltpu.VMEM(args[2].shape, jnp.int32),
        pltpu.VMEM(index_one.shape, jnp.int32),
        pltpu.VMEM(index_two.shape, jnp.int32),
        pltpu.VMEM((2 * units, hidden), BF16),
        pltpu.VMEM(out_grad.shape, BF16),
        pltpu.VMEM((papers // LOW * width, LOW), BF16),
        pltpu.VMEM((n_store, width, cap), BF16),
        pltpu.VMEM((n_store, width, cap), BF16),
        pltpu.VMEM((entries, nodes), jnp.int32),
        pltpu.VMEM((entries, cap, nodes), BF16),
        pltpu.VMEM((2 * pad, nodes), F32),
        pltpu.VMEM((n_feat, own_rows, 2 * pad), BF16),
        pltpu.VMEM((n_feat, own_rows, 2 * pad), BF16),
        pltpu.VMEM((2, width, hidden), BF16),
        pltpu.VMEM((n_feat, 2, pad, hidden), BF16),
        pltpu.VMEM((HALVES, own_rows, columns), BF16),
        pltpu.VMEM(blocks, BF16),
        pltpu.VMEM((nodes, targets), BF16),
        pltpu.VMEM((nodes, targets), BF16),
        pltpu.VMEM(blocks, BF16),
        pltpu.VMEM(blocks, BF16),
        pltpu.VMEM((HALVES, own_rows, columns), BF16),
        pltpu.VMEM(blocks, BF16),
        total_scratch(tiles2),
        total_scratch(tiles1),
        total_scratch(tiles1),
        pltpu.SemaphoreType.DMA((INPUTS,)),
        pltpu.SemaphoreType.DMA((len(SENDS),)),
        pltpu.SemaphoreType.DMA((len(SENDS),)),
        pltpu.SemaphoreType.DMA((GROUPS,)),
    ]
    return pl.pallas_call(
        functools.partial(kernel, n_store, n_feat),
        out_shape=[
            jax.ShapeDtypeStruct((units, targets), BF16),
            jax.ShapeDtypeStruct((width, hidden), F32),
            jax.ShapeDtypeStruct((width, hidden), F32),
            jax.ShapeDtypeStruct((units, hidden), F32),
            jax.ShapeDtypeStruct((units, hidden), F32),
        ],
        in_specs=[pl.BlockSpec(memory_space=pl.ANY)] * len(args),
        out_specs=[pl.BlockSpec(memory_space=pltpu.VMEM)] * 5,
        scratch_shapes=scratch,
        compiler_params=pltpu.CompilerParams(
            collective_id=0, has_side_effects=True, vmem_limit_bytes=48 * 1024 * 1024
        ),
    )(*args)


def solution(mesh):
    return jax.shard_map(
        functools.partial(body, mesh.shape["store"], mesh.shape["feat"]),
        mesh=mesh,
        in_specs=(
            P("feat", "store"),
            P("store", None, None),
            P("store", None),
            P("store", None, None),
            P("store", None, None),
            P("feat", None),
            P("feat", None),
            P("feat", None),
            P("feat", None),
            P("feat", "store"),
        ),
        out_specs=(
            P("feat", "store"),
            P("feat", None),
            P("feat", None),
            P("feat", None),
            P("feat", None),
        ),
        check_vma=False,
    )
```

```python
import functools

import jax
import jax.numpy as jnp
from jax import lax
from jax.experimental import pallas as pl
from jax.experimental.pallas import tpu as pltpu
from jax.sharding import PartitionSpec as P

MESH = pl.DeviceIdType.MESH
F32 = jnp.float32
BF16 = jnp.bfloat16
LOW = 256


def slope(values):
    sig = jax.nn.sigmoid(values)
    return sig * (1.0 + values * (1.0 - sig))


def nt_dot(left, right):
    return lax.dot_general(left, right, (((1,), (1,)), ((), ())), preferred_element_type=F32)


def dot(left, right):
    return jnp.dot(left, right, preferred_element_type=F32)


def halves(values):
    upper = values.astype(BF16)
    return upper, (values - upper.astype(F32)).astype(BF16)


def await_bytes(ref, sem):
    pltpu.make_async_copy(ref, ref, sem).wait()


SENDS = (
    ("rows", "w1", "w1_swap", "nodes")
    + tuple(what + half + step for what in ("hid", "back", "slope") for half in "01" for step in ("_near", "_far"))
    + tuple(total + step for total in ("w2", "w1_0", "w1_1") for step in ("_merge", "_reduce", "_spread", "_swap"))
)
INPUTS = 10
GROUPS = 8
HALVES = 2
VMEM_LIMIT = 60 * 1024 * 1024


def kernel(
    n_store,
    n_feat,
    features_hbm,
    serve_rows_hbm,
    row_counts_hbm,
    index_one_hbm,
    index_two_hbm,
    w1_self_hbm,
    w1_neigh_hbm,
    w2_self_hbm,
    w2_neigh_hbm,
    out_grad_hbm,
    h2,
    w2_sum,
    w1_sum_0,
    w1_sum_1,
    features,
    serve_rows,
    row_counts,
    index_rows,
    index_one,
    index_two,
    w2,
    out_grad,
    table,
    stage,
    rows_in,
    owner_of,
    pick,
    both,
    nodes_out,
    nodes_in,
    w1_own,
    w1_all,
    hid_own,
    hid_all,
    self_t,
    count_t,
    back_out,
    back_in_0,
    back_in_1,
    back_mid_0,
    back_mid_1,
    back_end_0,
    back_end_1,
    slope_own,
    slope_all,
    w2_total,
    w1_total_0,
    w1_total_1,
    input_sems,
    send_sems,
    recv_sems,
    group_sems,
):
    my_store, my_feat = lax.axis_index("store"), lax.axis_index("feat")
    my_chip, my_core = my_store // 2, lax.rem(my_store, 2)
    n_chip = n_store // 2
    n_x = 1 << (n_feat.bit_length() // 2)
    n_y = n_feat // n_x
    my_y, my_x = my_feat // n_x, lax.rem(my_feat, n_x)
    width, papers = features.shape
    cap = serve_rows.shape[2]
    entries, nodes = index_one.shape
    fan_one = entries - 1
    fan_two = index_two.shape[1] - 1
    units, hidden = w2.shape[0] // 2, w2.shape[1]
    columns = hidden // HALVES
    own_rows = nodes // n_feat
    pad = both.shape[0] // 2
    pending = []
    back_in, back_mid, back_end = (back_in_0, back_in_1), (back_mid_0, back_mid_1), (back_end_0, back_end_1)

    def store_peer(step):
        return lax.rem(my_store + step + n_store, n_store)

    def feat_peer(step):
        return lax.rem(my_feat + step + n_feat, n_feat)

    def chip_peer(step):
        return lax.rem(my_chip + step + n_chip, n_chip)

    def send(src, dst, name, recv_sem, axis, peer):
        pltpu.make_async_remote_copy(
            src_ref=src,
            dst_ref=dst,
            send_sem=send_sems.at[SENDS.index(name)],
            recv_sem=recv_sem,
            device_id={axis: peer},
            device_id_type=MESH,
        ).start()

    def recv_of(name):
        return recv_sems.at[SENDS.index(name)]

    def later(ref, name):
        pending.append(lambda: await_bytes(ref, send_sems.at[SENDS.index(name)]))

    def keep(src, dst, sem):
        pltpu.make_async_copy(src, dst, sem).start()

    def loop(low, high, fn):
        def step(k, carry):
            fn(k)
            return carry

        lax.fori_loop(low, high, step, 0)

    def share(src_of, dst, name):
        loop(1, n_feat, lambda k: send(src_of(feat_peer(k)), dst, name, recv_of(name), "feat", feat_peer(k)))
        keep(src_of(my_feat), dst, recv_of(name))

    def along(x, k):
        return my_y * n_x + lax.rem(my_x + k, n_x) if x else lax.rem(my_y + k, n_y) * n_x + my_x

    def count_of(x):
        return n_x if x else n_y

    def spread_near(name, own, dst, x):
        step, spot = name + "_near", dst.at[my_y, my_x]
        loop(1, count_of(x), lambda k: send(own, spot, step, recv_of(step), "feat", along(x, k)))
        keep(own, spot, recv_of(step))
        if count_of(x) > 1:
            later(dst.at[0, pl.ds(0, n_x - 1)] if x else dst.at[pl.ds(0, n_y - 1), 0], step)

    def spread_far(name, dst, x):
        step, line = name + "_far", dst.at[my_y] if x else dst.at[:, my_x]
        await_bytes(line, recv_of(name + "_near"))
        loop(1, count_of(not x), lambda k: send(line, line, step, recv_of(step), "feat", along(not x, k)))
        if count_of(not x) > 1:
            later(dst.at[pl.ds(0, n_y - 1)] if x else dst.at[:, pl.ds(0, n_x - 1)], step)

    def spread_end(name, dst, x):
        if count_of(not x) > 1:
            await_bytes(dst.at[pl.ds(0, n_y - 1)] if x else dst.at[:, pl.ds(0, n_x - 1)], recv_of(name + "_far"))

    def fold_far(name, src, dst, x):
        step, mine = name + "_far", my_x if x else my_y

        def lines(k):
            return src.at[:, lax.rem(my_x + k, n_x)] if x else src.at[lax.rem(my_y + k, n_y)]

        loop(1, count_of(x), lambda k: send(lines(k), dst.at[mine], step, recv_of(step), "feat", along(x, k)))
        keep(lines(0), dst.at[mine], recv_of(step))
        if count_of(x) > 1:
            later(dst.at[pl.ds(0, count_of(x) - 1)], step)

    def fold_near(name, src, middle, dst, x):
        await_bytes(src, recv_of(name + "_far"))
        total = src[0].astype(F32)
        for line in range(1, count_of(x)):
            total += src[line].astype(F32)
        middle[...] = total.astype(BF16)
        step, mine = name + "_near", my_y if x else my_x

        def block(k):
            return middle.at[lax.rem(my_y + k, n_y) if x else lax.rem(my_x + k, n_x)]

        loop(1, count_of(not x), lambda k: send(block(k), dst.at[mine], step, recv_of(step), "feat", along(not x, k)))
        keep(block(0), dst.at[mine], recv_of(step))
        if count_of(not x) > 1:
            later(dst.at[pl.ds(0, count_of(not x) - 1)], step)

    def fold_end(name, src, x):
        await_bytes(src, recv_of(name + "_near"))
        total = src[0].astype(F32)
        for line in range(1, count_of(not x)):
            total += src[line].astype(F32)
        return total

    barrier = pltpu.get_barrier_semaphore()

    def greet(axis, peer):
        pl.semaphore_signal(barrier, inc=1, device_id={axis: peer}, device_id_type=MESH)

    reads = (
        (features_hbm, features),
        (serve_rows_hbm, serve_rows),
        (w1_self_hbm, w1_own.at[0]),
        (w1_neigh_hbm, w1_own.at[1]),
        (row_counts_hbm, row_counts),
        (index_one_hbm, index_rows),
        (index_two_hbm, index_two),
        (w2_self_hbm, w2.at[pl.ds(0, units)]),
        (w2_neigh_hbm, w2.at[pl.ds(units, units)]),
        (out_grad_hbm, out_grad),
    )
    reads = [pltpu.make_async_copy(src, dst, input_sems.at[i]) for i, (src, dst) in enumerate(reads)]
    for read in reads:
        read.start()
    loop(1, n_store, lambda k: greet("store", store_peer(k)))
    loop(1, n_feat, lambda k: greet("feat", feat_peer(k)))
    for group in range(n_feat):
        for half in range(2):
            w1_all[group, half, width:, :] = jnp.zeros((pad - width, hidden), BF16)
    both[...] = jnp.zeros_like(both)

    reads[0].wait()
    reads[1].wait()
    highs = papers // LOW
    for high in range(highs):
        table[high * width : (high + 1) * width, :] = features[:, high * LOW : (high + 1) * LOW].astype(BF16)
    low_ids = lax.broadcasted_iota(jnp.int32, (LOW, cap), 0)

    def serve(trainer):
        wanted = serve_rows[0, pl.ds(trainer, 1), :]
        low, high_of = wanted & (LOW - 1), wanted // LOW
        one_hot = jnp.where(low_ids == low, 1.0, 0.0).astype(BF16)
        found = dot(table[...], one_hot)
        total = found[0:width, :]
        for high in range(1, highs):
            total = jnp.where(high_of == high, found[high * width : (high + 1) * width, :], total)
        stage[trainer] = total.astype(BF16)

    loop(0, n_store, serve)
    for read in reads[2:]:
        read.wait()
    pl.semaphore_wait(barrier, n_store + n_feat - 2)

    half_store = n_store // 2
    group_size = n_store // GROUPS

    def send_rows(trainer, rank):
        send(stage.at[trainer], rows_in.at[rank], "rows", group_sems.at[rank // group_size], "store", trainer)

    def send_w1(peer):
        send(w1_own.at[my_core], w1_all.at[my_feat, my_core, pl.ds(0, width)], "w1", recv_of("w1"), "feat", peer)

    def send_pair(i):
        send_rows(store_peer(half_store - i), 2 * i - 1)
        send_rows(store_peer(i - half_store), 2 * i)

    def send_pair_and_w1(i):
        send_pair(i)
        send_w1(feat_peer(i))

    send_rows(store_peer(half_store), 0)
    shared = min(half_store, n_feat)
    loop(1, shared, send_pair_and_w1)
    loop(shared, half_store, send_pair)
    loop(shared, n_feat, lambda i: send_w1(feat_peer(i)))
    keep(stage.at[my_store], rows_in.at[n_store - 1], group_sems.at[GROUPS - 1])
    keep(w1_own.at[my_core], w1_all.at[my_feat, my_core, pl.ds(0, width)], recv_of("w1"))
    later(stage.at[pl.ds(0, n_store - 1)], "rows")
    later(w1_all.at[pl.ds(0, n_feat - 1), 0, pl.ds(0, width)], "w1")

    for entry in range(entries):
        index_one[entry : entry + 1, :] = index_rows[entry]
    raw = index_one[...]
    owners = raw // cap
    place = (raw & (cap - 1)).astype(F32)
    counts = jnp.ones(raw.shape, F32)
    for owner in range(n_store):
        counts = jnp.where(owners == owner, row_counts[0:1, owner : owner + 1].astype(F32), counts)
    place = place - jnp.floor((place + 0.5) / counts) * counts
    owner_of[0:entries, :] = owners
    place = place.astype(jnp.int32)
    slot_ids = lax.broadcasted_iota(jnp.int32, (cap, nodes), 0)
    for entry in range(entries):
        pick[entry] = jnp.where(slot_ids == place[entry : entry + 1, :], 1.0, 0.0).astype(BF16)

    strip = 64
    targets = index_two.shape[2]

    def second_tables(part):
        node_ids = lax.broadcasted_iota(jnp.int32, (strip, targets), 0) + part * strip
        at = pl.ds(pl.multiple_of(part * strip, strip), strip)
        self_t[at, :] = jnp.where(node_ids == index_two[0, 0:1, :], 1.0, 0.0).astype(BF16)
        total = jnp.zeros((strip, targets), F32)
        for entry in range(1, fan_two + 1):
            total += jnp.where(node_ids == index_two[0, entry : entry + 1, :], 1.0, 0.0)
        count_t[at, :] = total.astype(BF16)

    loop(0, nodes // strip, second_tables)

    def gather(group):
        await_bytes(rows_in.at[pl.ds(group * group_size, group_size)], group_sems.at[group])
        arrived = rows_in[pl.ds(group * group_size, group_size)].reshape(group_size * width, cap)
        owners = []
        for member in range(group_size):
            rank = group * group_size + member
            offset = half_store - (rank + 1) // 2 if member % 2 else rank // 2 - half_store
            owners.append(store_peer(-offset))
        sums = [both[0:width, :], both[pad : pad + width, :]]
        for entry in range(entries):
            found = dot(arrived, pick[entry])
            of = owner_of[entry : entry + 1, :]
            mine = jnp.zeros((width, nodes), F32)
            for member in range(group_size):
                mine = jnp.where(of == owners[member], found[member * width : (member + 1) * width, :], mine)
            sums[min(entry, 1)] += mine
        both[0:width, :], both[pad : pad + width, :] = sums

    loop(0, GROUPS - 2, gather)
    await_bytes(w1_all.at[:, 0, pl.ds(0, width)], recv_of("w1"))
    mine = w1_all.at[:, my_core, pl.ds(0, width)]
    send(mine, mine, "w1_swap", recv_of("w1_swap"), "store", my_store + 1 - 2 * my_core)
    later(w1_all.at[:, 0, pl.ds(0, width)], "w1_swap")
    loop(GROUPS - 2, GROUPS, gather)
    both[pad : pad + width, :] = both[pad : pad + width, :] / fan_one
    node_inputs = both[...].astype(BF16)
    turned = both[...].T.astype(BF16)
    for group in range(n_feat):
        nodes_out[group] = turned[group * own_rows : (group + 1) * own_rows, :]

    share(lambda peer: nodes_out.at[peer], nodes_in.at[my_feat], "nodes")
    later(nodes_out.at[pl.ds(0, n_feat - 1)], "nodes")

    await_bytes(w1_all.at[:, 0, pl.ds(0, width)], recv_of("w1_swap"))
    await_bytes(nodes_in, recv_of("nodes"))
    own_nodes = jnp.concatenate([nodes_in[group] for group in range(n_feat)], axis=1)
    slope_one = []
    for half in range(HALVES):
        cols = slice(half * columns, (half + 1) * columns)
        pre_one = dot(own_nodes, w1_all[:, :, :, cols].reshape(n_feat * 2 * pad, columns))
        hid_own[half] = (pre_one * jax.nn.sigmoid(pre_one)).astype(BF16)
        spread_near(f"hid{half}", hid_own.at[half], hid_all.at[half], half == 0)
        slope_one.append(slope(pre_one))
    for half in range(HALVES):
        spread_far(f"hid{half}", hid_all.at[half], half == 0)

    mixed = jnp.zeros((2 * units, nodes), F32)
    hid = []
    for half in range(HALVES):
        spread_end(f"hid{half}", hid_all.at[half], half == 0)
        hid.append(hid_all[half].reshape(nodes, columns))
        mixed += nt_dot(w2[:, half * columns : (half + 1) * columns], hid[half])
    upper, lower = halves(mixed)
    self_term = dot(jnp.concatenate([upper[:units], lower[:units]], axis=0), self_t[...])
    neigh_term = dot(jnp.concatenate([upper[units:], lower[units:]], axis=0), count_t[...])
    pre_two = self_term[:units] + self_term[units:] + (neigh_term[:units] + neigh_term[units:]) / fan_two
    grad_two = (out_grad[...].astype(F32) * slope(pre_two)).astype(BF16)
    node_grad = jnp.concatenate([nt_dot(grad_two, self_t[...]), nt_dot(grad_two, count_t[...]) / fan_two], axis=0)
    upper, lower = halves(node_grad.T)
    turned = jnp.concatenate([upper, lower], axis=1)
    for half in range(HALVES):
        weights = w2[:, half * columns : (half + 1) * columns]
        back = dot(turned, jnp.concatenate([weights, weights], axis=0))
        back_out[half] = back.astype(BF16).reshape(n_y, n_x, own_rows, columns)
        fold_far(f"back{half}", back_out.at[half], back_in[half], half == 1)
    h2[...] = (pre_two * jax.nn.sigmoid(pre_two)).astype(BF16)

    sibling = my_store + 1 - 2 * my_core

    def total_of(ref, total, name):
        tiles = ref.shape[1] // 2
        per = -(-tiles // n_chip)
        summers = tiles // per
        spread = summers * 4 == n_chip * 3

        def sums(chip):
            return lax.rem(chip, 4) != 3 if spread else chip < summers

        def first(chip):
            return (chip - chip // 4 if spread else chip) * per

        part, merged, arrived = ref.at[0], ref.at[1], ref.at[2]

        def fill(half, grad, row0=0):
            across = grad.shape[1] // 128
            for row in range(grad.shape[0] // 16):
                for col in range(across):
                    part[half * tiles + row * across + col] = grad[
                        row * 16 : (row + 1) * 16, col * 128 : (col + 1) * 128
                    ]

        def merge():
            own = pl.ds((1 - my_core) * tiles, tiles)
            send(part.at[own], merged.at[pl.ds(0, tiles)], name + "_merge", recv_of(name + "_merge"), "store", sibling)
            later(part.at[pl.ds(0, tiles)], name + "_merge")

        def reduce():
            await_bytes(merged.at[pl.ds(0, tiles)], recv_of(name + "_merge"))
            both_cores = part[pl.ds(my_core * tiles, tiles)].astype(F32) + merged[0:tiles].astype(F32)
            merged[tiles : 2 * tiles] = both_cores.astype(BF16)

            def to(k):
                chip = chip_peer(k)

                @pl.when(sums(chip))
                def _():
                    send(
                        merged.at[pl.ds(tiles + first(chip), per)],
                        arrived.at[pl.ds(my_chip * per, per)],
                        name + "_reduce",
                        recv_of(name + "_reduce"),
                        "store",
                        chip * 2 + my_core,
                    )

            loop(1, n_chip, to)

            def sent():
                for count, wait_here in ((summers - 1, sums(my_chip)), (summers, jnp.logical_not(sums(my_chip)))):
                    if summers == n_chip and count == n_chip:
                        continue

                    @pl.when(wait_here)
                    def _(count=count):
                        await_bytes(merged.at[pl.ds(0, count * per)], send_sems.at[SENDS.index(name + "_reduce")])

            pending.append(sent)

        def spread_out():
            @pl.when(sums(my_chip))
            def _():
                mine = pl.ds(first(my_chip), per)
                keep(
                    merged.at[pl.ds(tiles + first(my_chip), per)],
                    arrived.at[pl.ds(my_chip * per, per)],
                    recv_of(name + "_reduce"),
                )
                await_bytes(arrived.at[pl.ds(0, n_chip * per)], recv_of(name + "_reduce"))
                summed = arrived[0:per].astype(F32)
                for chip in range(1, n_chip):
                    summed += arrived[chip * per : (chip + 1) * per].astype(F32)
                at = pl.ds(my_core * tiles + first(my_chip), per)
                total[at] = summed.astype(BF16)
                loop(
                    1,
                    n_chip,
                    lambda k: send(
                        total.at[at],
                        total.at[at],
                        name + "_spread",
                        recv_of(name + "_spread"),
                        "store",
                        chip_peer(k) * 2 + my_core,
                    ),
                )

            def sent():
                @pl.when(sums(my_chip))
                def _():
                    await_bytes(arrived.at[pl.ds(0, (n_chip - 1) * per)], send_sems.at[SENDS.index(name + "_spread")])

            pending.append(sent)

        def swap():
            for count, wait_here in ((summers - 1, sums(my_chip)), (summers, jnp.logical_not(sums(my_chip)))):
                if summers == n_chip and count == n_chip:
                    continue

                @pl.when(wait_here)
                def _(count=count):
                    await_bytes(total.at[pl.ds(0, count * per)], recv_of(name + "_spread"))

            mine = total.at[pl.ds(my_core * tiles, tiles)]
            send(mine, mine, name + "_swap", recv_of(name + "_swap"), "store", sibling)
            later(total.at[pl.ds(0, tiles)], name + "_swap")

        def finish():
            await_bytes(total.at[pl.ds(0, tiles)], recv_of(name + "_swap"))

        return fill, merge, reduce, spread_out, swap, finish

    fill, merge, reduce2, spread2, swap2, finish2 = total_of(w2_total, w2_sum, "w2")
    upper, lower = halves(node_grad)
    stacked = jnp.concatenate([upper, lower], axis=0)
    grad_w2 = jnp.concatenate([dot(stacked, part) for part in hid], axis=1)
    grad_w2 = (grad_w2[: 2 * units] + grad_w2[2 * units :]).astype(BF16)
    fill(0, grad_w2[:units])
    fill(1, grad_w2[units:])
    merge()
    reduce2()

    for half in range(HALVES):
        fold_near(f"back{half}", back_in[half], back_mid[half], back_end[half], half == 1)
    for half in range(HALVES):
        total = fold_end(f"back{half}", back_end[half], half == 1)
        slope_own[half] = (total * slope_one[half]).astype(BF16)
        spread_near(f"slope{half}", slope_own.at[half], slope_all.at[half], half == 0)
    for half in range(HALVES):
        spread_far(f"slope{half}", slope_all.at[half], half == 0)
    spread2()

    steps = []
    for half, (ref, total) in enumerate(((w1_total_0, w1_sum_0), (w1_total_1, w1_sum_1))):
        spread_end(f"slope{half}", slope_all.at[half], half == 0)
        grad_w1 = dot(node_inputs, slope_all[half].reshape(nodes, columns)).astype(BF16)
        fill, merge, *rest = total_of(ref, total, f"w1_{half}")
        steps.append(rest)
        fill(0, grad_w1[0:width])
        fill(1, grad_w1[pad : pad + width])
        merge()
        rest[0]()
    swap2()
    steps[0][1]()
    steps[1][1]()
    steps[0][2]()
    steps[1][2]()
    finish2()
    steps[0][3]()
    steps[1][3]()

    for wait in pending:
        wait()


def write_out(*refs):
    from_hbm, outs, held, wide, sems = refs[:4], refs[4:9], refs[9:12], refs[12:16], refs[16]
    to_out = [pltpu.make_async_copy(from_hbm[0], outs[0], sems.at[0])]
    to_out[0].start()
    reads = [pltpu.make_async_copy(src, dst, sems.at[1 + i]) for i, (src, dst) in enumerate(zip(from_hbm[1:], held))]
    for read in reads:
        read.start()
    across = wide[2].shape[1] // 128
    for part, where in enumerate((2, 3, 0, 1)):
        if part == 0:
            reads[0].wait()
        if part == 2:
            reads[1].wait()
            reads[2].wait()
        rows = wide[where].shape[0] // 16
        for row in range(rows):
            for col in range(across):
                if part < 2:
                    tile = held[0][(part * rows + row) * across + col]
                else:
                    each = across // HALVES
                    tile = held[1 + col // each][((part - 2) * rows + row) * each + col % each]
                wide[where][row * 16 : (row + 1) * 16, col * 128 : (col + 1) * 128] = tile.astype(F32)
        to_out.append(pltpu.make_async_copy(wide[where], outs[where + 1], sems.at[4 + where]))
        to_out[-1].start()
    for copy in to_out:
        copy.wait()


def body(n_store, n_feat, *args):
    args = list(args)
    args[3] = jnp.transpose(args[3], (1, 0, 2))
    features, serve_rows, _, index_one, index_two, w1_self, _, w2_self, _, out_grad = args
    width, papers = features.shape
    cap = serve_rows.shape[2]
    entries, _, nodes = index_one.shape
    targets = index_two.shape[2]
    hidden, units = w2_self.shape[1], w2_self.shape[0]
    own_rows = nodes // n_feat
    pad = -(-width // 64) * 64
    columns = hidden // HALVES
    n_x = 1 << (n_feat.bit_length() // 2)
    n_y = n_feat // n_x
    blocks = (HALVES, n_y, n_x, own_rows, columns)
    tiles2 = units // 16 * (hidden // 128)
    tiles1 = width // 16 * (columns // 128)

    def total_scratch(tiles):
        per = -(-tiles // (n_store // 2))
        return pltpu.VMEM((3, max(2 * tiles, n_store // 2 * per), 16, 128), BF16)

    scratch = [
        pltpu.VMEM(features.shape, F32),
        pltpu.VMEM(serve_rows.shape, jnp.int32),
        pltpu.VMEM(args[2].shape, jnp.int32),
        pltpu.VMEM((entries, 1, nodes), jnp.int32),
        pltpu.VMEM((entries, nodes), jnp.int32),
        pltpu.VMEM(index_two.shape, jnp.int32),
        pltpu.VMEM((2 * units, hidden), BF16),
        pltpu.VMEM(out_grad.shape, BF16),
        pltpu.VMEM((papers // LOW * width, LOW), BF16),
        pltpu.VMEM((n_store, width, cap), BF16),
        pltpu.VMEM((n_store, width, cap), BF16),
        pltpu.VMEM((entries, nodes), jnp.int32),
        pltpu.VMEM((entries, cap, nodes), BF16),
        pltpu.VMEM((2 * pad, nodes), F32),
        pltpu.VMEM((n_feat, own_rows, 2 * pad), BF16),
        pltpu.VMEM((n_feat, own_rows, 2 * pad), BF16),
        pltpu.VMEM((2, width, hidden), BF16),
        pltpu.VMEM((n_feat, 2, pad, hidden), BF16),
        pltpu.VMEM((HALVES, own_rows, columns), BF16),
        pltpu.VMEM(blocks, BF16),
        pltpu.VMEM((nodes, targets), BF16),
        pltpu.VMEM((nodes, targets), BF16),
        pltpu.VMEM(blocks, BF16),
        pltpu.VMEM((n_y, n_x, own_rows, columns), BF16),
        pltpu.VMEM((n_x, n_y, own_rows, columns), BF16),
        pltpu.VMEM((n_x, own_rows, columns), BF16),
        pltpu.VMEM((n_y, own_rows, columns), BF16),
        pltpu.VMEM((n_x, own_rows, columns), BF16),
        pltpu.VMEM((n_y, own_rows, columns), BF16),
        pltpu.VMEM((HALVES, own_rows, columns), BF16),
        pltpu.VMEM(blocks, BF16),
        total_scratch(tiles2),
        total_scratch(tiles1),
        total_scratch(tiles1),
        pltpu.SemaphoreType.DMA((INPUTS,)),
        pltpu.SemaphoreType.DMA((len(SENDS),)),
        pltpu.SemaphoreType.DMA((len(SENDS),)),
        pltpu.SemaphoreType.DMA((GROUPS,)),
    ]
    h2, *sums = pl.pallas_call(
        functools.partial(kernel, n_store, n_feat),
        out_shape=[
            jax.ShapeDtypeStruct((units, targets), BF16),
            jax.ShapeDtypeStruct((2 * tiles2, 16, 128), BF16),
            jax.ShapeDtypeStruct((2 * tiles1, 16, 128), BF16),
            jax.ShapeDtypeStruct((2 * tiles1, 16, 128), BF16),
        ],
        in_specs=[pl.BlockSpec(memory_space=pltpu.HBM)] * len(args),
        out_specs=[pl.BlockSpec(memory_space=pltpu.VMEM)] * 4,
        scratch_shapes=scratch,
        compiler_params=pltpu.CompilerParams(
            collective_id=0, has_side_effects=True, vmem_limit_bytes=VMEM_LIMIT
        ),
    )(*args)
    outs = [
        jax.ShapeDtypeStruct((units, targets), BF16),
        jax.ShapeDtypeStruct((width, hidden), F32),
        jax.ShapeDtypeStruct((width, hidden), F32),
        jax.ShapeDtypeStruct((units, hidden), F32),
        jax.ShapeDtypeStruct((units, hidden), F32),
    ]
    return pl.pallas_call(
        write_out,
        out_shape=outs,
        in_specs=[pl.BlockSpec(memory_space=pltpu.HBM)] * 4,
        out_specs=[pl.BlockSpec(memory_space=pltpu.HBM)] * 5,
        scratch_shapes=[pltpu.VMEM(total.shape, BF16) for total in sums]
        + [pltpu.VMEM(out.shape, F32) for out in outs[1:]]
        + [pltpu.SemaphoreType.DMA((8,))],
        compiler_params=pltpu.CompilerParams(vmem_limit_bytes=VMEM_LIMIT),
    )(h2, *sums)


def solution(mesh):
    return jax.shard_map(
        functools.partial(body, mesh.shape["store"], mesh.shape["feat"]),
        mesh=mesh,
        in_specs=(
            P("feat", "store"),
            P("store", None, None),
            P("store", None),
            P("store", None, None),
            P("store", None, None),
            P("feat", None),
            P("feat", None),
            P("feat", None),
            P("feat", None),
            P("feat", "store"),
        ),
        out_specs=(
            P("feat", "store"),
            P("feat", None),
            P("feat", None),
            P("feat", None),
            P("feat", None),
        ),
        check_vma=False,
    )
```

```python
import functools

import jax
import jax.numpy as jnp
from jax import lax
from jax.experimental import pallas as pl
from jax.experimental.pallas import tpu as pltpu
from jax.sharding import PartitionSpec as P

MESH = pl.DeviceIdType.MESH
F32 = jnp.float32
BF16 = jnp.bfloat16
LOW = 256


def slope(values):
    sig = jax.nn.sigmoid(values)
    return sig * (1.0 + values * (1.0 - sig))


def nt_dot(left, right):
    return lax.dot_general(left, right, (((1,), (1,)), ((), ())), preferred_element_type=F32)


def dot(left, right):
    return jnp.dot(left, right, preferred_element_type=F32)


def halves(values):
    upper = values.astype(BF16)
    return upper, (values - upper.astype(F32)).astype(BF16)


def await_bytes(ref, sem):
    pltpu.make_async_copy(ref, ref, sem).wait()


SENDS = (
    ("rows", "w1", "w1_swap", "nodes")
    + ("inputs", "sibling0", "sibling1")
    + tuple(what + quarter + step for what in ("hid", "back", "slope") for quarter in "0123" for step in ("_near", "_far"))
    + tuple(total + step for total in ("w2", "w1_0", "w1_1") for step in ("_merge", "_reduce", "_spread", "_swap"))
)
INPUTS = 10
GROUPS = 8
QUARTERS = 4
STAGES = ((0, 2), (1, 3))
VMEM_LIMIT = 60 * 1024 * 1024


def kernel(
    n_store,
    n_feat,
    features_hbm,
    serve_rows_hbm,
    row_counts_hbm,
    index_one_hbm,
    index_two_hbm,
    w1_self_hbm,
    w1_neigh_hbm,
    w2_self_hbm,
    w2_neigh_hbm,
    out_grad_hbm,
    h2,
    w2_sum,
    w1_sum_0,
    w1_sum_1,
    features,
    serve_rows,
    row_counts,
    index_rows,
    index_one,
    index_two,
    w2,
    out_grad,
    table,
    stage,
    rows_in,
    owner_of,
    pick,
    both,
    node_inputs,
    nodes_out,
    nodes_in,
    w1_own,
    w1_all,
    hid_own,
    hid_all,
    self_t,
    count_t,
    back_out,
    back_in_0,
    back_in_1,
    back_mid_0,
    back_mid_1,
    back_end_0,
    back_end_1,
    slope_own,
    slope_all,
    w2_total,
    w1_total_0,
    w1_total_1,
    input_sems,
    send_sems,
    recv_sems,
    group_sems,
):
    my_store, my_feat = lax.axis_index("store"), lax.axis_index("feat")
    my_chip, my_core = my_store // 2, lax.rem(my_store, 2)
    n_chip = n_store // 2
    n_x = 1 << (n_feat.bit_length() // 2)
    n_y = n_feat // n_x
    my_y, my_x = my_feat // n_x, lax.rem(my_feat, n_x)
    width, papers = features.shape
    cap = serve_rows.shape[2]
    entries, nodes = index_one.shape
    fan_one = entries - 1
    fan_two = index_two.shape[1] - 1
    units, hidden = w2.shape[0] // 2, w2.shape[1]
    columns = hidden // QUARTERS
    own_rows = nodes // n_feat
    pad = both.shape[0] // 2
    pending = []
    back_in = (back_in_0.at[0], back_in_0.at[1], back_in_1.at[0], back_in_1.at[1])
    back_mid = (back_mid_0.at[0], back_mid_0.at[1], back_mid_1.at[0], back_mid_1.at[1])
    back_end = (back_end_0.at[0], back_end_0.at[1], back_end_1.at[0], back_end_1.at[1])
    sibling = my_store + 1 - 2 * my_core

    def store_peer(step):
        return lax.rem(my_store + step + n_store, n_store)

    def feat_peer(step):
        return lax.rem(my_feat + step + n_feat, n_feat)

    def chip_peer(step):
        return lax.rem(my_chip + step + n_chip, n_chip)

    def send(src, dst, name, recv_sem, axis, peer):
        pltpu.make_async_remote_copy(
            src_ref=src,
            dst_ref=dst,
            send_sem=send_sems.at[SENDS.index(name)],
            recv_sem=recv_sem,
            device_id={axis: peer},
            device_id_type=MESH,
        ).start()

    def recv_of(name):
        return recv_sems.at[SENDS.index(name)]

    def later(ref, name):
        pending.append(lambda: await_bytes(ref, send_sems.at[SENDS.index(name)]))

    def keep(src, dst, sem):
        pltpu.make_async_copy(src, dst, sem).start()

    def loop(low, high, fn):
        def step(k, carry):
            fn(k)
            return carry

        lax.fori_loop(low, high, step, 0)

    def share(src_of, dst, name):
        loop(1, n_feat, lambda k: send(src_of(feat_peer(k)), dst, name, recv_of(name), "feat", feat_peer(k)))
        keep(src_of(my_feat), dst, recv_of(name))

    def along(x, k):
        return my_y * n_x + lax.rem(my_x + k, n_x) if x else lax.rem(my_y + k, n_y) * n_x + my_x

    def count_of(x):
        return n_x if x else n_y

    def spread_near(name, own, dst, x):
        step, spot = name + "_near", dst.at[my_y, my_x]
        loop(1, count_of(x), lambda k: send(own, spot, step, recv_of(step), "feat", along(x, k)))
        keep(own, spot, recv_of(step))
        if count_of(x) > 1:
            later(dst.at[0, pl.ds(0, n_x - 1)] if x else dst.at[pl.ds(0, n_y - 1), 0], step)

    def spread_far(name, dst, x):
        step, line = name + "_far", dst.at[my_y] if x else dst.at[:, my_x]
        await_bytes(line, recv_of(name + "_near"))
        loop(1, count_of(not x), lambda k: send(line, line, step, recv_of(step), "feat", along(not x, k)))
        if count_of(not x) > 1:
            later(dst.at[pl.ds(0, n_y - 1)] if x else dst.at[:, pl.ds(0, n_x - 1)], step)

    def spread_end(name, dst, x):
        if count_of(not x) > 1:
            await_bytes(dst.at[pl.ds(0, n_y - 1)] if x else dst.at[:, pl.ds(0, n_x - 1)], recv_of(name + "_far"))

    def fold_far(name, src, dst, x):
        step, mine = name + "_far", my_x if x else my_y

        def lines(k):
            return src.at[:, lax.rem(my_x + k, n_x)] if x else src.at[lax.rem(my_y + k, n_y)]

        loop(1, count_of(x), lambda k: send(lines(k), dst.at[mine], step, recv_of(step), "feat", along(x, k)))
        keep(lines(0), dst.at[mine], recv_of(step))
        if count_of(x) > 1:
            later(dst.at[pl.ds(0, count_of(x) - 1)], step)

    def fold_near(name, src, middle, dst, x):
        await_bytes(src, recv_of(name + "_far"))
        total = src[0].astype(F32)
        for line in range(1, count_of(x)):
            total += src[line].astype(F32)
        middle[...] = total.astype(BF16)
        step, mine = name + "_near", my_y if x else my_x

        def block(k):
            return middle.at[lax.rem(my_y + k, n_y) if x else lax.rem(my_x + k, n_x)]

        loop(1, count_of(not x), lambda k: send(block(k), dst.at[mine], step, recv_of(step), "feat", along(not x, k)))
        keep(block(0), dst.at[mine], recv_of(step))
        if count_of(not x) > 1:
            later(dst.at[pl.ds(0, count_of(not x) - 1)], step)

    def fold_end(name, src, x):
        await_bytes(src, recv_of(name + "_near"))
        total = src[0].astype(F32)
        for line in range(1, count_of(not x)):
            total += src[line].astype(F32)
        return total

    barrier = pltpu.get_barrier_semaphore()

    def greet(axis, peer):
        pl.semaphore_signal(barrier, inc=1, device_id={axis: peer}, device_id_type=MESH)

    reads = (
        (features_hbm, features),
        (serve_rows_hbm, serve_rows),
        (w1_self_hbm, w1_own.at[0]),
        (w1_neigh_hbm, w1_own.at[1]),
        (row_counts_hbm, row_counts),
        (index_one_hbm, index_rows),
        (index_two_hbm, index_two),
        (w2_self_hbm, w2.at[pl.ds(0, units)]),
        (w2_neigh_hbm, w2.at[pl.ds(units, units)]),
        (out_grad_hbm, out_grad),
    )
    reads = [pltpu.make_async_copy(src, dst, input_sems.at[i]) for i, (src, dst) in enumerate(reads)]
    for read in reads:
        read.start()
    loop(1, n_store, lambda k: greet("store", store_peer(k)))
    loop(1, n_feat, lambda k: greet("feat", feat_peer(k)))
    for group in range(n_feat):
        for half in range(2):
            w1_all[group, half, width:, :] = jnp.zeros((pad - width, hidden), BF16)
    both[...] = jnp.zeros_like(both)

    reads[0].wait()
    reads[1].wait()
    highs = papers // LOW
    for high in range(highs):
        table[high * width : (high + 1) * width, :] = features[:, high * LOW : (high + 1) * LOW].astype(BF16)
    low_ids = lax.broadcasted_iota(jnp.int32, (LOW, cap), 0)

    def serve(trainer):
        wanted = serve_rows[0, pl.ds(trainer, 1), :]
        low, high_of = wanted & (LOW - 1), wanted // LOW
        one_hot = jnp.where(low_ids == low, 1.0, 0.0).astype(BF16)
        found = dot(table[...], one_hot)
        total = found[0:width, :]
        for high in range(1, highs):
            total = jnp.where(high_of == high, found[high * width : (high + 1) * width, :], total)
        stage[trainer] = total.astype(BF16)

    loop(0, n_store, serve)
    for read in reads[2:]:
        read.wait()
    pl.semaphore_wait(barrier, n_store + n_feat - 2)

    half_store = n_store // 2
    group_size = n_store // GROUPS

    def send_rows(trainer, rank):
        send(stage.at[trainer], rows_in.at[rank], "rows", group_sems.at[rank // group_size], "store", trainer)

    def send_w1(peer):
        send(w1_own.at[my_core], w1_all.at[my_feat, my_core, pl.ds(0, width)], "w1", recv_of("w1"), "feat", peer)

    def send_pair(i):
        send_rows(store_peer(half_store - i), 2 * i - 1)
        send_rows(store_peer(i - half_store), 2 * i)

    def send_pair_and_w1(i):
        send_pair(i)
        send_w1(feat_peer(i))

    send_rows(store_peer(half_store), 0)
    shared = min(half_store, n_feat)
    loop(1, shared, send_pair_and_w1)
    loop(shared, half_store, send_pair)
    loop(shared, n_feat, lambda i: send_w1(feat_peer(i)))
    keep(stage.at[my_store], rows_in.at[n_store - 1], group_sems.at[GROUPS - 1])
    keep(w1_own.at[my_core], w1_all.at[my_feat, my_core, pl.ds(0, width)], recv_of("w1"))
    later(stage.at[pl.ds(0, n_store - 1)], "rows")
    later(w1_all.at[pl.ds(0, n_feat - 1), 0, pl.ds(0, width)], "w1")

    for entry in range(entries):
        index_one[entry : entry + 1, :] = index_rows[entry]
    raw = index_one[...]
    owners = raw // cap
    place = (raw & (cap - 1)).astype(F32)
    counts = jnp.ones(raw.shape, F32)
    for owner in range(n_store):
        counts = jnp.where(owners == owner, row_counts[0:1, owner : owner + 1].astype(F32), counts)
    place = place - jnp.floor((place + 0.5) / counts) * counts
    owner_of[0:entries, :] = owners
    place = place.astype(jnp.int32)
    slot_ids = lax.broadcasted_iota(jnp.int32, (cap, nodes), 0)
    for entry in range(entries):
        pick[entry] = jnp.where(slot_ids == place[entry : entry + 1, :], 1.0, 0.0).astype(BF16)

    strip = 64
    targets = index_two.shape[2]

    def second_tables(part):
        node_ids = lax.broadcasted_iota(jnp.int32, (strip, targets), 0) + part * strip
        at = pl.ds(pl.multiple_of(part * strip, strip), strip)
        self_t[at, :] = jnp.where(node_ids == index_two[0, 0:1, :], 1.0, 0.0).astype(BF16)
        total = jnp.zeros((strip, targets), F32)
        for entry in range(1, fan_two + 1):
            total += jnp.where(node_ids == index_two[0, entry : entry + 1, :], 1.0, 0.0)
        count_t[at, :] = total.astype(BF16)

    loop(0, nodes // strip, second_tables)

    def gather(group):
        await_bytes(rows_in.at[pl.ds(group * group_size, group_size)], group_sems.at[group])
        arrived = rows_in[pl.ds(group * group_size, group_size)].reshape(group_size * width, cap)
        owners = []
        for member in range(group_size):
            rank = group * group_size + member
            offset = half_store - (rank + 1) // 2 if member % 2 else rank // 2 - half_store
            owners.append(store_peer(-offset))
        sums = [both[0:width, :], both[pad : pad + width, :]]
        for entry in range(entries):
            found = dot(arrived, pick[entry])
            of = owner_of[entry : entry + 1, :]
            mine = jnp.zeros((width, nodes), F32)
            for member in range(group_size):
                mine = jnp.where(of == owners[member], found[member * width : (member + 1) * width, :], mine)
            sums[min(entry, 1)] += mine
        both[0:width, :], both[pad : pad + width, :] = sums

    loop(0, GROUPS - 2, gather)
    await_bytes(w1_all.at[:, 0, pl.ds(0, width)], recv_of("w1"))
    mine = w1_all.at[:, my_core, pl.ds(0, width)]
    send(mine, mine, "w1_swap", recv_of("w1_swap"), "store", my_store + 1 - 2 * my_core)
    later(w1_all.at[:, 0, pl.ds(0, width)], "w1_swap")
    loop(GROUPS - 2, GROUPS, gather)
    both[pad : pad + width, :] = both[pad : pad + width, :] / fan_one
    node_inputs[my_core] = both[...].astype(BF16)
    send(node_inputs.at[my_core], node_inputs.at[my_core], "inputs", recv_of("inputs"), "store", sibling)
    later(node_inputs.at[0], "inputs")
    turned = both[...].T.astype(BF16)
    for group in range(n_feat):
        nodes_out[group] = turned[group * own_rows : (group + 1) * own_rows, :]

    share(lambda peer: nodes_out.at[peer], nodes_in.at[my_feat], "nodes")
    later(nodes_out.at[pl.ds(0, n_feat - 1)], "nodes")

    await_bytes(w1_all.at[:, 0, pl.ds(0, width)], recv_of("w1_swap"))
    await_bytes(nodes_in, recv_of("nodes"))
    own_nodes = jnp.concatenate([nodes_in[group] for group in range(n_feat)], axis=1)
    slope_one = [None] * QUARTERS
    for stage_now in STAGES:
        for q in stage_now:
            cols = slice(q * columns, (q + 1) * columns)
            pre_one = dot(own_nodes, w1_all[:, :, :, cols].reshape(n_feat * 2 * pad, columns))
            hid_own[q] = (pre_one * jax.nn.sigmoid(pre_one)).astype(BF16)
            spread_near(f"hid{q}", hid_own.at[q], hid_all.at[q], q < 2)
            slope_one[q] = slope(pre_one)
    for stage_now in STAGES:
        for q in stage_now:
            spread_far(f"hid{q}", hid_all.at[q], q < 2)

    mixed = jnp.zeros((2 * units, nodes), F32)
    hid = [None] * QUARTERS
    for stage_now in STAGES:
        for q in stage_now:
            spread_end(f"hid{q}", hid_all.at[q], q < 2)
            hid[q] = hid_all[q].reshape(nodes, columns)
            mixed += nt_dot(w2[:, q * columns : (q + 1) * columns], hid[q])
    upper, lower = halves(mixed)
    self_term = dot(jnp.concatenate([upper[:units], lower[:units]], axis=0), self_t[...])
    neigh_term = dot(jnp.concatenate([upper[units:], lower[units:]], axis=0), count_t[...])
    pre_two = self_term[:units] + self_term[units:] + (neigh_term[:units] + neigh_term[units:]) / fan_two
    grad_two = (out_grad[...].astype(F32) * slope(pre_two)).astype(BF16)
    node_grad = jnp.concatenate([nt_dot(grad_two, self_t[...]), nt_dot(grad_two, count_t[...]) / fan_two], axis=0)
    upper, lower = halves(node_grad.T)
    turned = jnp.concatenate([upper, lower], axis=1)
    for stage_now in STAGES:
        for q in stage_now:
            weights = w2[:, q * columns : (q + 1) * columns]
            back = dot(turned, jnp.concatenate([weights, weights], axis=0))
            back_out[q] = back.astype(BF16).reshape(n_y, n_x, own_rows, columns)
            fold_far(f"back{q}", back_out.at[q], back_in[q], q >= 2)
    h2[...] = (pre_two * jax.nn.sigmoid(pre_two)).astype(BF16)

    def total_of(ref, total, name, merged_already=False):
        tiles = ref.shape[1] // 2
        per = -(-tiles // n_chip)
        summers = tiles // per
        spread = summers * 4 == n_chip * 3

        def sums(chip):
            return lax.rem(chip, 4) != 3 if spread else chip < summers

        def first(chip):
            return (chip - chip // 4 if spread else chip) * per

        part, merged, arrived = ref.at[0], ref.at[1], ref.at[2]

        def fill(half, grad, row0=0):
            across = grad.shape[1] // 128
            for row in range(grad.shape[0] // 16):
                for col in range(across):
                    tile = grad[row * 16 : (row + 1) * 16, col * 128 : (col + 1) * 128]
                    if merged_already:
                        merged[tiles + row * across + col] = tile
                    else:
                        part[half * tiles + row * across + col] = tile

        def merge():
            own = pl.ds((1 - my_core) * tiles, tiles)
            send(part.at[own], merged.at[pl.ds(0, tiles)], name + "_merge", recv_of(name + "_merge"), "store", sibling)
            later(part.at[pl.ds(0, tiles)], name + "_merge")

        def reduce():
            if not merged_already:
                await_bytes(merged.at[pl.ds(0, tiles)], recv_of(name + "_merge"))
                both_cores = part[pl.ds(my_core * tiles, tiles)].astype(F32) + merged[0:tiles].astype(F32)
                merged[tiles : 2 * tiles] = both_cores.astype(BF16)

            def to(k):
                chip = chip_peer(k)

                @pl.when(sums(chip))
                def _():
                    send(
                        merged.at[pl.ds(tiles + first(chip), per)],
                        arrived.at[pl.ds(my_chip * per, per)],
                        name + "_reduce",
                        recv_of(name + "_reduce"),
                        "store",
                        chip * 2 + my_core,
                    )

            loop(1, n_chip, to)

            def sent():
                for count, wait_here in ((summers - 1, sums(my_chip)), (summers, jnp.logical_not(sums(my_chip)))):
                    if summers == n_chip and count == n_chip:
                        continue

                    @pl.when(wait_here)
                    def _(count=count):
                        await_bytes(merged.at[pl.ds(0, count * per)], send_sems.at[SENDS.index(name + "_reduce")])

            pending.append(sent)

        def spread_out():
            @pl.when(sums(my_chip))
            def _():
                mine = pl.ds(first(my_chip), per)
                keep(
                    merged.at[pl.ds(tiles + first(my_chip), per)],
                    arrived.at[pl.ds(my_chip * per, per)],
                    recv_of(name + "_reduce"),
                )
                await_bytes(arrived.at[pl.ds(0, n_chip * per)], recv_of(name + "_reduce"))
                summed = arrived[0:per].astype(F32)
                for chip in range(1, n_chip):
                    summed += arrived[chip * per : (chip + 1) * per].astype(F32)
                at = pl.ds(my_core * tiles + first(my_chip), per)
                total[at] = summed.astype(BF16)
                loop(
                    1,
                    n_chip,
                    lambda k: send(
                        total.at[at],
                        total.at[at],
                        name + "_spread",
                        recv_of(name + "_spread"),
                        "store",
                        chip_peer(k) * 2 + my_core,
                    ),
                )

            def sent():
                @pl.when(sums(my_chip))
                def _():
                    await_bytes(arrived.at[pl.ds(0, (n_chip - 1) * per)], send_sems.at[SENDS.index(name + "_spread")])

            pending.append(sent)

        def swap():
            for count, wait_here in ((summers - 1, sums(my_chip)), (summers, jnp.logical_not(sums(my_chip)))):
                if summers == n_chip and count == n_chip:
                    continue

                @pl.when(wait_here)
                def _(count=count):
                    await_bytes(total.at[pl.ds(0, count * per)], recv_of(name + "_spread"))

            mine = total.at[pl.ds(my_core * tiles, tiles)]
            send(mine, mine, name + "_swap", recv_of(name + "_swap"), "store", sibling)
            later(total.at[pl.ds(0, tiles)], name + "_swap")

        def finish():
            await_bytes(total.at[pl.ds(0, tiles)], recv_of(name + "_swap"))

        return fill, merge, reduce, spread_out, swap, finish

    fill, merge, reduce2, spread2, swap2, finish2 = total_of(w2_total, w2_sum, "w2")
    upper, lower = halves(node_grad)
    stacked = jnp.concatenate([upper, lower], axis=0)
    grad_w2 = jnp.concatenate([dot(stacked, part) for part in hid], axis=1)
    grad_w2 = (grad_w2[: 2 * units] + grad_w2[2 * units :]).astype(BF16)
    fill(0, grad_w2[:units])
    fill(1, grad_w2[units:])
    merge()
    reduce2()

    def slope_near(stage_no):
        for core, q in enumerate(STAGES[stage_no]):
            x, step, spot = core == 0, f"slope{q}_near", slope_all.at[stage_no, my_core, my_y, my_x]
            arrival = recv_of(f"slope{stage_no}_near")
            total = fold_end(f"back{q}", back_end[q], q >= 2)
            slope_own[q] = (total * slope_one[q]).astype(BF16)

            def to_line(k, x=x, step=step, spot=spot, arrival=arrival, core=core, q=q):
                chip = along(x, k)
                pltpu.make_async_remote_copy(
                    src_ref=slope_own.at[q],
                    dst_ref=spot,
                    send_sem=send_sems.at[SENDS.index(step)],
                    recv_sem=arrival,
                    device_id={"store": my_chip * 2 + core, "feat": chip},
                    device_id_type=MESH,
                ).start()

            loop(1, count_of(x), to_line)
            if count_of(x) > 1:
                later(slope_all.at[0, 0, 0, pl.ds(0, n_x - 1)] if x else slope_all.at[0, 0, pl.ds(0, n_y - 1), 0], step)

            if core == 0:
                later(slope_own.at[0], f"sibling{stage_no}")

            @pl.when(my_core == core)
            def _(arrival=arrival, q=q, spot=spot):
                keep(slope_own.at[q], spot, arrival)

            @pl.when(my_core != core)
            def _(arrival=arrival, q=q, spot=spot):
                send(slope_own.at[q], spot, f"sibling{stage_no}", arrival, "store", sibling)

    def slope_line(stage_no, x):
        return slope_all.at[stage_no, :, my_y] if x else slope_all.at[stage_no, :, :, my_x]

    def slope_rest(stage_no, x):
        return slope_all.at[stage_no, :, pl.ds(0, n_y - 1)] if x else slope_all.at[stage_no, :, :, pl.ds(0, n_x - 1)]

    def on_core(core, fn):
        pl.when(my_core == core)(fn)

    def slope_far(stage_no):
        step = f"slope{stage_no}_far"
        for core in range(2):
            x = core == 0

            def forward(x=x):
                line = slope_line(stage_no, x)
                await_bytes(line, recv_of(f"slope{stage_no}_near"))
                loop(1, count_of(not x), lambda k: send(line, line, step, recv_of(step), "feat", along(not x, k)))

            on_core(core, forward)

    def slope_end(stage_no, sems):
        for core in range(2):
            x = core == 0
            if count_of(not x) > 1:
                on_core(
                    core,
                    lambda x=x: await_bytes(slope_rest(stage_no, x), sems.at[SENDS.index(f"slope{stage_no}_far")]),
                )

    def first_weights(stage_no, fill):
        slope_end(stage_no, recv_sems)
        grad = jnp.zeros((2 * pad, columns), F32)
        for core in range(2):
            grad += dot(node_inputs[core], slope_all[stage_no, core].reshape(nodes, columns))
        grad = grad.astype(BF16)
        fill(0, jnp.concatenate([grad[0:width], grad[pad : pad + width]], axis=0))

    def fold_middle(stage_no):
        for q in STAGES[stage_no]:
            fold_near(f"back{q}", back_in[q], back_mid[q], back_end[q], q >= 2)

    fill_a, _, reduce_a, spread_a, swap_a, finish_a = total_of(w1_total_0, w1_sum_0, "w1_0", merged_already=True)
    fill_b, _, reduce_b, spread_b, swap_b, finish_b = total_of(w1_total_1, w1_sum_1, "w1_1", merged_already=True)
    fold_middle(0)
    fold_middle(1)
    slope_near(0)
    slope_near(1)
    slope_far(0)
    slope_far(1)
    spread2()
    await_bytes(node_inputs.at[0], recv_of("inputs"))
    first_weights(0, fill_a)
    reduce_a()
    first_weights(1, fill_b)
    reduce_b()
    swap2()
    spread_a()
    spread_b()
    swap_a()
    swap_b()
    finish2()
    finish_a()
    finish_b()
    pending.append(lambda: slope_end(0, send_sems))
    pending.append(lambda: slope_end(1, send_sems))

    for wait in pending:
        wait()


def write_out(*refs):
    from_hbm, outs, held, wide, sems = refs[:4], refs[4:9], refs[9:12], refs[12:16], refs[16]
    to_out = [pltpu.make_async_copy(from_hbm[0], outs[0], sems.at[0])]
    to_out[0].start()
    reads = [pltpu.make_async_copy(src, dst, sems.at[1 + i]) for i, (src, dst) in enumerate(zip(from_hbm[1:], held))]
    for read in reads:
        read.start()
    across = wide[2].shape[1] // 128
    for part, where in enumerate((2, 3, 0, 1)):
        if part == 0:
            reads[0].wait()
        if part == 2:
            reads[1].wait()
            reads[2].wait()
        rows = wide[where].shape[0] // 16
        for row in range(rows):
            for col in range(across):
                if part < 2:
                    tile = held[0][(part * rows + row) * across + col]
                else:
                    each = across // QUARTERS
                    quarter = col // each
                    at = quarter // 2 * (2 * rows) + (part - 2) * rows + row
                    tile = held[1 + quarter % 2][at * each + col % each]
                wide[where][row * 16 : (row + 1) * 16, col * 128 : (col + 1) * 128] = tile.astype(F32)
        to_out.append(pltpu.make_async_copy(wide[where], outs[where + 1], sems.at[4 + where]))
        to_out[-1].start()
    for copy in to_out:
        copy.wait()


def body(n_store, n_feat, *args):
    args = list(args)
    args[3] = jnp.transpose(args[3], (1, 0, 2))
    features, serve_rows, _, index_one, index_two, w1_self, _, w2_self, _, out_grad = args
    width, papers = features.shape
    cap = serve_rows.shape[2]
    entries, _, nodes = index_one.shape
    targets = index_two.shape[2]
    hidden, units = w2_self.shape[1], w2_self.shape[0]
    own_rows = nodes // n_feat
    pad = -(-width // 64) * 64
    columns = hidden // QUARTERS
    n_x = 1 << (n_feat.bit_length() // 2)
    n_y = n_feat // n_x
    blocks = (QUARTERS, n_y, n_x, own_rows, columns)
    tiles2 = units // 16 * (hidden // 128)
    tiles1 = 2 * width // 16 * (columns // 128)

    def total_scratch(tiles):
        per = -(-tiles // (n_store // 2))
        return pltpu.VMEM((3, max(2 * tiles, n_store // 2 * per), 16, 128), BF16)

    scratch = [
        pltpu.VMEM(features.shape, F32),
        pltpu.VMEM(serve_rows.shape, jnp.int32),
        pltpu.VMEM(args[2].shape, jnp.int32),
        pltpu.VMEM((entries, 1, nodes), jnp.int32),
        pltpu.VMEM((entries, nodes), jnp.int32),
        pltpu.VMEM(index_two.shape, jnp.int32),
        pltpu.VMEM((2 * units, hidden), BF16),
        pltpu.VMEM(out_grad.shape, BF16),
        pltpu.VMEM((papers // LOW * width, LOW), BF16),
        pltpu.VMEM((n_store, width, cap), BF16),
        pltpu.VMEM((n_store, width, cap), BF16),
        pltpu.VMEM((entries, nodes), jnp.int32),
        pltpu.VMEM((entries, cap, nodes), BF16),
        pltpu.VMEM((2 * pad, nodes), F32),
        pltpu.VMEM((2, 2 * pad, nodes), BF16),
        pltpu.VMEM((n_feat, own_rows, 2 * pad), BF16),
        pltpu.VMEM((n_feat, own_rows, 2 * pad), BF16),
        pltpu.VMEM((2, width, hidden), BF16),
        pltpu.VMEM((n_feat, 2, pad, hidden), BF16),
        pltpu.VMEM((QUARTERS, own_rows, columns), BF16),
        pltpu.VMEM(blocks, BF16),
        pltpu.VMEM((nodes, targets), BF16),
        pltpu.VMEM((nodes, targets), BF16),
        pltpu.VMEM(blocks, BF16),
        pltpu.VMEM((2, n_y, n_x, own_rows, columns), BF16),
        pltpu.VMEM((2, n_x, n_y, own_rows, columns), BF16),
        pltpu.VMEM((2, n_x, own_rows, columns), BF16),
        pltpu.VMEM((2, n_y, own_rows, columns), BF16),
        pltpu.VMEM((2, n_x, own_rows, columns), BF16),
        pltpu.VMEM((2, n_y, own_rows, columns), BF16),
        pltpu.VMEM((QUARTERS, own_rows, columns), BF16),
        pltpu.VMEM((2, 2, n_y, n_x, own_rows, columns), BF16),
        total_scratch(tiles2),
        total_scratch(tiles1),
        total_scratch(tiles1),
        pltpu.SemaphoreType.DMA((INPUTS,)),
        pltpu.SemaphoreType.DMA((len(SENDS),)),
        pltpu.SemaphoreType.DMA((len(SENDS),)),
        pltpu.SemaphoreType.DMA((GROUPS,)),
    ]
    h2, *sums = pl.pallas_call(
        functools.partial(kernel, n_store, n_feat),
        out_shape=[
            jax.ShapeDtypeStruct((units, targets), BF16),
            jax.ShapeDtypeStruct((2 * tiles2, 16, 128), BF16),
            jax.ShapeDtypeStruct((2 * tiles1, 16, 128), BF16),
            jax.ShapeDtypeStruct((2 * tiles1, 16, 128), BF16),
        ],
        in_specs=[pl.BlockSpec(memory_space=pltpu.HBM)] * len(args),
        out_specs=[pl.BlockSpec(memory_space=pltpu.VMEM)] * 4,
        scratch_shapes=scratch,
        compiler_params=pltpu.CompilerParams(
            collective_id=0, has_side_effects=True, vmem_limit_bytes=VMEM_LIMIT
        ),
    )(*args)
    outs = [
        jax.ShapeDtypeStruct((units, targets), BF16),
        jax.ShapeDtypeStruct((width, hidden), F32),
        jax.ShapeDtypeStruct((width, hidden), F32),
        jax.ShapeDtypeStruct((units, hidden), F32),
        jax.ShapeDtypeStruct((units, hidden), F32),
    ]
    return pl.pallas_call(
        write_out,
        out_shape=outs,
        in_specs=[pl.BlockSpec(memory_space=pltpu.HBM)] * 4,
        out_specs=[pl.BlockSpec(memory_space=pltpu.HBM)] * 5,
        scratch_shapes=[pltpu.VMEM(total.shape, BF16) for total in sums]
        + [pltpu.VMEM(out.shape, F32) for out in outs[1:]]
        + [pltpu.SemaphoreType.DMA((8,))],
        compiler_params=pltpu.CompilerParams(vmem_limit_bytes=VMEM_LIMIT),
    )(h2, *sums)


def solution(mesh):
    return jax.shard_map(
        functools.partial(body, mesh.shape["store"], mesh.shape["feat"]),
        mesh=mesh,
        in_specs=(
            P("feat", "store"),
            P("store", None, None),
            P("store", None),
            P("store", None, None),
            P("store", None, None),
            P("feat", None),
            P("feat", None),
            P("feat", None),
            P("feat", None),
            P("feat", "store"),
        ),
        out_specs=(
            P("feat", "store"),
            P("feat", None),
            P("feat", None),
            P("feat", None),
            P("feat", None),
        ),
        check_vma=False,
    )
```

```python
import functools

import jax
import jax.numpy as jnp
from jax import lax
from jax.experimental import pallas as pl
from jax.experimental.pallas import tpu as pltpu
from jax.sharding import PartitionSpec as P

MESH = pl.DeviceIdType.MESH
F32 = jnp.float32
BF16 = jnp.bfloat16
LOW = 256


def slope(values):
    sig = jax.nn.sigmoid(values)
    return sig * (1.0 + values * (1.0 - sig))


def nt_dot(left, right):
    return lax.dot_general(left, right, (((1,), (1,)), ((), ())), preferred_element_type=F32)


def dot(left, right):
    return jnp.dot(left, right, preferred_element_type=F32)


def halves(values):
    upper = values.astype(BF16)
    return upper, (values - upper.astype(F32)).astype(BF16)


def await_bytes(ref, sem):
    pltpu.make_async_copy(ref, ref, sem).wait()


SENDS = (
    ("rows", "w1", "w1_swap", "nodes")
    + ("inputs", "sibling0", "sibling1")
    + tuple(what + quarter + step for what in ("hid", "back", "slope") for quarter in "0123" for step in ("_near", "_far"))
    + tuple(total + step for total in ("w2", "w1_0", "w1_1") for step in ("_merge", "_reduce", "_spread", "_swap"))
)
INPUTS = 10
GROUPS = 8
QUARTERS = 4
STAGES = ((0, 2), (1, 3))
VMEM_LIMIT = 60 * 1024 * 1024


def kernel(
    n_store,
    n_feat,
    features_hbm,
    serve_rows_hbm,
    row_counts_hbm,
    index_one_hbm,
    index_two_hbm,
    w1_self_hbm,
    w1_neigh_hbm,
    w2_self_hbm,
    w2_neigh_hbm,
    out_grad_hbm,
    h2_hbm,
    w1_self_out,
    w1_neigh_out,
    w2_self_out,
    w2_neigh_out,
    features,
    serve_rows,
    row_counts,
    index_rows,
    index_one,
    index_two,
    w2,
    out_grad,
    table,
    stage,
    rows_in,
    owner_of,
    pick,
    both,
    node_inputs,
    nodes_out,
    nodes_in,
    w1_own,
    w1_all,
    hid_own,
    hid_all,
    self_t,
    count_t,
    back_out,
    back_in_0,
    back_in_1,
    back_mid_0,
    back_mid_1,
    back_end_0,
    back_end_1,
    slope_own,
    slope_all,
    w2_total,
    w1_total_0,
    w1_total_1,
    w2_sum,
    w1_sum_0,
    w1_sum_1,
    h2,
    w1_wide,
    w2_wide,
    input_sems,
    output_sems,
    send_sems,
    recv_sems,
    group_sems,
):
    my_store, my_feat = lax.axis_index("store"), lax.axis_index("feat")
    my_chip, my_core = my_store // 2, lax.rem(my_store, 2)
    n_chip = n_store // 2
    n_x = 1 << (n_feat.bit_length() // 2)
    n_y = n_feat // n_x
    my_y, my_x = my_feat // n_x, lax.rem(my_feat, n_x)
    width, papers = features.shape
    cap = serve_rows.shape[2]
    entries, nodes = index_one.shape
    fan_one = entries - 1
    fan_two = index_two.shape[1] - 1
    units, hidden = w2.shape[0] // 2, w2.shape[1]
    columns = hidden // QUARTERS
    own_rows = nodes // n_feat
    pad = both.shape[0] // 2
    pending = []
    back_in = (back_in_0.at[0], back_in_0.at[1], back_in_1.at[0], back_in_1.at[1])
    back_mid = (back_mid_0.at[0], back_mid_0.at[1], back_mid_1.at[0], back_mid_1.at[1])
    back_end = (back_end_0.at[0], back_end_0.at[1], back_end_1.at[0], back_end_1.at[1])
    sibling = my_store + 1 - 2 * my_core

    def store_peer(step):
        return lax.rem(my_store + step + n_store, n_store)

    def feat_peer(step):
        return lax.rem(my_feat + step + n_feat, n_feat)

    def chip_peer(step):
        return lax.rem(my_chip + step + n_chip, n_chip)

    def send(src, dst, name, recv_sem, axis, peer):
        pltpu.make_async_remote_copy(
            src_ref=src,
            dst_ref=dst,
            send_sem=send_sems.at[SENDS.index(name)],
            recv_sem=recv_sem,
            device_id={axis: peer},
            device_id_type=MESH,
        ).start()

    def recv_of(name):
        return recv_sems.at[SENDS.index(name)]

    def later(ref, name):
        pending.append(lambda: await_bytes(ref, send_sems.at[SENDS.index(name)]))

    def keep(src, dst, sem):
        pltpu.make_async_copy(src, dst, sem).start()

    def write(src, dst, i):
        copy = pltpu.make_async_copy(src, dst, output_sems.at[i])
        copy.start()
        pending.append(copy.wait)

    def loop(low, high, fn):
        def step(k, carry):
            fn(k)
            return carry

        lax.fori_loop(low, high, step, 0)

    def share(src_of, dst, name):
        loop(1, n_feat, lambda k: send(src_of(feat_peer(k)), dst, name, recv_of(name), "feat", feat_peer(k)))
        keep(src_of(my_feat), dst, recv_of(name))

    def along(x, k):
        return my_y * n_x + lax.rem(my_x + k, n_x) if x else lax.rem(my_y + k, n_y) * n_x + my_x

    def count_of(x):
        return n_x if x else n_y

    def spread_near(name, own, dst, x):
        step, spot = name + "_near", dst.at[my_y, my_x]
        loop(1, count_of(x), lambda k: send(own, spot, step, recv_of(step), "feat", along(x, k)))
        keep(own, spot, recv_of(step))
        if count_of(x) > 1:
            later(dst.at[0, pl.ds(0, n_x - 1)] if x else dst.at[pl.ds(0, n_y - 1), 0], step)

    def spread_far(name, dst, x):
        step, line = name + "_far", dst.at[my_y] if x else dst.at[:, my_x]
        await_bytes(line, recv_of(name + "_near"))
        loop(1, count_of(not x), lambda k: send(line, line, step, recv_of(step), "feat", along(not x, k)))
        if count_of(not x) > 1:
            later(dst.at[pl.ds(0, n_y - 1)] if x else dst.at[:, pl.ds(0, n_x - 1)], step)

    def spread_end(name, dst, x):
        if count_of(not x) > 1:
            await_bytes(dst.at[pl.ds(0, n_y - 1)] if x else dst.at[:, pl.ds(0, n_x - 1)], recv_of(name + "_far"))

    def fold_far(name, src, dst, x):
        step, mine = name + "_far", my_x if x else my_y

        def lines(k):
            return src.at[:, lax.rem(my_x + k, n_x)] if x else src.at[lax.rem(my_y + k, n_y)]

        loop(1, count_of(x), lambda k: send(lines(k), dst.at[mine], step, recv_of(step), "feat", along(x, k)))
        keep(lines(0), dst.at[mine], recv_of(step))
        if count_of(x) > 1:
            later(dst.at[pl.ds(0, count_of(x) - 1)], step)

    def fold_near(name, src, middle, dst, x):
        await_bytes(src, recv_of(name + "_far"))
        total = src[0].astype(F32)
        for line in range(1, count_of(x)):
            total += src[line].astype(F32)
        middle[...] = total.astype(BF16)
        step, mine = name + "_near", my_y if x else my_x

        def block(k):
            return middle.at[lax.rem(my_y + k, n_y) if x else lax.rem(my_x + k, n_x)]

        loop(1, count_of(not x), lambda k: send(block(k), dst.at[mine], step, recv_of(step), "feat", along(not x, k)))
        keep(block(0), dst.at[mine], recv_of(step))
        if count_of(not x) > 1:
            later(dst.at[pl.ds(0, count_of(not x) - 1)], step)

    def fold_end(name, src, x):
        await_bytes(src, recv_of(name + "_near"))
        total = src[0].astype(F32)
        for line in range(1, count_of(not x)):
            total += src[line].astype(F32)
        return total

    barrier = pltpu.get_barrier_semaphore()

    def greet(axis, peer):
        pl.semaphore_signal(barrier, inc=1, device_id={axis: peer}, device_id_type=MESH)

    reads = (
        (features_hbm, features),
        (serve_rows_hbm, serve_rows),
        (w1_self_hbm, w1_own.at[0]),
        (w1_neigh_hbm, w1_own.at[1]),
        (row_counts_hbm, row_counts),
        (index_one_hbm, index_rows),
        (index_two_hbm, index_two),
        (w2_self_hbm, w2.at[pl.ds(0, units)]),
        (w2_neigh_hbm, w2.at[pl.ds(units, units)]),
        (out_grad_hbm, out_grad),
    )
    reads = [pltpu.make_async_copy(src, dst, input_sems.at[i]) for i, (src, dst) in enumerate(reads)]
    for read in reads[:2]:
        read.start()

    def greet_pair(i):
        greet("store", store_peer(n_store // 2 - i))
        greet("store", store_peer(i - n_store // 2))

    greet("store", store_peer(n_store // 2))
    loop(1, n_store // 2, greet_pair)
    loop(1, n_feat, lambda k: greet("feat", feat_peer(k)))
    for read in reads[2:]:
        read.start()
    for group in range(n_feat):
        for half in range(2):
            w1_all[group, half, width:, :] = jnp.zeros((pad - width, hidden), BF16)
    both[...] = jnp.zeros_like(both)

    reads[0].wait()
    reads[1].wait()
    highs = papers // LOW
    for high in range(highs):
        table[high * width : (high + 1) * width, :] = features[:, high * LOW : (high + 1) * LOW].astype(BF16)
    low_ids = lax.broadcasted_iota(jnp.int32, (LOW, cap), 0)

    def serve(trainer):
        wanted = serve_rows[0, pl.ds(trainer, 1), :]
        low, high_of = wanted & (LOW - 1), wanted // LOW
        one_hot = jnp.where(low_ids == low, 1.0, 0.0).astype(BF16)
        found = dot(table[...], one_hot)
        total = found[0:width, :]
        for high in range(1, highs):
            total = jnp.where(high_of == high, found[high * width : (high + 1) * width, :], total)
        stage[trainer] = total.astype(BF16)

    loop(0, n_store, serve)
    for read in reads[2:]:
        read.wait()
    pl.semaphore_wait(barrier, n_store + n_feat - 2)

    half_store = n_store // 2
    group_size = n_store // GROUPS

    def send_rows(trainer, rank):
        send(stage.at[trainer], rows_in.at[rank], "rows", group_sems.at[rank // group_size], "store", trainer)

    def send_w1(peer):
        send(w1_own.at[my_core], w1_all.at[my_feat, my_core, pl.ds(0, width)], "w1", recv_of("w1"), "feat", peer)

    def send_pair(i):
        send_rows(store_peer(half_store - i), 2 * i - 1)
        send_rows(store_peer(i - half_store), 2 * i)

    def send_pair_and_w1(i):
        send_pair(i)
        send_w1(feat_peer(i))

    send_rows(store_peer(half_store), 0)
    shared = min(half_store, n_feat)
    loop(1, shared, send_pair_and_w1)
    loop(shared, half_store, send_pair)
    loop(shared, n_feat, lambda i: send_w1(feat_peer(i)))
    keep(stage.at[my_store], rows_in.at[n_store - 1], group_sems.at[GROUPS - 1])
    keep(w1_own.at[my_core], w1_all.at[my_feat, my_core, pl.ds(0, width)], recv_of("w1"))
    later(stage.at[pl.ds(0, n_store - 1)], "rows")
    later(w1_all.at[pl.ds(0, n_feat - 1), 0, pl.ds(0, width)], "w1")

    for entry in range(entries):
        index_one[entry : entry + 1, :] = index_rows[entry]
    raw = index_one[...]
    owners = raw // cap
    place = (raw & (cap - 1)).astype(F32)
    counts = jnp.ones(raw.shape, F32)
    for owner in range(n_store):
        counts = jnp.where(owners == owner, row_counts[0:1, owner : owner + 1].astype(F32), counts)
    place = place - jnp.floor((place + 0.5) / counts) * counts
    owner_of[0:entries, :] = owners
    place = place.astype(jnp.int32)
    slot_ids = lax.broadcasted_iota(jnp.int32, (cap, nodes), 0)
    for entry in range(entries):
        pick[entry] = jnp.where(slot_ids == place[entry : entry + 1, :], 1.0, 0.0).astype(BF16)

    strip = 64
    targets = index_two.shape[2]

    def second_tables(part):
        node_ids = lax.broadcasted_iota(jnp.int32, (strip, targets), 0) + part * strip
        at = pl.ds(pl.multiple_of(part * strip, strip), strip)
        self_t[at, :] = jnp.where(node_ids == index_two[0, 0:1, :], 1.0, 0.0).astype(BF16)
        total = jnp.zeros((strip, targets), F32)
        for entry in range(1, fan_two + 1):
            total += jnp.where(node_ids == index_two[0, entry : entry + 1, :], 1.0, 0.0)
        count_t[at, :] = total.astype(BF16)

    loop(0, nodes // strip, second_tables)

    def gather(group):
        await_bytes(rows_in.at[pl.ds(group * group_size, group_size)], group_sems.at[group])
        arrived = rows_in[pl.ds(group * group_size, group_size)].reshape(group_size * width, cap)
        owners = []
        for member in range(group_size):
            rank = group * group_size + member
            offset = half_store - (rank + 1) // 2 if member % 2 else rank // 2 - half_store
            owners.append(store_peer(-offset))
        sums = [both[0:width, :], both[pad : pad + width, :]]
        for entry in range(entries):
            found = dot(arrived, pick[entry])
            of = owner_of[entry : entry + 1, :]
            mine = jnp.zeros((width, nodes), F32)
            for member in range(group_size):
                mine = jnp.where(of == owners[member], found[member * width : (member + 1) * width, :], mine)
            sums[min(entry, 1)] += mine
        both[0:width, :], both[pad : pad + width, :] = sums

    loop(0, GROUPS - 2, gather)
    await_bytes(w1_all.at[:, 0, pl.ds(0, width)], recv_of("w1"))
    mine = w1_all.at[:, my_core, pl.ds(0, width)]
    send(mine, mine, "w1_swap", recv_of("w1_swap"), "store", my_store + 1 - 2 * my_core)
    later(w1_all.at[:, 0, pl.ds(0, width)], "w1_swap")
    loop(GROUPS - 2, GROUPS, gather)
    both[pad : pad + width, :] = both[pad : pad + width, :] / fan_one
    node_inputs[my_core] = both[...].astype(BF16)
    send(node_inputs.at[my_core], node_inputs.at[my_core], "inputs", recv_of("inputs"), "store", sibling)
    later(node_inputs.at[0], "inputs")
    turned = both[...].T.astype(BF16)
    for group in range(n_feat):
        nodes_out[group] = turned[group * own_rows : (group + 1) * own_rows, :]

    share(lambda peer: nodes_out.at[peer], nodes_in.at[my_feat], "nodes")
    later(nodes_out.at[pl.ds(0, n_feat - 1)], "nodes")

    await_bytes(w1_all.at[:, 0, pl.ds(0, width)], recv_of("w1_swap"))
    await_bytes(nodes_in, recv_of("nodes"))
    own_nodes = jnp.concatenate([nodes_in[group] for group in range(n_feat)], axis=1)
    slope_one = [None] * QUARTERS
    for stage_now in STAGES:
        for q in stage_now:
            cols = slice(q * columns, (q + 1) * columns)
            pre_one = dot(own_nodes, w1_all[:, :, :, cols].reshape(n_feat * 2 * pad, columns))
            hid_own[q] = (pre_one * jax.nn.sigmoid(pre_one)).astype(BF16)
            spread_near(f"hid{q}", hid_own.at[q], hid_all.at[q], q < 2)
            slope_one[q] = slope(pre_one)
    for stage_now in STAGES:
        for q in stage_now:
            spread_far(f"hid{q}", hid_all.at[q], q < 2)

    mixed = jnp.zeros((2 * units, nodes), F32)
    hid = [None] * QUARTERS
    for stage_now in STAGES:
        for q in stage_now:
            spread_end(f"hid{q}", hid_all.at[q], q < 2)
            hid[q] = hid_all[q].reshape(nodes, columns)
            mixed += nt_dot(w2[:, q * columns : (q + 1) * columns], hid[q])
    upper, lower = halves(mixed)
    self_term = dot(jnp.concatenate([upper[:units], lower[:units]], axis=0), self_t[...])
    neigh_term = dot(jnp.concatenate([upper[units:], lower[units:]], axis=0), count_t[...])
    pre_two = self_term[:units] + self_term[units:] + (neigh_term[:units] + neigh_term[units:]) / fan_two
    grad_two = (out_grad[...].astype(F32) * slope(pre_two)).astype(BF16)
    node_grad = jnp.concatenate([nt_dot(grad_two, self_t[...]), nt_dot(grad_two, count_t[...]) / fan_two], axis=0)
    upper, lower = halves(node_grad.T)
    turned = jnp.concatenate([upper, lower], axis=1)
    for stage_now in STAGES:
        for q in stage_now:
            weights = w2[:, q * columns : (q + 1) * columns]
            back = dot(turned, jnp.concatenate([weights, weights], axis=0))
            back_out[q] = back.astype(BF16).reshape(n_y, n_x, own_rows, columns)
            fold_far(f"back{q}", back_out.at[q], back_in[q], q >= 2)
    h2[...] = (pre_two * jax.nn.sigmoid(pre_two)).astype(BF16)
    write(h2, h2_hbm, 0)

    def total_of(ref, total, name, merged_already=False):
        tiles = ref.shape[1] // 2
        per = -(-tiles // n_chip)
        summers = tiles // per
        spread = summers * 4 == n_chip * 3

        def sums(chip):
            return lax.rem(chip, 4) != 3 if spread else chip < summers

        def first(chip):
            return (chip - chip // 4 if spread else chip) * per

        part, merged, arrived = ref.at[0], ref.at[1], ref.at[2]

        def fill(half, grad, row0=0):
            across = grad.shape[1] // 128
            for row in range(grad.shape[0] // 16):
                for col in range(across):
                    tile = grad[row * 16 : (row + 1) * 16, col * 128 : (col + 1) * 128]
                    if merged_already:
                        merged[tiles + row * across + col] = tile
                    else:
                        part[half * tiles + row * across + col] = tile

        def merge():
            own = pl.ds((1 - my_core) * tiles, tiles)
            send(part.at[own], merged.at[pl.ds(0, tiles)], name + "_merge", recv_of(name + "_merge"), "store", sibling)
            later(part.at[pl.ds(0, tiles)], name + "_merge")

        def reduce():
            if not merged_already:
                await_bytes(merged.at[pl.ds(0, tiles)], recv_of(name + "_merge"))
                both_cores = part[pl.ds(my_core * tiles, tiles)].astype(F32) + merged[0:tiles].astype(F32)
                merged[tiles : 2 * tiles] = both_cores.astype(BF16)

            def to(k):
                chip = chip_peer(k)

                @pl.when(sums(chip))
                def _():
                    send(
                        merged.at[pl.ds(tiles + first(chip), per)],
                        arrived.at[pl.ds(my_chip * per, per)],
                        name + "_reduce",
                        recv_of(name + "_reduce"),
                        "store",
                        chip * 2 + my_core,
                    )

            loop(1, n_chip, to)

            def sent():
                for count, wait_here in ((summers - 1, sums(my_chip)), (summers, jnp.logical_not(sums(my_chip)))):
                    if summers == n_chip and count == n_chip:
                        continue

                    @pl.when(wait_here)
                    def _(count=count):
                        await_bytes(merged.at[pl.ds(0, count * per)], send_sems.at[SENDS.index(name + "_reduce")])

            pending.append(sent)

        def spread_out():
            @pl.when(sums(my_chip))
            def _():
                mine = pl.ds(first(my_chip), per)
                keep(
                    merged.at[pl.ds(tiles + first(my_chip), per)],
                    arrived.at[pl.ds(my_chip * per, per)],
                    recv_of(name + "_reduce"),
                )
                await_bytes(arrived.at[pl.ds(0, n_chip * per)], recv_of(name + "_reduce"))
                summed = arrived[0:per].astype(F32)
                for chip in range(1, n_chip):
                    summed += arrived[chip * per : (chip + 1) * per].astype(F32)
                at = pl.ds(my_core * tiles + first(my_chip), per)
                total[at] = summed.astype(BF16)
                loop(
                    1,
                    n_chip,
                    lambda k: send(
                        total.at[at],
                        total.at[at],
                        name + "_spread",
                        recv_of(name + "_spread"),
                        "store",
                        chip_peer(k) * 2 + my_core,
                    ),
                )

            def sent():
                @pl.when(sums(my_chip))
                def _():
                    await_bytes(arrived.at[pl.ds(0, (n_chip - 1) * per)], send_sems.at[SENDS.index(name + "_spread")])

            pending.append(sent)

        def swap():
            for count, wait_here in ((summers - 1, sums(my_chip)), (summers, jnp.logical_not(sums(my_chip)))):
                if summers == n_chip and count == n_chip:
                    continue

                @pl.when(wait_here)
                def _(count=count):
                    await_bytes(total.at[pl.ds(0, count * per)], recv_of(name + "_spread"))

            mine = total.at[pl.ds(my_core * tiles, tiles)]
            send(mine, mine, name + "_swap", recv_of(name + "_swap"), "store", sibling)
            later(total.at[pl.ds(0, tiles)], name + "_swap")

        def finish():
            await_bytes(total.at[pl.ds(0, tiles)], recv_of(name + "_swap"))

        return fill, merge, reduce, spread_out, swap, finish

    fill, merge, reduce2, spread2, swap2, finish2 = total_of(w2_total, w2_sum, "w2")
    upper, lower = halves(node_grad)
    stacked = jnp.concatenate([upper, lower], axis=0)
    grad_w2 = jnp.concatenate([dot(stacked, part) for part in hid], axis=1)
    grad_w2 = (grad_w2[: 2 * units] + grad_w2[2 * units :]).astype(BF16)
    fill(0, grad_w2[:units])
    fill(1, grad_w2[units:])
    merge()
    reduce2()

    def slope_near(stage_no):
        for core, q in enumerate(STAGES[stage_no]):
            x, step, spot = core == 0, f"slope{q}_near", slope_all.at[stage_no, my_core, my_y, my_x]
            arrival = recv_of(f"slope{stage_no}_near")
            total = fold_end(f"back{q}", back_end[q], q >= 2)
            slope_own[q] = (total * slope_one[q]).astype(BF16)

            def to_line(k, x=x, step=step, spot=spot, arrival=arrival, core=core, q=q):
                chip = along(x, k)
                pltpu.make_async_remote_copy(
                    src_ref=slope_own.at[q],
                    dst_ref=spot,
                    send_sem=send_sems.at[SENDS.index(step)],
                    recv_sem=arrival,
                    device_id={"store": my_chip * 2 + core, "feat": chip},
                    device_id_type=MESH,
                ).start()

            loop(1, count_of(x), to_line)
            if count_of(x) > 1:
                later(slope_all.at[0, 0, 0, pl.ds(0, n_x - 1)] if x else slope_all.at[0, 0, pl.ds(0, n_y - 1), 0], step)

            if core == 0:
                later(slope_own.at[0], f"sibling{stage_no}")

            @pl.when(my_core == core)
            def _(arrival=arrival, q=q, spot=spot):
                keep(slope_own.at[q], spot, arrival)

            @pl.when(my_core != core)
            def _(arrival=arrival, q=q, spot=spot):
                send(slope_own.at[q], spot, f"sibling{stage_no}", arrival, "store", sibling)

    def slope_line(stage_no, x):
        return slope_all.at[stage_no, :, my_y] if x else slope_all.at[stage_no, :, :, my_x]

    def slope_rest(stage_no, x):
        return slope_all.at[stage_no, :, pl.ds(0, n_y - 1)] if x else slope_all.at[stage_no, :, :, pl.ds(0, n_x - 1)]

    def on_core(core, fn):
        pl.when(my_core == core)(fn)

    def slope_far(stage_no):
        step = f"slope{stage_no}_far"
        for core in range(2):
            x = core == 0

            def forward(x=x):
                line = slope_line(stage_no, x)
                await_bytes(line, recv_of(f"slope{stage_no}_near"))
                loop(1, count_of(not x), lambda k: send(line, line, step, recv_of(step), "feat", along(not x, k)))

            on_core(core, forward)

    def slope_end(stage_no, sems):
        for core in range(2):
            x = core == 0
            if count_of(not x) > 1:
                on_core(
                    core,
                    lambda x=x: await_bytes(slope_rest(stage_no, x), sems.at[SENDS.index(f"slope{stage_no}_far")]),
                )

    def first_weights(stage_no, fill):
        slope_end(stage_no, recv_sems)
        grad = jnp.zeros((2 * pad, columns), F32)
        for core in range(2):
            grad += dot(node_inputs[core], slope_all[stage_no, core].reshape(nodes, columns))
        grad = grad.astype(BF16)
        fill(0, jnp.concatenate([grad[0:width], grad[pad : pad + width]], axis=0))

    def fold_middle(stage_no):
        for q in STAGES[stage_no]:
            fold_near(f"back{q}", back_in[q], back_mid[q], back_end[q], q >= 2)

    fill_a, _, reduce_a, spread_a, swap_a, finish_a = total_of(w1_total_0, w1_sum_0, "w1_0", merged_already=True)
    fill_b, _, reduce_b, spread_b, swap_b, finish_b = total_of(w1_total_1, w1_sum_1, "w1_1", merged_already=True)
    fold_middle(0)
    fold_middle(1)
    slope_near(0)
    slope_near(1)
    slope_far(0)
    slope_far(1)
    spread2()
    await_bytes(node_inputs.at[0], recv_of("inputs"))
    first_weights(0, fill_a)
    reduce_a()
    first_weights(1, fill_b)
    reduce_b()
    swap2()
    spread_a()
    spread_b()
    finish2()
    across = hidden // 128
    for part, out in enumerate((w2_self_out, w2_neigh_out)):
        for row in range(units // 16):
            for col in range(across):
                w2_wide[part, row * 16 : (row + 1) * 16, col * 128 : (col + 1) * 128] = w2_sum[
                    (part * (units // 16) + row) * across + col
                ].astype(F32)
        write(w2_wide.at[part], out, 3 + part)
    swap_a()
    swap_b()
    each = across // QUARTERS
    for stage_no, (finish, total) in enumerate(((finish_a, w1_sum_0), (finish_b, w1_sum_1))):
        finish()
        for core, q in enumerate(STAGES[stage_no]):
            for row in range(2 * width // 16):
                part, at = row // (width // 16), row % (width // 16) * 16
                for col in range(each):
                    left = (q * each + col) * 128
                    w1_wide[part, at : at + 16, left : left + 128] = total[
                        (core * (2 * width // 16) + row) * each + col
                    ].astype(F32)
    write(w1_wide.at[0], w1_self_out, 1)
    write(w1_wide.at[1], w1_neigh_out, 2)
    pending.append(lambda: slope_end(0, send_sems))
    pending.append(lambda: slope_end(1, send_sems))

    for wait in pending:
        wait()


def hand_over(*refs):
    copies = [pltpu.make_async_copy(refs[i], refs[5 + i], refs[10].at[i]) for i in range(5)]
    for copy in copies:
        copy.start()
    for copy in copies:
        copy.wait()


def body(n_store, n_feat, *args):
    args = list(args)
    args[3] = jnp.transpose(args[3], (1, 0, 2))
    features, serve_rows, _, index_one, index_two, w1_self, _, w2_self, _, out_grad = args
    width, papers = features.shape
    cap = serve_rows.shape[2]
    entries, _, nodes = index_one.shape
    targets = index_two.shape[2]
    hidden, units = w2_self.shape[1], w2_self.shape[0]
    own_rows = nodes // n_feat
    pad = -(-width // 64) * 64
    columns = hidden // QUARTERS
    n_x = 1 << (n_feat.bit_length() // 2)
    n_y = n_feat // n_x
    blocks = (QUARTERS, n_y, n_x, own_rows, columns)
    tiles2 = units // 16 * (hidden // 128)
    tiles1 = 2 * width // 16 * (columns // 128)

    def total_scratch(tiles):
        per = -(-tiles // (n_store // 2))
        return pltpu.VMEM((3, max(2 * tiles, n_store // 2 * per), 16, 128), BF16)

    scratch = [
        pltpu.VMEM(features.shape, F32),
        pltpu.VMEM(serve_rows.shape, jnp.int32),
        pltpu.VMEM(args[2].shape, jnp.int32),
        pltpu.VMEM((entries, 1, nodes), jnp.int32),
        pltpu.VMEM((entries, nodes), jnp.int32),
        pltpu.VMEM(index_two.shape, jnp.int32),
        pltpu.VMEM((2 * units, hidden), BF16),
        pltpu.VMEM(out_grad.shape, BF16),
        pltpu.VMEM((papers // LOW * width, LOW), BF16),
        pltpu.VMEM((n_store, width, cap), BF16),
        pltpu.VMEM((n_store, width, cap), BF16),
        pltpu.VMEM((entries, nodes), jnp.int32),
        pltpu.VMEM((entries, cap, nodes), BF16),
        pltpu.VMEM((2 * pad, nodes), F32),
        pltpu.VMEM((2, 2 * pad, nodes), BF16),
        pltpu.VMEM((n_feat, own_rows, 2 * pad), BF16),
        pltpu.VMEM((n_feat, own_rows, 2 * pad), BF16),
        pltpu.VMEM((2, width, hidden), BF16),
        pltpu.VMEM((n_feat, 2, pad, hidden), BF16),
        pltpu.VMEM((QUARTERS, own_rows, columns), BF16),
        pltpu.VMEM(blocks, BF16),
        pltpu.VMEM((nodes, targets), BF16),
        pltpu.VMEM((nodes, targets), BF16),
        pltpu.VMEM(blocks, BF16),
        pltpu.VMEM((2, n_y, n_x, own_rows, columns), BF16),
        pltpu.VMEM((2, n_x, n_y, own_rows, columns), BF16),
        pltpu.VMEM((2, n_x, own_rows, columns), BF16),
        pltpu.VMEM((2, n_y, own_rows, columns), BF16),
        pltpu.VMEM((2, n_x, own_rows, columns), BF16),
        pltpu.VMEM((2, n_y, own_rows, columns), BF16),
        pltpu.VMEM((QUARTERS, own_rows, columns), BF16),
        pltpu.VMEM((2, 2, n_y, n_x, own_rows, columns), BF16),
        total_scratch(tiles2),
        total_scratch(tiles1),
        total_scratch(tiles1),
        pltpu.VMEM((2 * tiles2, 16, 128), BF16),
        pltpu.VMEM((2 * tiles1, 16, 128), BF16),
        pltpu.VMEM((2 * tiles1, 16, 128), BF16),
        pltpu.VMEM((units, targets), BF16),
        pltpu.VMEM((2, width, hidden), F32),
        pltpu.VMEM((2, units, hidden), F32),
        pltpu.SemaphoreType.DMA((INPUTS,)),
        pltpu.SemaphoreType.DMA((5,)),
        pltpu.SemaphoreType.DMA((len(SENDS),)),
        pltpu.SemaphoreType.DMA((len(SENDS),)),
        pltpu.SemaphoreType.DMA((GROUPS,)),
    ]
    outs = [
        jax.ShapeDtypeStruct((units, targets), BF16),
        jax.ShapeDtypeStruct((width, hidden), F32),
        jax.ShapeDtypeStruct((width, hidden), F32),
        jax.ShapeDtypeStruct((units, hidden), F32),
        jax.ShapeDtypeStruct((units, hidden), F32),
    ]
    found = pl.pallas_call(
        functools.partial(kernel, n_store, n_feat),
        out_shape=outs,
        in_specs=[pl.BlockSpec(memory_space=pltpu.HBM)] * len(args),
        out_specs=[pl.BlockSpec(memory_space=pltpu.HBM)] * 5,
        scratch_shapes=scratch,
        compiler_params=pltpu.CompilerParams(collective_id=0, has_side_effects=True, vmem_limit_bytes=VMEM_LIMIT),
    )(*args)
    return pl.pallas_call(
        hand_over,
        out_shape=outs,
        in_specs=[pl.BlockSpec(memory_space=pltpu.HBM)] * 5,
        out_specs=[pl.BlockSpec(memory_space=pltpu.HBM)] * 5,
        scratch_shapes=[pltpu.SemaphoreType.DMA((5,))],
        compiler_params=pltpu.CompilerParams(vmem_limit_bytes=VMEM_LIMIT),
    )(*found)


def solution(mesh):
    return jax.shard_map(
        functools.partial(body, mesh.shape["store"], mesh.shape["feat"]),
        mesh=mesh,
        in_specs=(
            P("feat", "store"),
            P("store", None, None),
            P("store", None),
            P("store", None, None),
            P("store", None, None),
            P("feat", None),
            P("feat", None),
            P("feat", None),
            P("feat", None),
            P("feat", "store"),
        ),
        out_specs=(
            P("feat", "store"),
            P("feat", None),
            P("feat", None),
            P("feat", None),
            P("feat", None),
        ),
        check_vma=False,
    )
```

```python
import functools

import jax
import jax.numpy as jnp
from jax import lax
from jax.experimental import pallas as pl
from jax.experimental.pallas import tpu as pltpu
from jax.sharding import PartitionSpec as P

MESH = pl.DeviceIdType.MESH
F32 = jnp.float32
BF16 = jnp.bfloat16
LOW = 256


def slope(values):
    sig = jax.nn.sigmoid(values)
    return sig * (1.0 + values * (1.0 - sig))


def nt_dot(left, right):
    return lax.dot_general(left, right, (((1,), (1,)), ((), ())), preferred_element_type=F32)


def dot(left, right):
    return jnp.dot(left, right, preferred_element_type=F32)


def halves(values):
    upper = values.astype(BF16)
    return upper, (values - upper.astype(F32)).astype(BF16)


def await_bytes(ref, sem):
    pltpu.make_async_copy(ref, ref, sem).wait()


SENDS = (
    ("rows", "w1", "w1_swap", "nodes")
    + ("inputs", "sibling0", "sibling1")
    + tuple(what + quarter + step for what in ("hid", "back", "slope") for quarter in "0123" for step in ("_near", "_far"))
    + tuple(total + step for total in ("w2", "w1_0", "w1_1") for step in ("_merge", "_reduce", "_spread", "_swap"))
)
INPUTS = 10
GROUPS = 8
QUARTERS = 4
STAGES = ((0, 2), (1, 3))
VMEM_LIMIT = 60 * 1024 * 1024


def kernel(
    n_store,
    n_feat,
    features_hbm,
    serve_rows_hbm,
    row_counts_hbm,
    index_one_hbm,
    index_two_hbm,
    w1_self_hbm,
    w1_neigh_hbm,
    w2_self_hbm,
    w2_neigh_hbm,
    out_grad_hbm,
    h2_hbm,
    w1_self_out,
    w1_neigh_out,
    w2_self_out,
    w2_neigh_out,
    features,
    serve_rows,
    row_counts,
    index_rows,
    index_one,
    index_two,
    w2,
    out_grad,
    table,
    stage,
    rows_in,
    owner_of,
    pick,
    both,
    node_inputs,
    nodes_out,
    nodes_in,
    w1_own,
    w1_all,
    hid_own,
    hid_all,
    self_t,
    count_t,
    back_out,
    back_in_0,
    back_in_1,
    back_mid_0,
    back_mid_1,
    back_end_0,
    back_end_1,
    slope_own,
    slope_all,
    w2_total,
    w1_total_0,
    w1_total_1,
    w2_sum,
    w1_sum_0,
    w1_sum_1,
    h2,
    w1_wide,
    w2_wide,
    input_sems,
    output_sems,
    send_sems,
    recv_sems,
    group_sems,
):
    my_store, my_feat = lax.axis_index("store"), lax.axis_index("feat")
    my_chip, my_core = my_store // 2, lax.rem(my_store, 2)
    n_chip = n_store // 2
    n_x = 1 << (n_feat.bit_length() // 2)
    n_y = n_feat // n_x
    my_y, my_x = my_feat // n_x, lax.rem(my_feat, n_x)
    width, papers = features.shape
    cap = serve_rows.shape[2]
    entries, nodes = index_one.shape
    fan_one = entries - 1
    fan_two = index_two.shape[1] - 1
    units, hidden = w2.shape[0] // 2, w2.shape[1]
    columns = hidden // QUARTERS
    own_rows = nodes // n_feat
    pad = both.shape[0] // 2
    pending = []
    back_in = (back_in_0.at[0], back_in_0.at[1], back_in_1.at[0], back_in_1.at[1])
    back_mid = (back_mid_0.at[0], back_mid_0.at[1], back_mid_1.at[0], back_mid_1.at[1])
    back_end = (back_end_0.at[0], back_end_0.at[1], back_end_1.at[0], back_end_1.at[1])
    sibling = my_store + 1 - 2 * my_core

    def store_peer(step):
        return lax.rem(my_store + step + n_store, n_store)

    def feat_peer(step):
        return lax.rem(my_feat + step + n_feat, n_feat)

    def chip_peer(step):
        return lax.rem(my_chip + step + n_chip, n_chip)

    def send(src, dst, name, recv_sem, axis, peer):
        pltpu.make_async_remote_copy(
            src_ref=src,
            dst_ref=dst,
            send_sem=send_sems.at[SENDS.index(name)],
            recv_sem=recv_sem,
            device_id={axis: peer},
            device_id_type=MESH,
        ).start()

    def recv_of(name):
        return recv_sems.at[SENDS.index(name)]

    def later(ref, name):
        pending.append(lambda: await_bytes(ref, send_sems.at[SENDS.index(name)]))

    def keep(src, dst, sem):
        pltpu.make_async_copy(src, dst, sem).start()

    def write(src, dst, i):
        copy = pltpu.make_async_copy(src, dst, output_sems.at[i])
        copy.start()
        pending.append(copy.wait)

    def loop(low, high, fn):
        def step(k, carry):
            fn(k)
            return carry

        lax.fori_loop(low, high, step, 0)

    def each_chip(fn):
        fn(chip_peer(n_chip // 2))

        def pair(i):
            fn(chip_peer(n_chip // 2 - i))
            fn(chip_peer(i - n_chip // 2))

        loop(1, n_chip // 2, pair)

    def share(src_of, dst, name):
        loop(1, n_feat, lambda k: send(src_of(feat_peer(k)), dst, name, recv_of(name), "feat", feat_peer(k)))
        keep(src_of(my_feat), dst, recv_of(name))

    def along(x, k):
        return my_y * n_x + lax.rem(my_x + k, n_x) if x else lax.rem(my_y + k, n_y) * n_x + my_x

    def count_of(x):
        return n_x if x else n_y

    def spread_near(name, own, dst, x):
        step, spot = name + "_near", dst.at[my_y, my_x]
        loop(1, count_of(x), lambda k: send(own, spot, step, recv_of(step), "feat", along(x, k)))
        keep(own, spot, recv_of(step))
        if count_of(x) > 1:
            later(dst.at[0, pl.ds(0, n_x - 1)] if x else dst.at[pl.ds(0, n_y - 1), 0], step)

    def spread_far(name, dst, x):
        step, line = name + "_far", dst.at[my_y] if x else dst.at[:, my_x]
        await_bytes(line, recv_of(name + "_near"))
        loop(1, count_of(not x), lambda k: send(line, line, step, recv_of(step), "feat", along(not x, k)))
        if count_of(not x) > 1:
            later(dst.at[pl.ds(0, n_y - 1)] if x else dst.at[:, pl.ds(0, n_x - 1)], step)

    def spread_end(name, dst, x):
        if count_of(not x) > 1:
            await_bytes(dst.at[pl.ds(0, n_y - 1)] if x else dst.at[:, pl.ds(0, n_x - 1)], recv_of(name + "_far"))

    def fold_far(name, src, dst, x):
        step, mine = name + "_far", my_x if x else my_y

        def lines(k):
            return src.at[:, lax.rem(my_x + k, n_x)] if x else src.at[lax.rem(my_y + k, n_y)]

        loop(1, count_of(x), lambda k: send(lines(k), dst.at[mine], step, recv_of(step), "feat", along(x, k)))
        keep(lines(0), dst.at[mine], recv_of(step))
        if count_of(x) > 1:
            later(dst.at[pl.ds(0, count_of(x) - 1)], step)

    def fold_near(name, src, middle, dst, x):
        await_bytes(src, recv_of(name + "_far"))
        total = src[0].astype(F32)
        for line in range(1, count_of(x)):
            total += src[line].astype(F32)
        middle[...] = total.astype(BF16)
        step, mine = name + "_near", my_y if x else my_x

        def block(k):
            return middle.at[lax.rem(my_y + k, n_y) if x else lax.rem(my_x + k, n_x)]

        loop(1, count_of(not x), lambda k: send(block(k), dst.at[mine], step, recv_of(step), "feat", along(not x, k)))
        keep(block(0), dst.at[mine], recv_of(step))
        if count_of(not x) > 1:
            later(dst.at[pl.ds(0, count_of(not x) - 1)], step)

    def fold_end(name, src, x):
        await_bytes(src, recv_of(name + "_near"))
        total = src[0].astype(F32)
        for line in range(1, count_of(not x)):
            total += src[line].astype(F32)
        return total

    barrier = pltpu.get_barrier_semaphore()

    def greet(axis, peer):
        pl.semaphore_signal(barrier, inc=1, device_id={axis: peer}, device_id_type=MESH)

    reads = (
        (features_hbm, features),
        (serve_rows_hbm, serve_rows),
        (w1_self_hbm, w1_own.at[0]),
        (w1_neigh_hbm, w1_own.at[1]),
        (row_counts_hbm, row_counts),
        (index_one_hbm, index_rows),
        (index_two_hbm, index_two),
        (w2_self_hbm, w2.at[pl.ds(0, units)]),
        (w2_neigh_hbm, w2.at[pl.ds(units, units)]),
        (out_grad_hbm, out_grad),
    )
    reads = [pltpu.make_async_copy(src, dst, input_sems.at[i]) for i, (src, dst) in enumerate(reads)]
    for read in reads[:2]:
        read.start()

    def greet_pair(i):
        greet("store", store_peer(n_store // 2 - i))
        greet("store", store_peer(i - n_store // 2))

    greet("store", store_peer(n_store // 2))
    loop(1, n_store // 2, greet_pair)
    loop(1, n_feat, lambda k: greet("feat", feat_peer(k)))
    for read in reads[2:]:
        read.start()
    for group in range(n_feat):
        for half in range(2):
            w1_all[group, half, width:, :] = jnp.zeros((pad - width, hidden), BF16)
    both[...] = jnp.zeros_like(both)

    reads[0].wait()
    reads[1].wait()
    highs = papers // LOW
    for high in range(highs):
        table[high * width : (high + 1) * width, :] = features[:, high * LOW : (high + 1) * LOW].astype(BF16)
    low_ids = lax.broadcasted_iota(jnp.int32, (LOW, cap), 0)

    def serve(trainer):
        wanted = serve_rows[0, pl.ds(trainer, 1), :]
        low, high_of = wanted & (LOW - 1), wanted // LOW
        one_hot = jnp.where(low_ids == low, 1.0, 0.0).astype(BF16)
        found = dot(table[...], one_hot)
        total = found[0:width, :]
        for high in range(1, highs):
            total = jnp.where(high_of == high, found[high * width : (high + 1) * width, :], total)
        stage[trainer] = total.astype(BF16)

    def serve_two(i):
        serve(2 * i)
        serve(2 * i + 1)

    loop(0, n_store // 2, serve_two)
    for read in reads[2:]:
        read.wait()
    pl.semaphore_wait(barrier, n_store + n_feat - 2)

    half_store = n_store // 2
    group_size = n_store // GROUPS

    def send_rows(trainer, rank):
        send(stage.at[trainer], rows_in.at[rank], "rows", group_sems.at[rank // group_size], "store", trainer)

    def send_w1(peer):
        send(w1_own.at[my_core], w1_all.at[my_feat, my_core, pl.ds(0, width)], "w1", recv_of("w1"), "feat", peer)

    def send_pair(i):
        send_rows(store_peer(half_store - i), 2 * i - 1)
        send_rows(store_peer(i - half_store), 2 * i)

    def send_pair_and_w1(i):
        send_pair(i)
        send_w1(feat_peer(i))

    send_rows(store_peer(half_store), 0)
    shared = min(half_store, n_feat)
    loop(1, shared, send_pair_and_w1)
    loop(shared, half_store, send_pair)
    loop(shared, n_feat, lambda i: send_w1(feat_peer(i)))
    keep(stage.at[my_store], rows_in.at[n_store - 1], group_sems.at[GROUPS - 1])
    keep(w1_own.at[my_core], w1_all.at[my_feat, my_core, pl.ds(0, width)], recv_of("w1"))
    later(stage.at[pl.ds(0, n_store - 1)], "rows")
    later(w1_all.at[pl.ds(0, n_feat - 1), 0, pl.ds(0, width)], "w1")

    for entry in range(entries):
        index_one[entry : entry + 1, :] = index_rows[entry]
    raw = index_one[...]
    owners = raw // cap
    place = (raw & (cap - 1)).astype(F32)
    counts = jnp.ones(raw.shape, F32)
    for owner in range(n_store):
        counts = jnp.where(owners == owner, row_counts[0:1, owner : owner + 1].astype(F32), counts)
    place = place - jnp.floor((place + 0.5) / counts) * counts
    owner_of[0:entries, :] = owners
    place = place.astype(jnp.int32)
    slot_ids = lax.broadcasted_iota(jnp.int32, (cap, nodes), 0)
    for entry in range(entries):
        pick[entry] = jnp.where(slot_ids == place[entry : entry + 1, :], 1.0, 0.0).astype(BF16)

    strip = 64
    targets = index_two.shape[2]

    def second_tables(part):
        node_ids = lax.broadcasted_iota(jnp.int32, (strip, targets), 0) + part * strip
        at = pl.ds(pl.multiple_of(part * strip, strip), strip)
        self_t[at, :] = jnp.where(node_ids == index_two[0, 0:1, :], 1.0, 0.0).astype(BF16)
        total = jnp.zeros((strip, targets), F32)
        for entry in range(1, fan_two + 1):
            total += jnp.where(node_ids == index_two[0, entry : entry + 1, :], 1.0, 0.0)
        count_t[at, :] = total.astype(BF16)

    loop(0, nodes // strip, second_tables)

    def gather(group):
        await_bytes(rows_in.at[pl.ds(group * group_size, group_size)], group_sems.at[group])
        arrived = rows_in[pl.ds(group * group_size, group_size)].reshape(group_size * width, cap)
        owners = []
        for member in range(group_size):
            rank = group * group_size + member
            offset = half_store - (rank + 1) // 2 if member % 2 else rank // 2 - half_store
            owners.append(store_peer(-offset))
        sums = [both[0:width, :], both[pad : pad + width, :]]
        for entry in range(entries):
            found = dot(arrived, pick[entry])
            of = owner_of[entry : entry + 1, :]
            mine = jnp.zeros((width, nodes), F32)
            for member in range(group_size):
                mine = jnp.where(of == owners[member], found[member * width : (member + 1) * width, :], mine)
            sums[min(entry, 1)] += mine
        both[0:width, :], both[pad : pad + width, :] = sums

    loop(0, GROUPS - 2, gather)
    await_bytes(w1_all.at[:, 0, pl.ds(0, width)], recv_of("w1"))
    mine = w1_all.at[:, my_core, pl.ds(0, width)]
    send(mine, mine, "w1_swap", recv_of("w1_swap"), "store", my_store + 1 - 2 * my_core)
    later(w1_all.at[:, 0, pl.ds(0, width)], "w1_swap")
    loop(GROUPS - 2, GROUPS, gather)
    both[pad : pad + width, :] = both[pad : pad + width, :] / fan_one
    node_inputs[my_core] = both[...].astype(BF16)
    send(node_inputs.at[my_core], node_inputs.at[my_core], "inputs", recv_of("inputs"), "store", sibling)
    later(node_inputs.at[0], "inputs")
    turned = both[...].T.astype(BF16)
    for group in range(n_feat):
        nodes_out[group] = turned[group * own_rows : (group + 1) * own_rows, :]

    share(lambda peer: nodes_out.at[peer], nodes_in.at[my_feat], "nodes")
    later(nodes_out.at[pl.ds(0, n_feat - 1)], "nodes")

    await_bytes(w1_all.at[:, 0, pl.ds(0, width)], recv_of("w1_swap"))
    await_bytes(nodes_in, recv_of("nodes"))
    own_nodes = jnp.concatenate([nodes_in[group] for group in range(n_feat)], axis=1)
    slope_one = [None] * QUARTERS
    for stage_now in STAGES:
        for q in stage_now:
            cols = slice(q * columns, (q + 1) * columns)
            pre_one = dot(own_nodes, w1_all[:, :, :, cols].reshape(n_feat * 2 * pad, columns))
            hid_own[q] = (pre_one * jax.nn.sigmoid(pre_one)).astype(BF16)
            spread_near(f"hid{q}", hid_own.at[q], hid_all.at[q], q < 2)
            slope_one[q] = slope(pre_one)
    for stage_now in STAGES:
        for q in stage_now:
            spread_far(f"hid{q}", hid_all.at[q], q < 2)

    mixed = jnp.zeros((2 * units, nodes), F32)
    hid = [None] * QUARTERS
    for stage_now in STAGES:
        for q in stage_now:
            spread_end(f"hid{q}", hid_all.at[q], q < 2)
            hid[q] = hid_all[q].reshape(nodes, columns)
            mixed += nt_dot(w2[:, q * columns : (q + 1) * columns], hid[q])
    upper, lower = halves(mixed)
    self_term = dot(jnp.concatenate([upper[:units], lower[:units]], axis=0), self_t[...])
    neigh_term = dot(jnp.concatenate([upper[units:], lower[units:]], axis=0), count_t[...])
    pre_two = self_term[:units] + self_term[units:] + (neigh_term[:units] + neigh_term[units:]) / fan_two
    grad_two = (out_grad[...].astype(F32) * slope(pre_two)).astype(BF16)
    node_grad = jnp.concatenate([nt_dot(grad_two, self_t[...]), nt_dot(grad_two, count_t[...]) / fan_two], axis=0)
    upper, lower = halves(node_grad.T)
    turned = jnp.concatenate([upper, lower], axis=1)
    for stage_now in STAGES:
        for q in stage_now:
            weights = w2[:, q * columns : (q + 1) * columns]
            back = dot(turned, jnp.concatenate([weights, weights], axis=0))
            back_out[q] = back.astype(BF16).reshape(n_y, n_x, own_rows, columns)
            fold_far(f"back{q}", back_out.at[q], back_in[q], q >= 2)
    h2[...] = (pre_two * jax.nn.sigmoid(pre_two)).astype(BF16)
    write(h2, h2_hbm, 0)

    def total_of(ref, total, name, merged_already=False):
        tiles = ref.shape[1] // 2
        per = -(-tiles // n_chip)
        summers = tiles // per
        spread = summers * 4 == n_chip * 3

        def sums(chip):
            return lax.rem(chip, 4) != 3 if spread else chip < summers

        def first(chip):
            return (chip - chip // 4 if spread else chip) * per

        part, merged, arrived = ref.at[0], ref.at[1], ref.at[2]

        def fill(half, grad, row0=0):
            across = grad.shape[1] // 128
            for row in range(grad.shape[0] // 16):
                for col in range(across):
                    tile = grad[row * 16 : (row + 1) * 16, col * 128 : (col + 1) * 128]
                    if merged_already:
                        merged[tiles + row * across + col] = tile
                    else:
                        part[half * tiles + row * across + col] = tile

        def merge():
            own = pl.ds((1 - my_core) * tiles, tiles)
            send(part.at[own], merged.at[pl.ds(0, tiles)], name + "_merge", recv_of(name + "_merge"), "store", sibling)
            later(part.at[pl.ds(0, tiles)], name + "_merge")

        def reduce():
            if not merged_already:
                await_bytes(merged.at[pl.ds(0, tiles)], recv_of(name + "_merge"))
                both_cores = part[pl.ds(my_core * tiles, tiles)].astype(F32) + merged[0:tiles].astype(F32)
                merged[tiles : 2 * tiles] = both_cores.astype(BF16)

            def to(chip):
                @pl.when(sums(chip))
                def _():
                    send(
                        merged.at[pl.ds(tiles + first(chip), per)],
                        arrived.at[pl.ds(my_chip * per, per)],
                        name + "_reduce",
                        recv_of(name + "_reduce"),
                        "store",
                        chip * 2 + my_core,
                    )

            each_chip(to)

            def sent():
                for count, wait_here in ((summers - 1, sums(my_chip)), (summers, jnp.logical_not(sums(my_chip)))):
                    if summers == n_chip and count == n_chip:
                        continue

                    @pl.when(wait_here)
                    def _(count=count):
                        await_bytes(merged.at[pl.ds(0, count * per)], send_sems.at[SENDS.index(name + "_reduce")])

            pending.append(sent)

        def spread_out():
            @pl.when(sums(my_chip))
            def _():
                mine = pl.ds(first(my_chip), per)
                keep(
                    merged.at[pl.ds(tiles + first(my_chip), per)],
                    arrived.at[pl.ds(my_chip * per, per)],
                    recv_of(name + "_reduce"),
                )
                await_bytes(arrived.at[pl.ds(0, n_chip * per)], recv_of(name + "_reduce"))
                summed = arrived[0:per].astype(F32)
                for chip in range(1, n_chip):
                    summed += arrived[chip * per : (chip + 1) * per].astype(F32)
                at = pl.ds(my_core * tiles + first(my_chip), per)
                total[at] = summed.astype(BF16)
                each_chip(
                    lambda chip: send(
                        total.at[at],
                        total.at[at],
                        name + "_spread",
                        recv_of(name + "_spread"),
                        "store",
                        chip * 2 + my_core,
                    )
                )

            def sent():
                @pl.when(sums(my_chip))
                def _():
                    await_bytes(arrived.at[pl.ds(0, (n_chip - 1) * per)], send_sems.at[SENDS.index(name + "_spread")])

            pending.append(sent)

        def swap():
            for count, wait_here in ((summers - 1, sums(my_chip)), (summers, jnp.logical_not(sums(my_chip)))):
                if summers == n_chip and count == n_chip:
                    continue

                @pl.when(wait_here)
                def _(count=count):
                    await_bytes(total.at[pl.ds(0, count * per)], recv_of(name + "_spread"))

            mine = total.at[pl.ds(my_core * tiles, tiles)]
            send(mine, mine, name + "_swap", recv_of(name + "_swap"), "store", sibling)
            later(total.at[pl.ds(0, tiles)], name + "_swap")

        def finish():
            await_bytes(total.at[pl.ds(0, tiles)], recv_of(name + "_swap"))

        return fill, merge, reduce, spread_out, swap, finish

    fill, merge, reduce2, spread2, swap2, finish2 = total_of(w2_total, w2_sum, "w2")
    upper, lower = halves(node_grad)
    stacked = jnp.concatenate([upper, lower], axis=0)
    grad_w2 = jnp.concatenate([dot(stacked, part) for part in hid], axis=1)
    grad_w2 = (grad_w2[: 2 * units] + grad_w2[2 * units :]).astype(BF16)
    fill(0, grad_w2[:units])
    fill(1, grad_w2[units:])
    merge()
    reduce2()

    def slope_near(stage_no):
        for core, q in enumerate(STAGES[stage_no]):
            x, step, spot = core == 0, f"slope{q}_near", slope_all.at[stage_no, my_core, my_y, my_x]
            arrival = recv_of(f"slope{stage_no}_near")
            total = fold_end(f"back{q}", back_end[q], q >= 2)
            slope_own[q] = (total * slope_one[q]).astype(BF16)

            def to_line(k, x=x, step=step, spot=spot, arrival=arrival, core=core, q=q):
                chip = along(x, k)
                pltpu.make_async_remote_copy(
                    src_ref=slope_own.at[q],
                    dst_ref=spot,
                    send_sem=send_sems.at[SENDS.index(step)],
                    recv_sem=arrival,
                    device_id={"store": my_chip * 2 + core, "feat": chip},
                    device_id_type=MESH,
                ).start()

            loop(1, count_of(x), to_line)
            if count_of(x) > 1:
                later(slope_all.at[0, 0, 0, pl.ds(0, n_x - 1)] if x else slope_all.at[0, 0, pl.ds(0, n_y - 1), 0], step)

            if core == 0:
                later(slope_own.at[0], f"sibling{stage_no}")

            @pl.when(my_core == core)
            def _(arrival=arrival, q=q, spot=spot):
                keep(slope_own.at[q], spot, arrival)

            @pl.when(my_core != core)
            def _(arrival=arrival, q=q, spot=spot):
                send(slope_own.at[q], spot, f"sibling{stage_no}", arrival, "store", sibling)

    def slope_line(stage_no, x):
        return slope_all.at[stage_no, :, my_y] if x else slope_all.at[stage_no, :, :, my_x]

    def slope_rest(stage_no, x):
        return slope_all.at[stage_no, :, pl.ds(0, n_y - 1)] if x else slope_all.at[stage_no, :, :, pl.ds(0, n_x - 1)]

    def on_core(core, fn):
        pl.when(my_core == core)(fn)

    def slope_far(stage_no):
        step = f"slope{stage_no}_far"
        for core in range(2):
            x = core == 0

            def forward(x=x):
                line = slope_line(stage_no, x)
                await_bytes(line, recv_of(f"slope{stage_no}_near"))
                loop(1, count_of(not x), lambda k: send(line, line, step, recv_of(step), "feat", along(not x, k)))

            on_core(core, forward)

    def slope_end(stage_no, sems):
        for core in range(2):
            x = core == 0
            if count_of(not x) > 1:
                on_core(
                    core,
                    lambda x=x: await_bytes(slope_rest(stage_no, x), sems.at[SENDS.index(f"slope{stage_no}_far")]),
                )

    def first_weights(stage_no, fill):
        slope_end(stage_no, recv_sems)
        grad = jnp.zeros((2 * pad, columns), F32)
        for core in range(2):
            grad += dot(node_inputs[core], slope_all[stage_no, core].reshape(nodes, columns))
        grad = grad.astype(BF16)
        fill(0, jnp.concatenate([grad[0:width], grad[pad : pad + width]], axis=0))

    def fold_middle(stage_no):
        for q in STAGES[stage_no]:
            fold_near(f"back{q}", back_in[q], back_mid[q], back_end[q], q >= 2)

    fill_a, _, reduce_a, spread_a, swap_a, finish_a = total_of(w1_total_0, w1_sum_0, "w1_0", merged_already=True)
    fill_b, _, reduce_b, spread_b, swap_b, finish_b = total_of(w1_total_1, w1_sum_1, "w1_1", merged_already=True)
    fold_middle(0)
    fold_middle(1)
    slope_near(0)
    slope_near(1)
    slope_far(0)
    slope_far(1)
    spread2()
    await_bytes(node_inputs.at[0], recv_of("inputs"))
    first_weights(0, fill_a)
    reduce_a()
    first_weights(1, fill_b)
    reduce_b()
    swap2()
    spread_a()
    spread_b()
    finish2()
    across = hidden // 128
    for part, out in enumerate((w2_self_out, w2_neigh_out)):
        for row in range(units // 16):
            for col in range(across):
                w2_wide[part, row * 16 : (row + 1) * 16, col * 128 : (col + 1) * 128] = w2_sum[
                    (part * (units // 16) + row) * across + col
                ].astype(F32)
        write(w2_wide.at[part], out, 3 + part)
    swap_a()
    swap_b()
    each = across // QUARTERS
    for stage_no, (finish, total) in enumerate(((finish_a, w1_sum_0), (finish_b, w1_sum_1))):
        finish()
        for core, q in enumerate(STAGES[stage_no]):
            for row in range(2 * width // 16):
                part, at = row // (width // 16), row % (width // 16) * 16
                for col in range(each):
                    left = (q * each + col) * 128
                    w1_wide[part, at : at + 16, left : left + 128] = total[
                        (core * (2 * width // 16) + row) * each + col
                    ].astype(F32)
    write(w1_wide.at[0], w1_self_out, 1)
    write(w1_wide.at[1], w1_neigh_out, 2)
    pending.append(lambda: slope_end(0, send_sems))
    pending.append(lambda: slope_end(1, send_sems))

    for wait in pending:
        wait()


def hand_over(*refs):
    src, dst, held, sems = refs[:5], refs[5:10], refs[10:15], refs[15]
    reads = [pltpu.make_async_copy(src[i], held[i], sems.at[i]) for i in range(5)]
    writes = [pltpu.make_async_copy(held[i], dst[i], sems.at[5 + i]) for i in range(5)]
    for read in reads:
        read.start()
    for read, copy in zip(reads, writes):
        read.wait()
        copy.start()
    for copy in writes:
        copy.wait()


def body(n_store, n_feat, *args):
    args = list(args)
    args[3] = jnp.transpose(args[3], (1, 0, 2))
    features, serve_rows, _, index_one, index_two, w1_self, _, w2_self, _, out_grad = args
    width, papers = features.shape
    cap = serve_rows.shape[2]
    entries, _, nodes = index_one.shape
    targets = index_two.shape[2]
    hidden, units = w2_self.shape[1], w2_self.shape[0]
    own_rows = nodes // n_feat
    pad = -(-width // 64) * 64
    columns = hidden // QUARTERS
    n_x = 1 << (n_feat.bit_length() // 2)
    n_y = n_feat // n_x
    blocks = (QUARTERS, n_y, n_x, own_rows, columns)
    tiles2 = units // 16 * (hidden // 128)
    tiles1 = 2 * width // 16 * (columns // 128)

    def total_scratch(tiles):
        per = -(-tiles // (n_store // 2))
        return pltpu.VMEM((3, max(2 * tiles, n_store // 2 * per), 16, 128), BF16)

    scratch = [
        pltpu.VMEM(features.shape, F32),
        pltpu.VMEM(serve_rows.shape, jnp.int32),
        pltpu.VMEM(args[2].shape, jnp.int32),
        pltpu.VMEM((entries, 1, nodes), jnp.int32),
        pltpu.VMEM((entries, nodes), jnp.int32),
        pltpu.VMEM(index_two.shape, jnp.int32),
        pltpu.VMEM((2 * units, hidden), BF16),
        pltpu.VMEM(out_grad.shape, BF16),
        pltpu.VMEM((papers // LOW * width, LOW), BF16),
        pltpu.VMEM((n_store, width, cap), BF16),
        pltpu.VMEM((n_store, width, cap), BF16),
        pltpu.VMEM((entries, nodes), jnp.int32),
        pltpu.VMEM((entries, cap, nodes), BF16),
        pltpu.VMEM((2 * pad, nodes), F32),
        pltpu.VMEM((2, 2 * pad, nodes), BF16),
        pltpu.VMEM((n_feat, own_rows, 2 * pad), BF16),
        pltpu.VMEM((n_feat, own_rows, 2 * pad), BF16),
        pltpu.VMEM((2, width, hidden), BF16),
        pltpu.VMEM((n_feat, 2, pad, hidden), BF16),
        pltpu.VMEM((QUARTERS, own_rows, columns), BF16),
        pltpu.VMEM(blocks, BF16),
        pltpu.VMEM((nodes, targets), BF16),
        pltpu.VMEM((nodes, targets), BF16),
        pltpu.VMEM(blocks, BF16),
        pltpu.VMEM((2, n_y, n_x, own_rows, columns), BF16),
        pltpu.VMEM((2, n_x, n_y, own_rows, columns), BF16),
        pltpu.VMEM((2, n_x, own_rows, columns), BF16),
        pltpu.VMEM((2, n_y, own_rows, columns), BF16),
        pltpu.VMEM((2, n_x, own_rows, columns), BF16),
        pltpu.VMEM((2, n_y, own_rows, columns), BF16),
        pltpu.VMEM((QUARTERS, own_rows, columns), BF16),
        pltpu.VMEM((2, 2, n_y, n_x, own_rows, columns), BF16),
        total_scratch(tiles2),
        total_scratch(tiles1),
        total_scratch(tiles1),
        pltpu.VMEM((2 * tiles2, 16, 128), BF16),
        pltpu.VMEM((2 * tiles1, 16, 128), BF16),
        pltpu.VMEM((2 * tiles1, 16, 128), BF16),
        pltpu.VMEM((units, targets), BF16),
        pltpu.VMEM((2, width, hidden), F32),
        pltpu.VMEM((2, units, hidden), F32),
        pltpu.SemaphoreType.DMA((INPUTS,)),
        pltpu.SemaphoreType.DMA((5,)),
        pltpu.SemaphoreType.DMA((len(SENDS),)),
        pltpu.SemaphoreType.DMA((len(SENDS),)),
        pltpu.SemaphoreType.DMA((GROUPS,)),
    ]
    outs = [
        jax.ShapeDtypeStruct((units, targets), BF16),
        jax.ShapeDtypeStruct((width, hidden), F32),
        jax.ShapeDtypeStruct((width, hidden), F32),
        jax.ShapeDtypeStruct((units, hidden), F32),
        jax.ShapeDtypeStruct((units, hidden), F32),
    ]
    found = pl.pallas_call(
        functools.partial(kernel, n_store, n_feat),
        out_shape=outs,
        in_specs=[pl.BlockSpec(memory_space=pltpu.HBM)] * len(args),
        out_specs=[pl.BlockSpec(memory_space=pltpu.HBM)] * 5,
        scratch_shapes=scratch,
        compiler_params=pltpu.CompilerParams(collective_id=0, has_side_effects=True, vmem_limit_bytes=VMEM_LIMIT),
    )(*args)
    return pl.pallas_call(
        hand_over,
        out_shape=outs,
        in_specs=[pl.BlockSpec(memory_space=pltpu.HBM)] * 5,
        out_specs=[pl.BlockSpec(memory_space=pltpu.HBM)] * 5,
        scratch_shapes=[pltpu.VMEM(out.shape, out.dtype) for out in outs] + [pltpu.SemaphoreType.DMA((10,))],
        compiler_params=pltpu.CompilerParams(vmem_limit_bytes=VMEM_LIMIT),
    )(*found)


def solution(mesh):
    return jax.shard_map(
        functools.partial(body, mesh.shape["store"], mesh.shape["feat"]),
        mesh=mesh,
        in_specs=(
            P("feat", "store"),
            P("store", None, None),
            P("store", None),
            P("store", None, None),
            P("store", None, None),
            P("feat", None),
            P("feat", None),
            P("feat", None),
            P("feat", None),
            P("feat", "store"),
        ),
        out_specs=(
            P("feat", "store"),
            P("feat", None),
            P("feat", None),
            P("feat", None),
            P("feat", None),
        ),
        check_vma=False,
    )
```

```python
import functools

import jax
import jax.numpy as jnp
from jax import lax
from jax.experimental import pallas as pl
from jax.experimental.pallas import tpu as pltpu
from jax.sharding import PartitionSpec as P

MESH = pl.DeviceIdType.MESH
F32 = jnp.float32
BF16 = jnp.bfloat16
LOW = 256


def slope(values):
    sig = jax.nn.sigmoid(values)
    return sig * (1.0 + values * (1.0 - sig))


def nt_dot(left, right):
    return lax.dot_general(left, right, (((1,), (1,)), ((), ())), preferred_element_type=F32)


def dot(left, right):
    return jnp.dot(left, right, preferred_element_type=F32)


def halves(values):
    upper = values.astype(BF16)
    return upper, (values - upper.astype(F32)).astype(BF16)


def await_bytes(ref, sem):
    pltpu.make_async_copy(ref, ref, sem).wait()


SENDS = (
    ("rows", "w1", "w1_swap", "nodes")
    + ("inputs", "sibling0", "sibling1")
    + tuple(what + quarter + step for what in ("hid", "back", "slope") for quarter in "0123" for step in ("_near", "_far"))
    + tuple(total + step for total in ("w2", "w1_0", "w1_1") for step in ("_merge", "_reduce", "_spread", "_swap"))
)
INPUTS = 10
GROUPS = 8
QUARTERS = 4
STAGES = ((0, 2), (1, 3))
VMEM_LIMIT = 60 * 1024 * 1024


def kernel(
    n_store,
    n_feat,
    features_hbm,
    serve_rows_hbm,
    row_counts_hbm,
    index_one_hbm,
    index_two_hbm,
    w1_self_hbm,
    w1_neigh_hbm,
    w2_self_hbm,
    w2_neigh_hbm,
    out_grad_hbm,
    h2_hbm,
    w1_self_out,
    w1_neigh_out,
    w2_self_out,
    w2_neigh_out,
    features,
    serve_rows,
    row_counts,
    index_rows,
    index_one,
    index_two,
    w2,
    out_grad,
    table,
    stage,
    rows_in,
    owner_of,
    pick,
    both,
    node_inputs,
    nodes_out,
    nodes_in,
    w1_own,
    w1_all,
    hid_own,
    hid_all,
    self_t,
    count_t,
    back_out,
    back_in_0,
    back_in_1,
    back_mid_0,
    back_mid_1,
    back_end_0,
    back_end_1,
    slope_own,
    slope_all,
    w2_total,
    w1_total_0,
    w1_total_1,
    w2_sum,
    w1_sum_0,
    w1_sum_1,
    h2,
    w1_wide,
    w2_wide,
    input_sems,
    output_sems,
    send_sems,
    recv_sems,
    group_sems,
):
    my_store, my_feat = lax.axis_index("store"), lax.axis_index("feat")
    my_chip, my_core = my_store // 2, lax.rem(my_store, 2)
    n_chip = n_store // 2
    n_x = 1 << (n_feat.bit_length() // 2)
    n_y = n_feat // n_x
    my_y, my_x = my_feat // n_x, lax.rem(my_feat, n_x)
    width, papers = features.shape
    cap = serve_rows.shape[2]
    entries, nodes = index_one.shape
    fan_one = entries - 1
    fan_two = index_two.shape[1] - 1
    units, hidden = w2.shape[0] // 2, w2.shape[1]
    columns = hidden // QUARTERS
    own_rows = nodes // n_feat
    pad = both.shape[0] // 2
    pending = []
    back_in = (back_in_0.at[0], back_in_0.at[1], back_in_1.at[0], back_in_1.at[1])
    back_mid = (back_mid_0.at[0], back_mid_0.at[1], back_mid_1.at[0], back_mid_1.at[1])
    back_end = (back_end_0.at[0], back_end_0.at[1], back_end_1.at[0], back_end_1.at[1])
    sibling = my_store + 1 - 2 * my_core

    def store_peer(step):
        return lax.rem(my_store + step + n_store, n_store)

    def feat_peer(step):
        return lax.rem(my_feat + step + n_feat, n_feat)

    def chip_peer(step):
        return lax.rem(my_chip + step + n_chip, n_chip)

    def send(src, dst, name, recv_sem, axis, peer):
        pltpu.make_async_remote_copy(
            src_ref=src,
            dst_ref=dst,
            send_sem=send_sems.at[SENDS.index(name)],
            recv_sem=recv_sem,
            device_id={axis: peer},
            device_id_type=MESH,
        ).start()

    def recv_of(name):
        return recv_sems.at[SENDS.index(name)]

    def later(ref, name):
        pending.append(lambda: await_bytes(ref, send_sems.at[SENDS.index(name)]))

    def keep(src, dst, sem):
        pltpu.make_async_copy(src, dst, sem).start()

    def write(src, dst, i):
        copy = pltpu.make_async_copy(src, dst, output_sems.at[i])
        copy.start()
        pending.append(copy.wait)

    def loop(low, high, fn):
        def step(k, carry):
            fn(k)
            return carry

        lax.fori_loop(low, high, step, 0)

    def far_first(n):
        return sorted(range(1, n), key=lambda k: -min(k, n - k))

    def each_chip(fn):
        fn(chip_peer(n_chip // 2))

        def pair(i):
            fn(chip_peer(n_chip // 2 - i))
            fn(chip_peer(i - n_chip // 2))

        loop(1, n_chip // 2, pair)

    def share(src_of, dst, name):
        for down in far_first(n_y) + [0]:
            for right in far_first(n_x) + [0]:
                if down or right:
                    peer = lax.rem(my_y + down, n_y) * n_x + lax.rem(my_x + right, n_x)
                    send(src_of(peer), dst, name, recv_of(name), "feat", peer)
        keep(src_of(my_feat), dst, recv_of(name))

    def along(x, k):
        return my_y * n_x + lax.rem(my_x + k, n_x) if x else lax.rem(my_y + k, n_y) * n_x + my_x

    def count_of(x):
        return n_x if x else n_y

    def spread_near(name, own, dst, x):
        step, spot = name + "_near", dst.at[my_y, my_x]
        for k in far_first(count_of(x)):
            send(own, spot, step, recv_of(step), "feat", along(x, k))
        keep(own, spot, recv_of(step))
        if count_of(x) > 1:
            later(dst.at[0, pl.ds(0, n_x - 1)] if x else dst.at[pl.ds(0, n_y - 1), 0], step)

    def spread_far(name, dst, x):
        step, line = name + "_far", dst.at[my_y] if x else dst.at[:, my_x]
        await_bytes(line, recv_of(name + "_near"))
        for k in far_first(count_of(not x)):
            send(line, line, step, recv_of(step), "feat", along(not x, k))
        if count_of(not x) > 1:
            later(dst.at[pl.ds(0, n_y - 1)] if x else dst.at[:, pl.ds(0, n_x - 1)], step)

    def spread_end(name, dst, x):
        if count_of(not x) > 1:
            await_bytes(dst.at[pl.ds(0, n_y - 1)] if x else dst.at[:, pl.ds(0, n_x - 1)], recv_of(name + "_far"))

    def fold_far(name, src, dst, x):
        step, mine = name + "_far", my_x if x else my_y

        def lines(k):
            return src.at[:, lax.rem(my_x + k, n_x)] if x else src.at[lax.rem(my_y + k, n_y)]

        for k in far_first(count_of(x)):
            send(lines(k), dst.at[mine], step, recv_of(step), "feat", along(x, k))
        keep(lines(0), dst.at[mine], recv_of(step))
        if count_of(x) > 1:
            later(dst.at[pl.ds(0, count_of(x) - 1)], step)

    def fold_near(name, src, middle, dst, x):
        await_bytes(src, recv_of(name + "_far"))
        total = src[0].astype(F32)
        for line in range(1, count_of(x)):
            total += src[line].astype(F32)
        middle[...] = total.astype(BF16)
        step, mine = name + "_near", my_y if x else my_x

        def block(k):
            return middle.at[lax.rem(my_y + k, n_y) if x else lax.rem(my_x + k, n_x)]

        for k in far_first(count_of(not x)):
            send(block(k), dst.at[mine], step, recv_of(step), "feat", along(not x, k))
        keep(block(0), dst.at[mine], recv_of(step))
        if count_of(not x) > 1:
            later(dst.at[pl.ds(0, count_of(not x) - 1)], step)

    def fold_end(name, src, x):
        await_bytes(src, recv_of(name + "_near"))
        total = src[0].astype(F32)
        for line in range(1, count_of(not x)):
            total += src[line].astype(F32)
        return total

    barrier = pltpu.get_barrier_semaphore()

    def greet(axis, peer):
        pl.semaphore_signal(barrier, inc=1, device_id={axis: peer}, device_id_type=MESH)

    reads = (
        (features_hbm, features),
        (serve_rows_hbm, serve_rows),
        (w1_self_hbm, w1_own.at[0]),
        (w1_neigh_hbm, w1_own.at[1]),
        (row_counts_hbm, row_counts),
        (index_one_hbm, index_rows),
        (index_two_hbm, index_two),
        (w2_self_hbm, w2.at[pl.ds(0, units)]),
        (w2_neigh_hbm, w2.at[pl.ds(units, units)]),
        (out_grad_hbm, out_grad),
    )
    reads = [pltpu.make_async_copy(src, dst, input_sems.at[i]) for i, (src, dst) in enumerate(reads)]
    for read in reads[:2]:
        read.start()

    def greet_pair(i):
        greet("store", store_peer(n_store // 2 - i))
        greet("store", store_peer(i - n_store // 2))

    greet("store", store_peer(n_store // 2))
    loop(1, n_store // 2, greet_pair)
    loop(1, n_feat, lambda k: greet("feat", feat_peer(k)))
    for read in reads[2:]:
        read.start()
    for group in range(n_feat):
        for half in range(2):
            w1_all[group, half, width:, :] = jnp.zeros((pad - width, hidden), BF16)
    both[...] = jnp.zeros_like(both)

    reads[0].wait()
    reads[1].wait()
    highs = papers // LOW
    for high in range(highs):
        table[high * width : (high + 1) * width, :] = features[:, high * LOW : (high + 1) * LOW].astype(BF16)
    low_ids = lax.broadcasted_iota(jnp.int32, (LOW, cap), 0)

    def serve(trainer):
        wanted = serve_rows[0, pl.ds(trainer, 1), :]
        low, high_of = wanted & (LOW - 1), wanted // LOW
        one_hot = jnp.where(low_ids == low, 1.0, 0.0).astype(BF16)
        found = dot(table[...], one_hot)
        total = found[0:width, :]
        for high in range(1, highs):
            total = jnp.where(high_of == high, found[high * width : (high + 1) * width, :], total)
        stage[trainer] = total.astype(BF16)

    def serve_some(i):
        for j in range(4):
            serve(4 * i + j)

    loop(0, n_store // 4, serve_some)
    for read in reads[2:]:
        read.wait()
    pl.semaphore_wait(barrier, n_store + n_feat - 2)

    half_store = n_store // 2
    group_size = n_store // GROUPS

    def send_rows(trainer, rank):
        send(stage.at[trainer], rows_in.at[rank], "rows", group_sems.at[rank // group_size], "store", trainer)

    def send_w1(peer):
        send(w1_own.at[my_core], w1_all.at[my_feat, my_core, pl.ds(0, width)], "w1", recv_of("w1"), "feat", peer)

    def send_pair(i):
        send_rows(store_peer(half_store - i), 2 * i - 1)
        send_rows(store_peer(i - half_store), 2 * i)

    def send_pair_and_w1(i):
        send_pair(i)
        send_w1(feat_peer(i))

    send_rows(store_peer(half_store), 0)
    shared = min(half_store, n_feat)
    loop(1, shared, send_pair_and_w1)
    loop(shared, half_store, send_pair)
    loop(shared, n_feat, lambda i: send_w1(feat_peer(i)))
    keep(stage.at[my_store], rows_in.at[n_store - 1], group_sems.at[GROUPS - 1])
    keep(w1_own.at[my_core], w1_all.at[my_feat, my_core, pl.ds(0, width)], recv_of("w1"))
    later(stage.at[pl.ds(0, n_store - 1)], "rows")
    later(w1_all.at[pl.ds(0, n_feat - 1), 0, pl.ds(0, width)], "w1")

    for entry in range(entries):
        index_one[entry : entry + 1, :] = index_rows[entry]
    raw = index_one[...]
    owners = raw // cap
    place = (raw & (cap - 1)).astype(F32)
    counts = jnp.ones(raw.shape, F32)
    for owner in range(n_store):
        counts = jnp.where(owners == owner, row_counts[0:1, owner : owner + 1].astype(F32), counts)
    place = place - jnp.floor((place + 0.5) / counts) * counts
    owner_of[0:entries, :] = owners
    place = place.astype(jnp.int32)
    slot_ids = lax.broadcasted_iota(jnp.int32, (cap, nodes), 0)
    for entry in range(entries):
        pick[entry] = jnp.where(slot_ids == place[entry : entry + 1, :], 1.0, 0.0).astype(BF16)

    strip = 64
    targets = index_two.shape[2]

    def second_tables(part):
        node_ids = lax.broadcasted_iota(jnp.int32, (strip, targets), 0) + part * strip
        at = pl.ds(pl.multiple_of(part * strip, strip), strip)
        self_t[at, :] = jnp.where(node_ids == index_two[0, 0:1, :], 1.0, 0.0).astype(BF16)
        total = jnp.zeros((strip, targets), F32)
        for entry in range(1, fan_two + 1):
            total += jnp.where(node_ids == index_two[0, entry : entry + 1, :], 1.0, 0.0)
        count_t[at, :] = total.astype(BF16)

    loop(0, nodes // strip, second_tables)

    def gather(group):
        await_bytes(rows_in.at[pl.ds(group * group_size, group_size)], group_sems.at[group])
        arrived = rows_in[pl.ds(group * group_size, group_size)].reshape(group_size * width, cap)
        owners = []
        for member in range(group_size):
            rank = group * group_size + member
            offset = half_store - (rank + 1) // 2 if member % 2 else rank // 2 - half_store
            owners.append(store_peer(-offset))
        sums = [both[0:width, :], both[pad : pad + width, :]]
        for entry in range(entries):
            found = dot(arrived, pick[entry])
            of = owner_of[entry : entry + 1, :]
            mine = jnp.zeros((width, nodes), F32)
            for member in range(group_size):
                mine = jnp.where(of == owners[member], found[member * width : (member + 1) * width, :], mine)
            sums[min(entry, 1)] += mine
        both[0:width, :], both[pad : pad + width, :] = sums

    loop(0, GROUPS - 2, gather)
    await_bytes(w1_all.at[:, 0, pl.ds(0, width)], recv_of("w1"))
    mine = w1_all.at[:, my_core, pl.ds(0, width)]
    send(mine, mine, "w1_swap", recv_of("w1_swap"), "store", my_store + 1 - 2 * my_core)
    later(w1_all.at[:, 0, pl.ds(0, width)], "w1_swap")
    loop(GROUPS - 2, GROUPS, gather)
    both[pad : pad + width, :] = both[pad : pad + width, :] / fan_one
    node_inputs[my_core] = both[...].astype(BF16)
    send(node_inputs.at[my_core], node_inputs.at[my_core], "inputs", recv_of("inputs"), "store", sibling)
    later(node_inputs.at[0], "inputs")
    turned = both[...].T.astype(BF16)
    for group in range(n_feat):
        nodes_out[group] = turned[group * own_rows : (group + 1) * own_rows, :]

    share(lambda peer: nodes_out.at[peer], nodes_in.at[my_feat], "nodes")
    later(nodes_out.at[pl.ds(0, n_feat - 1)], "nodes")

    await_bytes(w1_all.at[:, 0, pl.ds(0, width)], recv_of("w1_swap"))
    await_bytes(nodes_in, recv_of("nodes"))
    own_nodes = jnp.concatenate([nodes_in[group] for group in range(n_feat)], axis=1)
    slope_one = [None] * QUARTERS
    for stage_now in STAGES:
        for q in stage_now:
            cols = slice(q * columns, (q + 1) * columns)
            pre_one = dot(own_nodes, w1_all[:, :, :, cols].reshape(n_feat * 2 * pad, columns))
            hid_own[q] = (pre_one * jax.nn.sigmoid(pre_one)).astype(BF16)
            spread_near(f"hid{q}", hid_own.at[q], hid_all.at[q], q < 2)
            slope_one[q] = slope(pre_one)
    for stage_now in STAGES:
        for q in stage_now:
            spread_far(f"hid{q}", hid_all.at[q], q < 2)

    mixed = jnp.zeros((2 * units, nodes), F32)
    hid = [None] * QUARTERS
    for stage_now in STAGES:
        for q in stage_now:
            spread_end(f"hid{q}", hid_all.at[q], q < 2)
            hid[q] = hid_all[q].reshape(nodes, columns)
            mixed += nt_dot(w2[:, q * columns : (q + 1) * columns], hid[q])
    upper, lower = halves(mixed)
    self_term = dot(jnp.concatenate([upper[:units], lower[:units]], axis=0), self_t[...])
    neigh_term = dot(jnp.concatenate([upper[units:], lower[units:]], axis=0), count_t[...])
    pre_two = self_term[:units] + self_term[units:] + (neigh_term[:units] + neigh_term[units:]) / fan_two
    grad_two = (out_grad[...].astype(F32) * slope(pre_two)).astype(BF16)
    node_grad = jnp.concatenate([nt_dot(grad_two, self_t[...]), nt_dot(grad_two, count_t[...]) / fan_two], axis=0)
    upper, lower = halves(node_grad.T)
    turned = jnp.concatenate([upper, lower], axis=1)
    for stage_now in STAGES:
        for q in stage_now:
            weights = w2[:, q * columns : (q + 1) * columns]
            back = dot(turned, jnp.concatenate([weights, weights], axis=0))
            back_out[q] = back.astype(BF16).reshape(n_y, n_x, own_rows, columns)
            fold_far(f"back{q}", back_out.at[q], back_in[q], q >= 2)
    h2[...] = (pre_two * jax.nn.sigmoid(pre_two)).astype(BF16)
    write(h2, h2_hbm, 0)

    def total_of(ref, total, name, merged_already=False):
        tiles = ref.shape[1] // 2
        per = -(-tiles // n_chip)
        summers = tiles // per
        spread = summers * 4 == n_chip * 3

        def sums(chip):
            return lax.rem(chip, 4) != 3 if spread else chip < summers

        def first(chip):
            return (chip - chip // 4 if spread else chip) * per

        part, merged, arrived = ref.at[0], ref.at[1], ref.at[2]

        def fill(half, grad, row0=0):
            across = grad.shape[1] // 128
            for row in range(grad.shape[0] // 16):
                for col in range(across):
                    tile = grad[row * 16 : (row + 1) * 16, col * 128 : (col + 1) * 128]
                    if merged_already:
                        merged[tiles + row * across + col] = tile
                    else:
                        part[half * tiles + row * across + col] = tile

        def merge():
            own = pl.ds((1 - my_core) * tiles, tiles)
            send(part.at[own], merged.at[pl.ds(0, tiles)], name + "_merge", recv_of(name + "_merge"), "store", sibling)
            later(part.at[pl.ds(0, tiles)], name + "_merge")

        def reduce():
            if not merged_already:
                await_bytes(merged.at[pl.ds(0, tiles)], recv_of(name + "_merge"))
                both_cores = part[pl.ds(my_core * tiles, tiles)].astype(F32) + merged[0:tiles].astype(F32)
                merged[tiles : 2 * tiles] = both_cores.astype(BF16)

            def to(chip):
                @pl.when(sums(chip))
                def _():
                    send(
                        merged.at[pl.ds(tiles + first(chip), per)],
                        arrived.at[pl.ds(my_chip * per, per)],
                        name + "_reduce",
                        recv_of(name + "_reduce"),
                        "store",
                        chip * 2 + my_core,
                    )

            each_chip(to)

            def sent():
                for count, wait_here in ((summers - 1, sums(my_chip)), (summers, jnp.logical_not(sums(my_chip)))):
                    if summers == n_chip and count == n_chip:
                        continue

                    @pl.when(wait_here)
                    def _(count=count):
                        await_bytes(merged.at[pl.ds(0, count * per)], send_sems.at[SENDS.index(name + "_reduce")])

            pending.append(sent)

        def spread_out():
            @pl.when(sums(my_chip))
            def _():
                mine = pl.ds(first(my_chip), per)
                keep(
                    merged.at[pl.ds(tiles + first(my_chip), per)],
                    arrived.at[pl.ds(my_chip * per, per)],
                    recv_of(name + "_reduce"),
                )
                await_bytes(arrived.at[pl.ds(0, n_chip * per)], recv_of(name + "_reduce"))
                summed = arrived[0:per].astype(F32)
                for chip in range(1, n_chip):
                    summed += arrived[chip * per : (chip + 1) * per].astype(F32)
                at = pl.ds(my_core * tiles + first(my_chip), per)
                total[at] = summed.astype(BF16)
                each_chip(
                    lambda chip: send(
                        total.at[at],
                        total.at[at],
                        name + "_spread",
                        recv_of(name + "_spread"),
                        "store",
                        chip * 2 + my_core,
                    )
                )

            def sent():
                @pl.when(sums(my_chip))
                def _():
                    await_bytes(arrived.at[pl.ds(0, (n_chip - 1) * per)], send_sems.at[SENDS.index(name + "_spread")])

            pending.append(sent)

        def swap():
            for count, wait_here in ((summers - 1, sums(my_chip)), (summers, jnp.logical_not(sums(my_chip)))):
                if summers == n_chip and count == n_chip:
                    continue

                @pl.when(wait_here)
                def _(count=count):
                    await_bytes(total.at[pl.ds(0, count * per)], recv_of(name + "_spread"))

            mine = total.at[pl.ds(my_core * tiles, tiles)]
            send(mine, mine, name + "_swap", recv_of(name + "_swap"), "store", sibling)
            later(total.at[pl.ds(0, tiles)], name + "_swap")

        def finish():
            await_bytes(total.at[pl.ds(0, tiles)], recv_of(name + "_swap"))

        return fill, merge, reduce, spread_out, swap, finish

    fill, merge, reduce2, spread2, swap2, finish2 = total_of(w2_total, w2_sum, "w2")
    upper, lower = halves(node_grad)
    stacked = jnp.concatenate([upper, lower], axis=0)
    grad_w2 = jnp.concatenate([dot(stacked, part) for part in hid], axis=1)
    grad_w2 = (grad_w2[: 2 * units] + grad_w2[2 * units :]).astype(BF16)
    fill(0, grad_w2[:units])
    fill(1, grad_w2[units:])
    merge()
    reduce2()

    def slope_near(stage_no):
        for core, q in enumerate(STAGES[stage_no]):
            x, step, spot = core == 0, f"slope{q}_near", slope_all.at[stage_no, my_core, my_y, my_x]
            arrival = recv_of(f"slope{stage_no}_near")
            total = fold_end(f"back{q}", back_end[q], q >= 2)
            slope_own[q] = (total * slope_one[q]).astype(BF16)

            def to_line(k, x=x, step=step, spot=spot, arrival=arrival, core=core, q=q):
                chip = along(x, k)
                pltpu.make_async_remote_copy(
                    src_ref=slope_own.at[q],
                    dst_ref=spot,
                    send_sem=send_sems.at[SENDS.index(step)],
                    recv_sem=arrival,
                    device_id={"store": my_chip * 2 + core, "feat": chip},
                    device_id_type=MESH,
                ).start()

            for k in far_first(count_of(x)):
                to_line(k)
            if count_of(x) > 1:
                later(slope_all.at[0, 0, 0, pl.ds(0, n_x - 1)] if x else slope_all.at[0, 0, pl.ds(0, n_y - 1), 0], step)

            if core == 0:
                later(slope_own.at[0], f"sibling{stage_no}")

            @pl.when(my_core == core)
            def _(arrival=arrival, q=q, spot=spot):
                keep(slope_own.at[q], spot, arrival)

            @pl.when(my_core != core)
            def _(arrival=arrival, q=q, spot=spot):
                send(slope_own.at[q], spot, f"sibling{stage_no}", arrival, "store", sibling)

    def slope_line(stage_no, x):
        return slope_all.at[stage_no, :, my_y] if x else slope_all.at[stage_no, :, :, my_x]

    def slope_rest(stage_no, x):
        return slope_all.at[stage_no, :, pl.ds(0, n_y - 1)] if x else slope_all.at[stage_no, :, :, pl.ds(0, n_x - 1)]

    def on_core(core, fn):
        pl.when(my_core == core)(fn)

    def slope_far(stage_no):
        step = f"slope{stage_no}_far"
        for core in range(2):
            x = core == 0

            def forward(x=x):
                line = slope_line(stage_no, x)
                await_bytes(line, recv_of(f"slope{stage_no}_near"))
                for k in far_first(count_of(not x)):
                    send(line, line, step, recv_of(step), "feat", along(not x, k))

            on_core(core, forward)

    def slope_end(stage_no, sems):
        for core in range(2):
            x = core == 0
            if count_of(not x) > 1:
                on_core(
                    core,
                    lambda x=x: await_bytes(slope_rest(stage_no, x), sems.at[SENDS.index(f"slope{stage_no}_far")]),
                )

    def first_weights(stage_no, fill):
        slope_end(stage_no, recv_sems)
        grad = jnp.zeros((2 * pad, columns), F32)
        for core in range(2):
            grad += dot(node_inputs[core], slope_all[stage_no, core].reshape(nodes, columns))
        grad = grad.astype(BF16)
        fill(0, jnp.concatenate([grad[0:width], grad[pad : pad + width]], axis=0))

    def fold_middle(stage_no):
        for q in STAGES[stage_no]:
            fold_near(f"back{q}", back_in[q], back_mid[q], back_end[q], q >= 2)

    fill_a, _, reduce_a, spread_a, swap_a, finish_a = total_of(w1_total_0, w1_sum_0, "w1_0", merged_already=True)
    fill_b, _, reduce_b, spread_b, swap_b, finish_b = total_of(w1_total_1, w1_sum_1, "w1_1", merged_already=True)
    fold_middle(0)
    fold_middle(1)
    slope_near(0)
    slope_near(1)
    slope_far(0)
    slope_far(1)
    spread2()
    await_bytes(node_inputs.at[0], recv_of("inputs"))
    first_weights(0, fill_a)
    reduce_a()
    first_weights(1, fill_b)
    reduce_b()
    spread_a()
    spread_b()
    swap2()
    finish2()
    across = hidden // 128
    for part, out in enumerate((w2_self_out, w2_neigh_out)):
        for row in range(units // 16):
            for col in range(across):
                w2_wide[part, row * 16 : (row + 1) * 16, col * 128 : (col + 1) * 128] = w2_sum[
                    (part * (units // 16) + row) * across + col
                ].astype(F32)
        write(w2_wide.at[part], out, 3 + part)
    swap_a()
    swap_b()
    each = across // QUARTERS
    for stage_no, (finish, total) in enumerate(((finish_a, w1_sum_0), (finish_b, w1_sum_1))):
        finish()
        for core, q in enumerate(STAGES[stage_no]):
            for row in range(2 * width // 16):
                part, at = row // (width // 16), row % (width // 16) * 16
                for col in range(each):
                    left = (q * each + col) * 128
                    w1_wide[part, at : at + 16, left : left + 128] = total[
                        (core * (2 * width // 16) + row) * each + col
                    ].astype(F32)
    write(w1_wide.at[0], w1_self_out, 1)
    write(w1_wide.at[1], w1_neigh_out, 2)
    pending.append(lambda: slope_end(0, send_sems))
    pending.append(lambda: slope_end(1, send_sems))

    for wait in pending:
        wait()


def hand_over(*refs):
    src, dst, held, sems = refs[:5], refs[5:10], refs[10:15], refs[15]
    reads = [pltpu.make_async_copy(src[i], held[i], sems.at[i]) for i in range(5)]
    writes = [pltpu.make_async_copy(held[i], dst[i], sems.at[5 + i]) for i in range(5)]
    for read in reads:
        read.start()
    for read, copy in zip(reads, writes):
        read.wait()
        copy.start()
    for copy in writes:
        copy.wait()


def body(n_store, n_feat, *args):
    args = list(args)
    args[3] = jnp.transpose(args[3], (1, 0, 2))
    features, serve_rows, _, index_one, index_two, w1_self, _, w2_self, _, out_grad = args
    width, papers = features.shape
    cap = serve_rows.shape[2]
    entries, _, nodes = index_one.shape
    targets = index_two.shape[2]
    hidden, units = w2_self.shape[1], w2_self.shape[0]
    own_rows = nodes // n_feat
    pad = -(-width // 64) * 64
    columns = hidden // QUARTERS
    n_x = 1 << (n_feat.bit_length() // 2)
    n_y = n_feat // n_x
    blocks = (QUARTERS, n_y, n_x, own_rows, columns)
    tiles2 = units // 16 * (hidden // 128)
    tiles1 = 2 * width // 16 * (columns // 128)

    def total_scratch(tiles):
        per = -(-tiles // (n_store // 2))
        return pltpu.VMEM((3, max(2 * tiles, n_store // 2 * per), 16, 128), BF16)

    scratch = [
        pltpu.VMEM(features.shape, F32),
        pltpu.VMEM(serve_rows.shape, jnp.int32),
        pltpu.VMEM(args[2].shape, jnp.int32),
        pltpu.VMEM((entries, 1, nodes), jnp.int32),
        pltpu.VMEM((entries, nodes), jnp.int32),
        pltpu.VMEM(index_two.shape, jnp.int32),
        pltpu.VMEM((2 * units, hidden), BF16),
        pltpu.VMEM(out_grad.shape, BF16),
        pltpu.VMEM((papers // LOW * width, LOW), BF16),
        pltpu.VMEM((n_store, width, cap), BF16),
        pltpu.VMEM((n_store, width, cap), BF16),
        pltpu.VMEM((entries, nodes), jnp.int32),
        pltpu.VMEM((entries, cap, nodes), BF16),
        pltpu.VMEM((2 * pad, nodes), F32),
        pltpu.VMEM((2, 2 * pad, nodes), BF16),
        pltpu.VMEM((n_feat, own_rows, 2 * pad), BF16),
        pltpu.VMEM((n_feat, own_rows, 2 * pad), BF16),
        pltpu.VMEM((2, width, hidden), BF16),
        pltpu.VMEM((n_feat, 2, pad, hidden), BF16),
        pltpu.VMEM((QUARTERS, own_rows, columns), BF16),
        pltpu.VMEM(blocks, BF16),
        pltpu.VMEM((nodes, targets), BF16),
        pltpu.VMEM((nodes, targets), BF16),
        pltpu.VMEM(blocks, BF16),
        pltpu.VMEM((2, n_y, n_x, own_rows, columns), BF16),
        pltpu.VMEM((2, n_x, n_y, own_rows, columns), BF16),
        pltpu.VMEM((2, n_x, own_rows, columns), BF16),
        pltpu.VMEM((2, n_y, own_rows, columns), BF16),
        pltpu.VMEM((2, n_x, own_rows, columns), BF16),
        pltpu.VMEM((2, n_y, own_rows, columns), BF16),
        pltpu.VMEM((QUARTERS, own_rows, columns), BF16),
        pltpu.VMEM((2, 2, n_y, n_x, own_rows, columns), BF16),
        total_scratch(tiles2),
        total_scratch(tiles1),
        total_scratch(tiles1),
        pltpu.VMEM((2 * tiles2, 16, 128), BF16),
        pltpu.VMEM((2 * tiles1, 16, 128), BF16),
        pltpu.VMEM((2 * tiles1, 16, 128), BF16),
        pltpu.VMEM((units, targets), BF16),
        pltpu.VMEM((2, width, hidden), F32),
        pltpu.VMEM((2, units, hidden), F32),
        pltpu.SemaphoreType.DMA((INPUTS,)),
        pltpu.SemaphoreType.DMA((5,)),
        pltpu.SemaphoreType.DMA((len(SENDS),)),
        pltpu.SemaphoreType.DMA((len(SENDS),)),
        pltpu.SemaphoreType.DMA((GROUPS,)),
    ]
    outs = [
        jax.ShapeDtypeStruct((units, targets), BF16),
        jax.ShapeDtypeStruct((width, hidden), F32),
        jax.ShapeDtypeStruct((width, hidden), F32),
        jax.ShapeDtypeStruct((units, hidden), F32),
        jax.ShapeDtypeStruct((units, hidden), F32),
    ]
    found = pl.pallas_call(
        functools.partial(kernel, n_store, n_feat),
        out_shape=outs,
        in_specs=[pl.BlockSpec(memory_space=pltpu.HBM)] * len(args),
        out_specs=[pl.BlockSpec(memory_space=pltpu.HBM)] * 5,
        scratch_shapes=scratch,
        compiler_params=pltpu.CompilerParams(collective_id=0, has_side_effects=True, vmem_limit_bytes=VMEM_LIMIT),
    )(*args)
    return pl.pallas_call(
        hand_over,
        out_shape=outs,
        in_specs=[pl.BlockSpec(memory_space=pltpu.HBM)] * 5,
        out_specs=[pl.BlockSpec(memory_space=pltpu.HBM)] * 5,
        scratch_shapes=[pltpu.VMEM(out.shape, out.dtype) for out in outs] + [pltpu.SemaphoreType.DMA((10,))],
        compiler_params=pltpu.CompilerParams(vmem_limit_bytes=VMEM_LIMIT),
    )(*found)


def solution(mesh):
    return jax.shard_map(
        functools.partial(body, mesh.shape["store"], mesh.shape["feat"]),
        mesh=mesh,
        in_specs=(
            P("feat", "store"),
            P("store", None, None),
            P("store", None),
            P("store", None, None),
            P("store", None, None),
            P("feat", None),
            P("feat", None),
            P("feat", None),
            P("feat", None),
            P("feat", "store"),
        ),
        out_specs=(
            P("feat", "store"),
            P("feat", None),
            P("feat", None),
            P("feat", None),
            P("feat", None),
        ),
        check_vma=False,
    )
```
